128 devices in a mesh: fsdp: 8 (over y_lo, z), ctx: 16 (over y_hi, x, core).
Axes of the slice: x: 4, y: 4 (y_hi: 2, y_lo: 2; y = y_hi * 2 + y_lo), z: 4, core: 2. Of those that a mesh axis runs over, the one named last changes fastest.
Arguments:
- tokens: bfloat16 [16384, 1024], P(('fsdp', 'ctx')), may hold values from -6 to 6
- cotangent: bfloat16 [16384, 1024], P(('fsdp', 'ctx')), may hold values from -6 to 6
- w_query: bfloat16 [1024, 2048], P('fsdp'), may hold values from -0.1875 to 0.1875
- w_key: bfloat16 [1024, 1024], P('fsdp'), may hold values from -0.1875 to 0.1875
- w_value: bfloat16 [1024, 1024], P('fsdp'), may hold values from -0.1875 to 0.1875
- w_output: bfloat16 [1024, 2048], P('fsdp'), may hold values from -2 to 2
- w_gate: bfloat16 [1024, 3072], P('fsdp'), may hold values from -0.1875 to 0.1875
- w_up: bfloat16 [1024, 3072], P('fsdp'), may hold values from -0.1875 to 0.1875
- w_down: bfloat16 [1024, 3072], P('fsdp'), may hold values from -0.109375 to 0.109375
- norm_gain: float32 [1024], replicated, may hold values from 0.5 to 1.5
- mlp_gain: float32 [1024], replicated, may hold values from 0.5 to 1.5
- query_gain: float32 [128], replicated, may hold values from 0.1 to 1.9
- key_gain: float32 [128], replicated, may hold values from 0.1 to 1.9
Outputs:
- mixed: bfloat16 [16384, 1024], P(('fsdp', 'ctx'))
- input_grad: float32 [16384, 1024], P(('fsdp', 'ctx'))
- grad_query: float32 [1024, 2048], P('fsdp')
- grad_key: float32 [1024, 1024], P('fsdp')
- grad_value: float32 [1024, 1024], P('fsdp')
- grad_output: float32 [1024, 2048], P('fsdp')
- grad_gate: float32 [1024, 3072], P('fsdp')
- grad_up: float32 [1024, 3072], P('fsdp')
- grad_down: float32 [1024, 3072], P('fsdp')
- grad_norm_gain: float32 [1024], replicated
- grad_mlp_gain: float32 [1024], replicated
- grad_query_gain: float32 [128], replicated
- grad_key_gain: float32 [128], replicated
The draws below stay inside these ranges and needn't reach their ends.
All inputs are finite; a program needn't handle non-finite values.
Results may differ from the reference program's by a relative error of at most 0.028.
Values may be sent and summed in bfloat16 or wider, within the bound.
A program may use at most 192 MiB of HBM per device.

```python
import math
import jax
import jax.numpy as jnp
from jax import lax

D = 1024
HEADS = 16
KV_HEADS = 8
HEAD_DIM = 128
FF = 3072
SEQ = 2048
SEQS = 8
TOKENS = 16384


def level_of(rng, extent, cuts, least, high):
    loudness, own = 1.0, jax.random.fold_in(rng, 6)
    for position, parts in cuts:
        steps = jnp.exp(jax.random.uniform(jax.random.fold_in(own, position), (parts,), jnp.float32, least / len(cuts), high / len(cuts)))
        loudness = loudness * jnp.repeat(steps, extent[position] // parts).reshape([-1 if axis == position else 1 for axis in range(len(extent))])
    return loudness


def centred(stream_key, extent, scale, reach, cuts=(), kind=jnp.bfloat16):
    level = level_of(stream_key, extent, cuts, -0.22, 0.18) if cuts else 1.0
    array = jax.random.normal(stream_key, extent, jnp.float32) * scale * level
    return jnp.minimum(jnp.maximum(array, -reach), reach).astype(kind)


def setup_inputs(seed: int = 0) -> dict:
    arg_keys = jax.random.split(jax.random.key(seed), 14)
    tokens = centred(arg_keys[0], (TOKENS, D), 1.0, 6.0, ((0, 128),))
    cotangent = centred(arg_keys[1], (TOKENS, D), 1.0, 6.0, ((0, 128),))
    w_query = centred(arg_keys[2], (D, HEADS * HEAD_DIM), D ** -0.5, 0.1875, ((0, 8),))
    w_key = centred(arg_keys[3], (D, KV_HEADS * HEAD_DIM), D ** -0.5, 0.1875, ((0, 8),))
    w_value = centred(arg_keys[4], (D, KV_HEADS * HEAD_DIM), D ** -0.5, 0.1875, ((0, 8),))
    w_output = centred(arg_keys[5], (D, HEADS * HEAD_DIM), (max(HEADS * HEAD_DIM // 256, 1)) ** -0.5, 2.0, ((0, 8),))
    w_gate = centred(arg_keys[6], (D, FF), D ** -0.5, 0.1875, ((0, 8),))
    w_up = centred(arg_keys[7], (D, FF), D ** -0.5, 0.1875, ((0, 8),))
    w_down = centred(arg_keys[8], (D, FF), FF ** -0.5, 0.109375, ((0, 8),))
    norm_gain = jnp.clip(1.0 + 0.1 * jax.random.normal(arg_keys[9], (D,), jnp.float32), 0.5, 1.5)
    mlp_gain = jnp.clip(1.0 + 0.1 * jax.random.normal(arg_keys[10], (D,), jnp.float32), 0.5, 1.5)
    query_gain = jnp.clip(1.0 + 0.18 * jax.random.normal(arg_keys[11], (HEAD_DIM,), jnp.float32), 0.1, 1.9)
    key_gain = jnp.clip(1.0 + 0.18 * jax.random.normal(arg_keys[12], (HEAD_DIM,), jnp.float32), 0.1, 1.9)
    return {"tokens": tokens, "cotangent": cotangent, "w_query": w_query, "w_key": w_key, "w_value": w_value, "w_output": w_output, "w_gate": w_gate, "w_up": w_up, "w_down": w_down, "norm_gain": norm_gain, "mlp_gain": mlp_gain, "query_gain": query_gain, "key_gain": key_gain}


@jax.custom_vjp
def low(v):
    return lax.optimization_barrier(v.astype(jnp.bfloat16)).astype(jnp.float32)

@jax.custom_vjp
def low_back(v):
    return v

def low_keep(v):
    return (low(v), None)

def low_pass(kept, grad):
    return (grad,)

def back_keep(v):
    return (v, None)

def back_low(kept, grad):
    return (low(grad),)
low.defvjp(low_keep, low_pass)
low_back.defvjp(back_keep, back_low)
EPSILON = 1e-06
THETA = 1000000.0
NEGATIVE = -1e+30
HIGH = lax.Precision.HIGHEST

def rope_tables(length, head_dim):
    half = head_dim // 2
    freqs = jnp.power(THETA, -2.0 * jnp.arange(half, dtype=jnp.float32) / head_dim)
    angles = jnp.arange(length, dtype=jnp.float32)[:, None] * freqs[None, :]
    return (jnp.cos(angles), jnp.sin(angles))

def rotate(heads, cosine, sine):
    half = heads.shape[-1] // 2
    first = heads[..., :half]
    second = heads[..., half:]
    cosine = cosine[:, None, :]
    sine = sine[:, None, :]
    return jnp.concatenate([first * cosine - second * sine, second * cosine + first * sine], axis=-1)

def head_norm(heads, gain):
    return heads * lax.rsqrt(lax.optimization_barrier(jnp.mean(heads * heads, -1, keepdims=True)) + EPSILON) * gain

def row_norm(rows, gain):
    return rows * lax.rsqrt(lax.optimization_barrier(jnp.mean(rows * rows, -1, keepdims=True)) + EPSILON) * gain

def attention(queries, key_heads, value_heads):
    length = queries.shape[0]
    block = math.gcd(length, 512)
    count = length // block
    group = HEADS // KV_HEADS
    grouped = queries.reshape(count, block, KV_HEADS, group, HEAD_DIM)
    starts = block * jnp.arange(count, dtype=jnp.int32)
    key_pos = jnp.arange(length, dtype=jnp.int32)
    scale_factor = 1.0 / math.sqrt(HEAD_DIM)

    def one_block(operands):
        query_block, start = operands
        scores = jnp.einsum('qhgd,khd->hgqk', query_block, key_heads, precision=HIGH) * scale_factor
        scores = low_back(scores)
        query_pos = start + jnp.arange(block, dtype=jnp.int32)
        allowed = key_pos[None, :] <= query_pos[:, None]
        scores = jnp.where(allowed, scores, NEGATIVE)
        row_max = lax.optimization_barrier(jnp.max(scores, -1, keepdims=True))
        raised = jnp.where(allowed, jnp.exp(scores - row_max), 0.0)
        weights_soft = low(raised / lax.optimization_barrier(jnp.sum(raised, -1, keepdims=True)))
        return jnp.einsum('hgqk,khd->qhgd', weights_soft, value_heads, precision=HIGH)
    result = lax.map(jax.checkpoint(one_block), (grouped, starts))
    return result.reshape(length, HEADS * HEAD_DIM)

def layer_forward(inputs, w_query, w_key, w_value, w_output, w_gate, w_up, w_down, norm_gain, mlp_gain, query_gain, key_gain):
    length = inputs.shape[0]
    cosine, sine = rope_tables(length, HEAD_DIM)
    normed_in = low(row_norm(inputs, norm_gain))
    query_raw = low_back(jnp.dot(normed_in, w_query, precision=HIGH))
    key_raw = low_back(jnp.dot(normed_in, w_key, precision=HIGH))
    value_rows = low(low_back(jnp.dot(normed_in, w_value, precision=HIGH)))
    query_heads = low(rotate(head_norm(query_raw.reshape(length, HEADS, HEAD_DIM), query_gain), cosine, sine))
    key_heads = low(rotate(head_norm(key_raw.reshape(length, KV_HEADS, HEAD_DIM), key_gain), cosine, sine))
    mixed_heads = attention(query_heads, key_heads, value_rows.reshape(length, KV_HEADS, HEAD_DIM))
    attended = low(low_back(mixed_heads))
    branch = low_back(jnp.dot(attended, w_output.T, precision=HIGH))
    resid = inputs + branch
    mlp_in = low(row_norm(resid, mlp_gain))
    gate = low_back(jnp.dot(mlp_in, w_gate, precision=HIGH))
    up_proj = low_back(jnp.dot(mlp_in, w_up, precision=HIGH))
    hidden = low(jax.nn.silu(gate) * up_proj)
    return resid + jnp.dot(hidden, w_down.T, precision=HIGH)

def reference(tokens, cotangent, w_query, w_key, w_value, w_output, w_gate, w_up, w_down, norm_gain, mlp_gain, query_gain, key_gain):
    weights = tuple((weight.astype(jnp.float32) for weight in (w_query, w_key, w_value, w_output, w_gate, w_up, w_down, norm_gain, mlp_gain, query_gain, key_gain)))
    inputs = tokens.astype(jnp.float32).reshape(SEQS, SEQ, D)
    cot_rows = cotangent.astype(jnp.float32).reshape(SEQS, SEQ, D)

    def one_sequence(totals, pair):
        seq_in, seq_cot = pair
        outputs, pull = jax.vjp(layer_forward, seq_in, *weights)
        grads = pull(seq_cot)
        totals = tuple((first_term + second_term for first_term, second_term in zip(totals, grads[1:])))
        return (totals, (outputs, grads[0]))
    zeros = tuple((jnp.zeros_like(weight) for weight in weights))
    totals, (outputs, input_grads) = lax.scan(one_sequence, zeros, (inputs, cot_rows))
    return (outputs.reshape(TOKENS, D).astype(jnp.bfloat16), input_grads.reshape(TOKENS, D), totals[0], totals[1], totals[2], totals[3], totals[4], totals[5], totals[6], totals[7], totals[8], totals[9], totals[10])
```

```python
import math

import jax
import jax.numpy as jnp
import numpy as np
from jax import lax
from jax.experimental import pallas as pl
from jax.experimental.pallas import tpu as pltpu
from jax.sharding import PartitionSpec as P

MESH = pl.DeviceIdType.MESH
EPSILON = 1e-06
THETA = 1000000.0
HEAD_DIM = 128
SCALE = 1.0 / math.sqrt(HEAD_DIM)
SCALE_LOG2 = SCALE * math.log2(math.e)
F32 = jnp.float32
BF16 = jnp.bfloat16
DIST = (1, 3, 2)
SLOT = {1: 0, 3: 1, 2: 2}
COPIES = 256
COLS_MLP, COLS_OUT, COLS_QKV = 1152, 256, 512
FIRST = {COLS_MLP: 640, COLS_OUT: 128, COLS_QKV: 256}


def mm(left, right):
    return jnp.dot(left, right, preferred_element_type=F32)


def mm_last(left, right):
    return lax.dot_general(left, right, (((1,), (1,)), ((), ())), preferred_element_type=F32)


def mm_first(left, right):
    return lax.dot_general(left, right, (((0,), (0,)), ((), ())), preferred_element_type=F32)


def rms_scale(rows):
    return lax.rsqrt(jnp.mean(rows * rows, -1, keepdims=True) + EPSILON)


def swap_halves(heads):
    return pltpu.roll(heads, HEAD_DIM // 2, 1)


def rope_split(table):
    lane = lax.broadcasted_iota(jnp.int32, table.shape, 1)
    other = swap_halves(table)
    cosine = jnp.where(lane < HEAD_DIM // 2, table, other)
    sine = jnp.where(lane < HEAD_DIM // 2, -other, table)
    return cosine, sine


class Remote:
    def __init__(self, sems, src, dst, device, landing):
        send, recv, index = sems
        self.out = pltpu.make_async_remote_copy(
            src_ref=src,
            dst_ref=dst,
            send_sem=send.at[index],
            recv_sem=recv.at[index],
            device_id=device,
            device_id_type=MESH,
        )
        self.into = pltpu.make_async_remote_copy(
            src_ref=landing,
            dst_ref=landing,
            send_sem=send.at[index],
            recv_sem=recv.at[index],
            device_id=device,
            device_id_type=MESH,
        )

    def start(self):
        self.out.start()
        return self

    def wait_send(self):
        self.out.wait_send()

    def wait_recv(self):
        self.into.wait_recv()


def kernel(
    tok_ref, cot_ref, wq, wk, wv, wo, wg, wu, wd, ng_ref, mg_ref, qg_ref, kg_ref, rope_hbm,
    mixed_ref, ig_ref, out_m, out_o, out_a, gains_ref,
    g1, g2, g3, g4, w_a, w_o, w_m, raw, qh, kk, vx, rope, oa, att, do, dq, dk, dv, dqkv,
    hid, dgu, lse_row, delta_row, resid, d_resid,
    rs_send, rs_sib, rs_x, dkv_send, dkv_recv,
    gw_m, gw_o, gw_a, z1_m, z1_o, z1_a, y1_m, y1_o, y1_a,
    z2s_m, z2s_o, z2s_a, y2s_m, y2s_o, y2s_a, y2_m, y2_o, y2_a, z2_m, z2_o, z2_a,
    f_m, f_o, f_a, gain_own, gain_sib, gain_x, gain_y, gain_z,
    send, recv, local_sem,
):
    f_index = lax.axis_index("fsdp")
    c_index = lax.axis_index("ctx")
    z = lax.rem(f_index, 4)
    ylo = lax.div(f_index, 4)
    core = lax.rem(c_index, 2)
    x = lax.rem(lax.div(c_index, 2), 4)
    yhi = lax.div(c_index, 8)
    y = yhi * 2 + ylo
    slice_index = x * 2 + core

    def wrap(value):
        return lax.rem(value + 8, 4)

    def device(dx=0, dy=0, dz=0, dcore=0):
        to_x, to_y, to_z = wrap(x + dx), wrap(y + dy), wrap(z + dz)
        to_core = lax.rem(core + dcore, 2)
        return {
            "fsdp": lax.rem(to_y, 2) * 4 + to_z,
            "ctx": lax.div(to_y, 2) * 8 + to_x * 2 + to_core,
        }

    counter = [0]

    def sems():
        index = counter[0]
        counter[0] += 1
        assert index < COPIES
        return (send, recv, index)

    pending = []

    def remote(src, dst, to, landing):
        copy = Remote(sems(), src, dst, to, landing)
        copy.start()
        pending.append(copy)
        return copy

    def drain():
        while pending:
            pending.pop().wait_send()

    def rows(which):
        return pl.ds(pl.multiple_of(which * 128, 128), 128)

    mine, theirs = rows(core), rows(1 - core)
    sibling = device(dcore=1)
    partners = [sibling]
    partners += [device(dx=d) for d in DIST]
    partners += [device(dy=d) for d in DIST]
    partners += [device(dz=d) for d in DIST]
    partners += [device(dx=d, dy=2) for d in DIST]

    def columns(ref, width):
        return ref.at[:, pl.ds(pl.multiple_of(slice_index * width, 128), width)]

    local = []

    def fetch(src, dst):
        copy = pltpu.make_async_copy(src, dst, local_sem.at[len(local)])
        copy.start()
        local.append(copy)
        return copy

    fetch_a = [
        fetch(columns(wq, 256), w_a.at[f_index, :, 0:256]),
        fetch(columns(wk, 128), w_a.at[f_index, :, 256:384]),
        fetch(columns(wv, 128), w_a.at[f_index, :, 384:512]),
    ]
    fetch_o = [fetch(columns(wo, 256), w_o.at[f_index])]
    fetch_m = [
        fetch(columns(wg, 384), w_m.at[f_index, :, 0:384]),
        fetch(columns(wu, 384), w_m.at[f_index, :, 384:768]),
        fetch(columns(wd, 384), w_m.at[f_index, :, 768:1152]),
    ]
    fetch_rope = fetch(rope_hbm.at[pl.ds(yhi * 4, 4)], rope)

    barrier = pltpu.get_barrier_semaphore()
    for partner in partners:
        pl.semaphore_signal(barrier, inc=1, device_id=partner, device_id_type=MESH)

    class Gather:
        def __init__(self, ref):
            self.ref = ref
            own = ref.at[x, mine]
            self.ring = {
                d: remote(own, own, device(dx=d), ref.at[wrap(x - d), mine]) for d in DIST
            }
            self.pair = {0: remote(own, own, sibling, ref.at[x, theirs])}

        def forward(self, d):
            self.ring[d].wait_recv()
            block = self.ref.at[wrap(x - d), mine]
            self.pair[d] = remote(block, block, sibling, self.ref.at[wrap(x - d), theirs])

        def ready(self, d):
            self.pair[d].wait_recv()

    class Scatter:
        def __init__(self, index, buffer):
            self.part = rs_send.at[buffer]
            self.pair = rs_sib.at[index]
            self.ring = rs_x.at[index]
            self.pair_copy = {}
            self.ring_copy = {}

        def emit(self, d, value):
            self.part[d] = value.astype(BF16)
            self.pair_copy[d] = remote(
                self.part.at[d, theirs], self.pair.at[d], sibling, self.pair.at[d]
            )

        def forward(self, d):
            self.pair_copy[d].wait_recv()
            total = self.part[d, mine, :].astype(F32) + self.pair[d].astype(F32)
            self.pair[d] = total.astype(BF16)
            slot = self.ring.at[SLOT[d]]
            self.ring_copy[d] = remote(self.pair.at[d], slot, device(dx=d), slot)

        def release(self):
            for copy in self.pair_copy.values():
                copy.wait_send()
                pending.remove(copy)

        def total(self):
            self.pair_copy[0].wait_recv()
            value = self.part[0, mine, :].astype(F32) + self.pair[0].astype(F32)
            for d in DIST:
                self.ring_copy[d].wait_recv()
                value = value + self.ring[SLOT[d]].astype(F32)
            return value

    class WeightGather:
        def __init__(self, ref, fetched):
            self.ref = ref
            for copy in fetched:
                copy.wait()
            own = ref.at[f_index]
            self.along_z = {
                d: remote(own, own, device(dz=d), ref.at[ylo * 4 + wrap(z - d)]) for d in DIST
            }
            self.along_y = []
            self.spread(0)

        def spread(self, d):
            if d:
                self.along_z[d].wait_recv()
            held = ylo * 4 + wrap(z - d)
            coming = (1 - ylo) * 4 + wrap(z - d)
            for dy, part in ((1, pl.ds(0, 64)), (3, pl.ds(64, 64))):
                block = self.ref.at[held, part]
                self.along_y.append(
                    remote(block, block, device(dy=dy), self.ref.at[coming, part])
                )

        def finish(self):
            for copy in self.along_y:
                copy.wait_recv()

    class WeightGrad:
        def __init__(self, cols, gw, z1, y1, z2s, y2s, y2, z2, full, out):
            self.cols, self.gw, self.z1, self.y1 = cols, gw, z1, y1
            self.z2s, self.y2s, self.y2, self.z2 = z2s, y2s, y2, z2
            self.full, self.out = full, out
            self.left = slice(0, FIRST[cols])
            self.right = slice(FIRST[cols], cols)

        def stage_one(self):
            self.one_z, self.one_y = {}, {}
            for d in DIST:
                to_z, to_y = wrap(z + d), wrap(y + d)
                slot = self.z1.at[SLOT[d]]
                self.one_z[d] = remote(
                    self.gw.at[:, to_z, :, self.left], slot, device(dz=d), slot
                )
                slot = self.y1.at[SLOT[d]]
                half = pl.ds(pl.multiple_of(lax.div(to_y, 2) * 64, 64), 64)
                self.one_y[d] = remote(
                    self.gw.at[lax.rem(to_y, 2), :, half, self.right], slot, device(dy=d), slot
                )

        def stage_two(self):
            for d in DIST:
                self.one_z[d].wait_recv()
            total = self.gw[:, z, :, self.left].astype(F32)
            for d in DIST:
                total = total + self.z1[SLOT[d]].astype(F32)
            self.z2s[...] = total.astype(BF16).reshape(self.z2s.shape)
            self.two_y, self.two_z = {}, {}
            for d in DIST:
                to_y = wrap(y + d)
                slot = self.y2.at[SLOT[d]]
                self.two_y[d] = remote(
                    self.z2s.at[lax.rem(to_y, 2), lax.div(to_y, 2)], slot, device(dy=d), slot
                )
            for d in DIST:
                self.one_y[d].wait_recv()
            half = pl.ds(pl.multiple_of(yhi * 64, 64), 64)
            total = self.gw[ylo, :, half, self.right].astype(F32)
            for d in DIST:
                total = total + self.y1[SLOT[d]].astype(F32)
            self.y2s[...] = total.astype(BF16)
            for d in DIST:
                slot = self.z2.at[SLOT[d]]
                self.two_z[d] = remote(self.y2s.at[wrap(z + d)], slot, device(dz=d), slot)

        def stage_three(self):
            for d in DIST:
                self.two_y[d].wait_recv()
            total = self.z2s[ylo, yhi].astype(F32)
            for d in DIST:
                total = total + self.y2[SLOT[d]].astype(F32)
            self.full[yhi, x, core, :, self.left] = total.astype(BF16)
            for d in DIST:
                self.two_z[d].wait_recv()
            total = self.y2s[z].astype(F32)
            for d in DIST:
                total = total + self.z2[SLOT[d]].astype(F32)
            self.full[yhi, x, core, :, self.right] = total.astype(BF16)
            own = self.full.at[yhi, x, core]
            self.three = []
            for flip in (0, 1):
                for d in (0,) + DIST:
                    if d or flip:
                        from_hi = 1 - yhi if flip else yhi
                        self.three.append(
                            remote(
                                own, own, device(dx=d, dy=2 * flip),
                                self.full.at[from_hi, wrap(x - d), core],
                            )
                        )

        def stage_four(self):
            for copy in self.three:
                copy.wait_recv()
            held = self.full.at[:, :, core]
            self.four = remote(held, held, sibling, self.full.at[:, :, 1 - core])

        def stage_five(self):
            self.four.wait_recv()
            fetch(self.full, self.out)

    grad_m = WeightGrad(COLS_MLP, gw_m, z1_m, y1_m, z2s_m, y2s_m, y2_m, z2_m, f_m, out_m)
    grad_o = WeightGrad(COLS_OUT, gw_o, z1_o, y1_o, z2s_o, y2s_o, y2_o, z2_o, f_o, out_o)
    grad_a = WeightGrad(COLS_QKV, gw_a, z1_a, y1_a, z2s_a, y2s_a, y2_a, z2_a, f_a, out_a)

    def weight_grad(gw, parts):
        def chunk(index, carry):
            lanes = pl.ds(pl.multiple_of(index * 256, 256), 256)
            for left, right, cols in parts:
                value = mm_first(
                    left[:, :, lanes].reshape(1024, 256),
                    right[...].reshape(1024, right.shape[-1]),
                )
                block = pl.ds(lax.rem(index, 2) * 2, 2)
                gw[lax.div(index, 2), block, :, cols] = value.astype(BF16).reshape(
                    2, 128, right.shape[-1]
                )
            return carry

        lax.fori_loop(0, 4, chunk, 0)

    with jax.named_scope("first_norm"):
        inputs = tok_ref[...].astype(F32)
        g1[x, mine, :] = (inputs * rms_scale(inputs) * ng_ref[...]).astype(BF16)
        g3[x, mine, :] = cot_ref[...]
        vx[:, :, 128:256] = jnp.ones((8, 256, 128), BF16)
        gain_own[...] = jnp.zeros_like(gain_own)
    with jax.named_scope("entry_barrier"):
        pl.semaphore_wait(barrier, len(partners))
    with jax.named_scope("gather_start"):
        rows_one = Gather(g1)
        gather_a = WeightGather(w_a, fetch_a)
        for d in DIST:
            gather_a.spread(d)
            rows_one.forward(d)
        gather_o = WeightGather(w_o, fetch_o)
        gather_m = WeightGather(w_m, fetch_m)
        rows_cot = Gather(g3)
        gather_a.finish()
        fetch_rope.wait()

    def project(t):
        value = mm(g1[t], w_a[...].reshape(1024, COLS_QKV))
        cosine, sine = rope_split(rope[t])
        raw[t] = value[:, 0:384]
        for head in range(3):
            one = value[:, head * 128 : head * 128 + 128]
            gain = qg_ref[...] if head < 2 else kg_ref[...]
            scaled = one * rms_scale(one) * gain
            turned = (scaled * cosine + swap_halves(scaled) * sine).astype(BF16)
            if head < 2:
                qh[t, head * 256 : head * 256 + 256, :] = turned
            else:
                kk[yhi * 4 + t] = turned
        vx[yhi * 4 + t, :, 0:128] = value[:, 384:512].astype(BF16)

    with jax.named_scope("qkv"):
        for d in (0,) + DIST:
            rows_one.ready(d)
            project(wrap(x - d))

    across = device(dy=2)
    keys_half = kk.at[0:4]
    values_half = vx.at[0:4, :, 0:128]
    send_keys = Remote(sems(), keys_half, keys_half, across, keys_half)
    send_values = Remote(sems(), values_half, values_half, across, values_half)

    @pl.when(yhi == 0)
    def _():
        send_keys.start()
        send_values.start()

    def scores_full(i, key_rows):
        return jnp.exp2(mm_last(qh[i], key_rows) * SCALE_LOG2)

    def attend_own(i, carry):
        row = lax.broadcasted_iota(jnp.int32, (512, 256), 0)
        col = lax.broadcasted_iota(jnp.int32, (512, 256), 1)
        soft = jnp.where(col <= lax.rem(row, 256), scores_full(i, kk[yhi * 4 + i]), 0.0)
        oa[i] = mm(soft.astype(BF16), vx[yhi * 4 + i])

        def inner(j, carry):
            soft = scores_full(i, kk[yhi * 4 + j]).astype(BF16)
            oa[i] += mm(soft, vx[yhi * 4 + j])
            return carry

        lax.fori_loop(0, i, inner, 0)
        return carry

    with jax.named_scope("attend_own"):
        lax.fori_loop(0, 4, attend_own, 0)
    with jax.named_scope("spread_weights"):
        for d in DIST:
            gather_o.spread(d)
        for d in DIST:
            gather_m.spread(d)
        for d in DIST:
            rows_cot.forward(d)

    with jax.named_scope("attend_across"):

        @pl.when(yhi == 1)
        def _():
            send_keys.wait_recv()
            send_values.wait_recv()

            def attend_across(step, carry):
                i, j = lax.div(step, 2), lax.rem(step, 2)
                two = pl.ds(j * 2, 2)
                soft = scores_full(i, kk[two].reshape(512, 128)).astype(BF16)
                oa[i] += mm(soft, vx[two].reshape(512, 256))
                return carry

            lax.fori_loop(0, 8, attend_across, 0)

    with jax.named_scope("attend_end"):

        def attend_end(i, carry):
            both = oa[i]
            total = both[:, 128:256]
            exact = both[:, 0:128] / total
            oa[i, :, 0:128] = exact
            lse_row[i] = jnp.transpose(jnp.log(total) * math.log2(math.e))[0:8, :]
            att[i, :, 0:128] = exact[0:256].astype(BF16)
            att[i, :, 128:256] = exact[256:512].astype(BF16)
            return carry

        lax.fori_loop(0, 4, attend_end, 0)

    with jax.named_scope("branch"):
        gather_o.finish()
        branch = Scatter(0, 0)
        order = (2, 1, 3, 0)
        for place, d in enumerate(order):
            branch.emit(d, mm_last(att[wrap(x + d)], w_o[...].reshape(1024, COLS_OUT)))
            if place:
                branch.forward(order[place - 1])
    with jax.named_scope("resid"):
        value = branch.total() + tok_ref[...].astype(F32)
        resid[...] = value
        g2[x, mine, :] = (value * rms_scale(value) * mg_ref[...]).astype(BF16)
        rows_two = Gather(g2)
        gather_m.finish()
        branch.release()

    back_two = Scatter(1, 1)
    mlp_out = Scatter(2, 0)

    def feed_forward(d):
        t = wrap(x - d)
        w_gate_up = w_m[:, :, 0:768].reshape(1024, 768)
        w_d = w_m[:, :, 768:1152].reshape(1024, 384)
        both = mm(g2[t], w_gate_up)
        d_hidden = mm(g3[t], w_d)
        gate, up = both[:, 0:384], both[:, 384:768]
        sig = jax.nn.sigmoid(gate)
        active = gate * sig
        hid[t] = (active * up).astype(BF16)
        dgu[t, :, 0:384] = (d_hidden * up * sig * (1.0 + gate * (1.0 - sig))).astype(BF16)
        dgu[t, :, 384:768] = (d_hidden * active).astype(BF16)
        back_two.emit((4 - d) % 4, mm_last(dgu[t], w_gate_up))

    def feed_forward_out(d):
        w_d = w_m[:, :, 768:1152].reshape(1024, 384)
        mlp_out.emit((4 - d) % 4, mm_last(hid[wrap(x - d)], w_d))

    with jax.named_scope("mlp"):
        rows_cot.ready(0)
        rows_two.ready(0)
        feed_forward(0)
        for place, d in enumerate(DIST):
            rows_two.forward(d)
            rows_cot.ready(d)
            rows_two.ready(d)
            feed_forward(d)
            if place:
                back_two.forward((4 - DIST[place - 1]) % 4)
        back_two.forward(2)
    with jax.named_scope("mlp_out"):
        for place, d in enumerate((2, 1, 3, 0)):
            feed_forward_out(d)
            if place:
                mlp_out.forward((4 - (2, 1, 3)[place - 1]) % 4)
    with jax.named_scope("mlp_weight_grads"):
        weight_grad(gw_m, ((g2, dgu, slice(0, 768)), (g3, hid, slice(768, 1152))))
        grad_m.stage_one()
    with jax.named_scope("d_resid"):
        d_normed = back_two.total()
        value = resid[...]
        scaling = rms_scale(value)
        normed = value * scaling
        gain_own[0:1, :] = jnp.sum(d_normed * normed, 0, keepdims=True)
        d_normed = d_normed * mg_ref[...]
        value = scaling * (
            d_normed - normed * jnp.mean(d_normed * normed, -1, keepdims=True)
        ) + cot_ref[...].astype(F32)
        d_resid[...] = value
        g4[x, mine, :] = value.astype(BF16)
        rows_back = Gather(g4)
    with jax.named_scope("mixed"):
        mixed_ref[...] = (resid[...] + mlp_out.total()).astype(BF16)

    def back_out(t):
        value = mm(g4[t], w_o[...].reshape(1024, COLS_OUT)).astype(BF16)
        do[t, 0:256, :] = value[:, 0:128]
        do[t, 256:512, :] = value[:, 128:256]
        product = do[t].astype(F32) * oa[t, :, 0:128]
        delta_row[t] = jnp.broadcast_to(
            jnp.sum(jnp.transpose(product), 0, keepdims=True), (8, 512)
        )

    with jax.named_scope("d_attended"):
        rows_back.ready(0)
        back_out(x)
        for d in DIST:
            rows_back.forward(d)
            rows_back.ready(d)
            back_out(wrap(x - d))
    with jax.named_scope("out_weight_grads"):
        weight_grad(gw_o, ((g4, att, slice(0, 256)),))
        grad_o.stage_one()
        grad_m.stage_two()

    def tile(i, j, masked):
        key_rows, queries, grads = kk[j], qh[i], do[i]
        soft = jnp.exp2(mm_last(key_rows, queries) * SCALE_LOG2 - lse_row[i, 0:1, :])
        if masked:
            row = lax.broadcasted_iota(jnp.int32, (256, 512), 0)
            col = lax.broadcasted_iota(jnp.int32, (256, 512), 1)
            soft = jnp.where(row <= lax.rem(col, 256), soft, 0.0)
        d_soft = mm_last(vx[j, :, 0:128], grads)
        d_scores = (soft * (d_soft - delta_row[i, 0:1, :])).astype(BF16)
        dv[j] += mm(soft.astype(BF16), grads)
        dk[j] += mm(d_scores, queries)
        dq[i] += mm_first(d_scores, key_rows)

    with jax.named_scope("attend_back_across"):
        dq[...] = jnp.zeros_like(dq)
        dk[...] = jnp.zeros_like(dk)
        dv[...] = jnp.zeros_like(dv)

        send_back = Remote(sems(), dkv_send, dkv_recv, across, dkv_recv)

        @pl.when(yhi == 1)
        def _():
            def back_across(step, carry):
                tile(lax.rem(step, 4), lax.div(step, 4), False)
                return carry

            lax.fori_loop(0, 16, back_across, 0)
            dkv_send[0] = dk[0:4].astype(BF16)
            dkv_send[1] = dv[0:4].astype(BF16)
            send_back.start()

    with jax.named_scope("grad_stages"):
        grad_m.stage_three()
        grad_o.stage_two()

    with jax.named_scope("attend_back_own"):

        def back_own(i, carry):
            tile(i, yhi * 4 + i, True)

            def inner(j, carry):
                tile(i, yhi * 4 + j, False)
                return carry

            lax.fori_loop(0, i, inner, 0)
            return carry

        lax.fori_loop(0, 4, back_own, 0)

    with jax.named_scope("grad_stages_two"):
        grad_m.stage_four()
        grad_o.stage_three()

    with jax.named_scope("head_norm_back"):

        @pl.when(yhi == 0)
        def _():
            send_back.wait_recv()
            dk[0:4] += dkv_recv[0].astype(F32)
            dv[0:4] += dkv_recv[1].astype(F32)

        def head_back(t, carry):
            q_sum, k_sum = carry
            cosine, sine = rope_split(rope[t])
            for head in range(3):
                one = raw[t, :, head * 128 : head * 128 + 128]
                if head < 2:
                    grads, gain = dq[t, head * 256 : head * 256 + 256, :], qg_ref[...]
                else:
                    grads, gain = dk[yhi * 4 + t], kg_ref[...]
                grads = grads * SCALE
                grads = grads * cosine - swap_halves(grads) * sine
                scaling = rms_scale(one)
                normed = one * scaling
                part = jnp.sum(grads * normed, 0, keepdims=True)
                if head < 2:
                    q_sum = q_sum + part
                else:
                    k_sum = k_sum + part
                grads = grads * gain
                value = scaling * (grads - normed * jnp.mean(grads * normed, -1, keepdims=True))
                dqkv[t, :, head * 128 : head * 128 + 128] = value.astype(BF16)
            dqkv[t, :, 384:512] = dv[yhi * 4 + t].astype(BF16)
            return q_sum, k_sum

        zero = jnp.zeros((1, 128), F32)
        q_sum, k_sum = lax.fori_loop(0, 4, head_back, (zero, zero))
        gain_own[2:3, 0:128] = q_sum
        gain_own[2:3, 128:256] = k_sum

    with jax.named_scope("d_normed"):
        back_two.release()
        back_one = Scatter(3, 1)
        for place, d in enumerate(order):
            back_one.emit(d, mm_last(dqkv[wrap(x + d)], w_a[...].reshape(1024, COLS_QKV)))
            if place:
                back_one.forward(order[place - 1])
    with jax.named_scope("qkv_weight_grads"):
        weight_grad(gw_a, ((g1, dqkv, slice(0, 512)),))
        grad_a.stage_one()
        grad_m.stage_five()
        grad_o.stage_four()
    with jax.named_scope("input_grad"):
        d_normed = back_one.total()
        inputs = tok_ref[...].astype(F32)
        scaling = rms_scale(inputs)
        normed = inputs * scaling
        gain_own[1:2, :] = jnp.sum(d_normed * normed, 0, keepdims=True)
        d_normed = d_normed * ng_ref[...]
        ig_ref[...] = (
            scaling * (d_normed - normed * jnp.mean(d_normed * normed, -1, keepdims=True))
            + d_resid[...]
        )

    def ring_sum(slots, place, value, reach):
        slots[place] = value
        copies = []
        for d in DIST:
            own = slots.at[place]
            copies.append(remote(own, own, reach(d), slots.at[wrap(place - d)]))
        return copies

    def ring_total(slots, copies):
        for copy in copies:
            copy.wait_recv()
        return ((slots[0] + slots[1]) + slots[2]) + slots[3]

    with jax.named_scope("tail"):
        pair = remote(gain_own, gain_sib, sibling, gain_sib)
        pair.wait_recv()
        copies = ring_sum(gain_x, x, gain_own[...] + gain_sib[...], lambda d: device(dx=d))
        grad_a.stage_two()
        value = ring_total(gain_x, copies)
        copies = ring_sum(gain_y, y, value, lambda d: device(dy=d))
        grad_o.stage_five()
        grad_a.stage_three()
        value = ring_total(gain_y, copies)
        copies = ring_sum(gain_z, z, value, lambda d: device(dz=d))
        gains_ref[...] = ring_total(gain_z, copies)
        grad_a.stage_four()
        grad_a.stage_five()
    with jax.named_scope("drain"):
        drain()

        @pl.when(yhi == 0)
        def _():
            send_keys.wait_send()
            send_values.wait_send()

        @pl.when(yhi == 1)
        def _():
            send_back.wait_send()

        for copy in local[-3:]:
            copy.wait()


def rope_table(length):
    half = HEAD_DIM // 2
    freqs = np.power(np.float32(THETA), np.float32(-2.0) * np.arange(half, dtype=np.float32) / HEAD_DIM)
    angles = np.arange(length, dtype=np.float32)[:, None] * freqs.astype(np.float32)[None, :]
    table = np.concatenate([np.cos(angles), np.sin(angles)], 1).astype(np.float32)
    return table.reshape(length // 256, 256, HEAD_DIM)


def on_device(
    tokens, cotangent, w_query, w_key, w_value, w_output, w_gate, w_up, w_down,
    norm_gain, mlp_gain, query_gain, key_gain,
):
    vmem = pl.BlockSpec(memory_space=pltpu.VMEM)
    hbm = pl.BlockSpec(memory_space=pl.ANY)
    groups = (COLS_MLP, COLS_OUT, COLS_QKV)

    def v(shape, dtype=BF16):
        return pltpu.VMEM(shape, dtype)

    scratch = [v((4, 256, 1024)) for _ in range(4)]
    scratch += [v((8, 128, COLS_QKV)), v((8, 128, COLS_OUT)), v((8, 128, COLS_MLP))]
    scratch += [
        v((4, 256, 384), F32),
        v((4, 512, 128)),
        v((8, 256, 128)),
        v((8, 256, 256)),
        v((4, 256, 128), F32),
        v((4, 512, 256), F32),
        v((4, 256, 256)),
        v((4, 512, 128)),
        v((4, 512, 128), F32),
        v((8, 256, 128), F32),
        v((8, 256, 128), F32),
        v((4, 256, 512)),
        v((4, 256, 384)),
        v((4, 256, 768)),
        v((4, 8, 512), F32),
        v((4, 8, 512), F32),
        v((128, 1024), F32),
        v((128, 1024), F32),
        v((2, 4, 256, 1024)),
        v((4, 4, 128, 1024)),
        v((4, 3, 128, 1024)),
        v((2, 4, 256, 128)),
        v((2, 4, 256, 128)),
    ]
    scratch += [v((2, 4, 128, cols)) for cols in groups]
    scratch += [v((3, 2, 128, FIRST[cols])) for cols in groups]
    scratch += [v((3, 4, 64, cols - FIRST[cols])) for cols in groups]
    scratch += [v((2, 2, 64, FIRST[cols])) for cols in groups]
    scratch += [v((4, 64, cols - FIRST[cols])) for cols in groups]
    scratch += [v((3, 64, FIRST[cols])) for cols in groups]
    scratch += [v((3, 64, cols - FIRST[cols])) for cols in groups]
    scratch += [v((2, 4, 2, 64, cols)) for cols in groups]
    scratch += [v((8, 1024), F32), v((8, 1024), F32)]
    scratch += [v((4, 8, 1024), F32) for _ in range(3)]
    scratch += [
        pltpu.SemaphoreType.DMA((COPIES,)),
        pltpu.SemaphoreType.DMA((COPIES,)),
        pltpu.SemaphoreType.DMA((16,)),
    ]
    mixed, input_grad, full_m, full_o, full_a, gains = pl.pallas_call(
        kernel,
        name="layer",
        out_shape=(
            jax.ShapeDtypeStruct((128, 1024), BF16),
            jax.ShapeDtypeStruct((128, 1024), F32),
            *(jax.ShapeDtypeStruct((2, 4, 2, 64, cols), BF16) for cols in groups),
            jax.ShapeDtypeStruct((8, 1024), F32),
        ),
        in_specs=[vmem, vmem] + [hbm] * 7 + [vmem] * 4 + [hbm],
        out_specs=(vmem, vmem, hbm, hbm, hbm, vmem),
        scratch_shapes=scratch,
        compiler_params=pltpu.CompilerParams(
            collective_id=0, has_side_effects=True, vmem_limit_bytes=63 * 2**20
        ),
    )(
        tokens, cotangent, w_query, w_key, w_value, w_output, w_gate, w_up, w_down,
        norm_gain[None, :], mlp_gain[None, :], query_gain[None, :], key_gain[None, :],
        jnp.asarray(rope_table(2048)),
    )

    def whole(full, start, width):
        part = full[..., start : start + width].reshape(2, 8, 64, width)
        return part.transpose(0, 2, 1, 3).reshape(128, 8 * width).astype(F32)

    return (
        mixed,
        input_grad,
        whole(full_a, 0, 256),
        whole(full_a, 256, 128),
        whole(full_a, 384, 128),
        whole(full_o, 0, 256),
        whole(full_m, 0, 384),
        whole(full_m, 384, 384),
        whole(full_m, 768, 384),
        gains[1],
        gains[0],
        gains[2, 0:128],
        gains[2, 128:256],
    )


def solution(mesh):
    rows = P(("fsdp", "ctx"), None)
    weight = P("fsdp", None)
    return jax.shard_map(
        on_device,
        mesh=mesh,
        in_specs=(rows, rows) + (weight,) * 7 + (P(),) * 4,
        out_specs=(rows, rows) + (weight,) * 7 + (P(),) * 4,
        check_vma=False,
    )
```

```python
import math

import jax
import jax.numpy as jnp
import numpy as np
from jax import lax
from jax.experimental import pallas as pl
from jax.experimental.pallas import tpu as pltpu
from jax.sharding import PartitionSpec as P

MESH = pl.DeviceIdType.MESH
EPSILON = 1e-06
THETA = 1000000.0
HEAD_DIM = 128
SCALE = 1.0 / math.sqrt(HEAD_DIM)
SCALE_LOG2 = SCALE * math.log2(math.e)
F32 = jnp.float32
BF16 = jnp.bfloat16
DIST = (1, 3, 2)
SLOT = {1: 0, 3: 1, 2: 2}
COPIES = 205
LOCAL_COPIES = 18
COLS_MLP, COLS_OUT, COLS_QKV = 1152, 256, 512
FIRST = {COLS_MLP: 640, COLS_OUT: 128, COLS_QKV: 256}


def mm(left, right):
    return jnp.dot(left, right, preferred_element_type=F32)


def mm_last(left, right):
    return lax.dot_general(left, right, (((1,), (1,)), ((), ())), preferred_element_type=F32)


def mm_first(left, right):
    return lax.dot_general(left, right, (((0,), (0,)), ((), ())), preferred_element_type=F32)


def rms_scale(rows):
    return lax.rsqrt(jnp.mean(rows * rows, -1, keepdims=True) + EPSILON)


def swap_halves(heads):
    return pltpu.roll(heads, HEAD_DIM // 2, 1)


def rope_split(table):
    lane = lax.broadcasted_iota(jnp.int32, table.shape, 1)
    other = swap_halves(table)
    cosine = jnp.where(lane < HEAD_DIM // 2, table, other)
    sine = jnp.where(lane < HEAD_DIM // 2, -other, table)
    return cosine, sine


class Remote:
    def __init__(self, sems, src, dst, device, landing):
        self.sems, self.device = sems, device
        self.src, self.dst, self.landing = src, dst, landing

    def describe(self, src, dst):
        send, recv, index = self.sems
        return pltpu.make_async_remote_copy(
            src_ref=src,
            dst_ref=dst,
            send_sem=send.at[index],
            recv_sem=recv.at[index],
            device_id=self.device,
            device_id_type=MESH,
        )

    def start(self):
        self.describe(self.src, self.dst).start()

    def wait_send(self):
        self.describe(self.src, self.dst).wait_send()

    def wait_recv(self):
        self.describe(self.landing, self.landing).wait_recv()


def kernel(
    tok_hbm, cot_hbm, wq, wk, wv, wo, wg, wu, wd, ng_hbm, mg_hbm, qg_hbm, kg_hbm, rope_hbm,
    mixed_ref, ig_ref, out_m, out_o, out_a, gains_ref,
    tok, ng_ref, mg_ref, qg_ref, kg_ref,
    g1, g2, g3, g4, g1_turned, w_a, w_o, w_m, raw, qh, kk, vx, rope, oa, att, do, dq, dk, dv, dqkv,
    hid, dgu, lse_row, delta_row, resid, d_resid,
    rs_send, rs_sib, rs_x, dkv_send, dkv_recv,
    gw_m, gw_o, gw_a, z1_m, z1_o, z1_a, y1_m, y1_o, y1_a,
    z2s_m, z2s_o, z2s_a, y2s_m, y2s_o, y2s_a, y2_m, y2_o, y2_a, z2_m, z2_o, z2_a,
    f_m, f_o, f_a, gain_own, gain_sib, gain_x, gain_y, gain_z,
    send, recv, local_sem,
):
    f_index = lax.axis_index("fsdp")
    c_index = lax.axis_index("ctx")
    z = lax.rem(f_index, 4)
    ylo = lax.div(f_index, 4)
    core = lax.rem(c_index, 2)
    x = lax.rem(lax.div(c_index, 2), 4)
    yhi = lax.div(c_index, 8)
    y = yhi * 2 + ylo
    slice_index = x * 2 + core

    def wrap(value):
        return lax.rem(value + 8, 4)

    def device(dx=0, dy=0, dz=0, dcore=0):
        to_x, to_y, to_z = wrap(x + dx), wrap(y + dy), wrap(z + dz)
        to_core = lax.rem(core + dcore, 2)
        return {
            "fsdp": lax.rem(to_y, 2) * 4 + to_z,
            "ctx": lax.div(to_y, 2) * 8 + to_x * 2 + to_core,
        }

    counter = [0]

    def sems():
        index = counter[0]
        counter[0] += 1
        assert index < COPIES
        return (send, recv, index)

    pending = []

    def remote(src, dst, to, landing):
        copy = Remote(sems(), src, dst, to, landing)
        copy.start()
        pending.append(copy)
        return copy

    def drain():
        while pending:
            pending.pop().wait_send()

    def rows(start, size):
        return pl.ds(pl.multiple_of(start, size), size)

    sibling = device(dcore=1)
    partners = [sibling]
    partners += [device(dx=d) for d in DIST]
    partners += [device(dy=d) for d in DIST]
    partners += [device(dz=d) for d in DIST]
    partners += [device(dx=d, dy=2) for d in DIST]

    def columns(ref, width):
        return ref.at[:, pl.ds(pl.multiple_of(slice_index * width, 128), width)]

    local = []

    def fetch(src, dst):
        assert len(local) < LOCAL_COPIES
        copy = pltpu.make_async_copy(src, dst, local_sem.at[len(local)])
        copy.start()
        local.append(copy)
        return copy

    fetch_tok = [fetch(tok_hbm, tok), fetch(ng_hbm, ng_ref)]
    fetch_a = [
        fetch(columns(wq, 256), w_a.at[f_index, :, 0:256]),
        fetch(columns(wk, 128), w_a.at[f_index, :, 256:384]),
        fetch(columns(wv, 128), w_a.at[f_index, :, 384:512]),
    ]
    fetch_o = [fetch(columns(wo, 256), w_o.at[f_index])]
    fetch_m = [
        fetch(columns(wg, 384), w_m.at[f_index, :, 0:384]),
        fetch(columns(wu, 384), w_m.at[f_index, :, 384:768]),
        fetch(columns(wd, 384), w_m.at[f_index, :, 768:1152]),
    ]
    fetch_rest = [
        fetch(rope_hbm.at[pl.ds(yhi * 4, 4)], rope),
        fetch(cot_hbm.at[0:64], g3.at[0, x, rows(core * 64, 64)]),
        fetch(cot_hbm.at[64:128], g3.at[1, x, rows(core * 64, 64)]),
        fetch(mg_hbm, mg_ref),
        fetch(qg_hbm, qg_ref),
        fetch(kg_hbm, kg_ref),
    ]

    barrier = pltpu.get_barrier_semaphore()
    for partner in partners:
        pl.semaphore_signal(barrier, inc=1, device_id=partner, device_id_type=MESH)

    class Gather:
        def __init__(self, part, whole):
            self.part, self.whole = part, whole

            def to(dx, half):
                block = part(x, core, half)
                return remote(block, block, device(dx=dx), part(wrap(x - dx), core, half))

            self.plus = {0: to(1, 0)}
            self.minus = {1: to(3, 1)}
            self.plus[1] = to(1, 1)
            self.minus[0] = to(3, 0)
            own = whole(x, core)
            self.pair = {0: remote(own, own, sibling, whole(x, 1 - core))}

        def relay(self):
            self.plus[0].wait_recv()
            block = self.part(wrap(x - 1), core, 0)
            self.far_plus = remote(block, block, device(dx=1), self.part(wrap(x - 2), core, 0))
            self.minus[1].wait_recv()
            block = self.part(wrap(x + 1), core, 1)
            self.far_minus = remote(block, block, device(dx=3), self.part(wrap(x + 2), core, 1))

        def forward(self, d):
            if d == 1:
                self.plus[1].wait_recv()
            elif d == 3:
                self.minus[0].wait_recv()
            else:
                self.far_plus.wait_recv()
                self.far_minus.wait_recv()
            block = self.whole(wrap(x - d), core)
            self.pair[d] = remote(block, block, sibling, self.whole(wrap(x - d), 1 - core))

        def ready(self, d):
            self.pair[d].wait_recv()

    def gather_plain(ref):
        return Gather(
            lambda t, c, half: ref.at[t, rows(c * 128 + half * 64, 64)],
            lambda t, c: ref.at[t, rows(c * 128, 128)],
        )

    def gather_batch(ref, batch):
        return Gather(
            lambda t, c, half: ref.at[batch, t, rows(c * 64 + half * 32, 32)],
            lambda t, c: ref.at[batch, t, rows(c * 64, 64)],
        )

    def gather_batches(ref):
        return Gather(
            lambda t, c, half: ref.at[half, t, rows(c * 64, 64)],
            lambda t, c: ref.at[:, t, rows(c * 64, 64)],
        )

    class Scatter:
        def __init__(self, index, buffer, half, batch=0):
            self.half, self.batch = half, batch
            self.part, self.pair, self.ring = rs_send.at[buffer], rs_sib.at[index], rs_x.at[index]
            self.pair_copy, self.near, self.far = {}, {}, {}

        def part_rows(self, which, half=None):
            start = self.batch * 4 * self.half + which * 2 * self.half
            if half is None:
                return rows(start, 2 * self.half)
            return rows(start + half * self.half, self.half)

        def pair_rows(self, half=None):
            start = self.batch * 2 * self.half
            if half is None:
                return pl.ds(start, 2 * self.half)
            return pl.ds(start + half * self.half, self.half)

        def emit(self, d):
            slot = self.pair.at[d, self.pair_rows()]
            self.pair_copy[d] = remote(self.part.at[d, self.part_rows(1 - core)], slot, sibling, slot)

        def store(self, d, value):
            self.part[d, pl.ds(self.batch * 4 * self.half, 4 * self.half), :] = value.astype(BF16)
            self.emit(d)

        def summed(self, d, half=None):
            return self.part[d, self.part_rows(core, half), :].astype(F32) + self.pair[
                d, self.pair_rows(half), :
            ].astype(F32)

        def to(self, d, place, half, dx):
            slot = self.ring.at[place, self.pair_rows(half)]
            return remote(self.pair.at[d, self.pair_rows(half)], slot, device(dx=dx), slot)

        def forward(self, d):
            self.pair_copy[d].wait_recv()
            if d == 2:
                self.pair[d, self.pair_rows(), :] = self.summed(d).astype(BF16)
                self.far = {0: self.to(2, 2, 0, 1), 1: self.to(2, 2, 1, 3)}
            else:
                half, place = (1, 0) if d == 1 else (0, 1)
                self.pair[d, self.pair_rows(half), :] = self.summed(d, half).astype(BF16)
                self.near[d] = self.to(d, place, half, d)

        def relay(self):
            for d, half, place in ((1, 0, 0), (3, 1, 1)):
                self.far[half].wait_recv()
                value = self.summed(d, half) + self.ring[2, self.pair_rows(half), :].astype(F32)
                self.pair[d, self.pair_rows(half), :] = value.astype(BF16)
                self.near[d, half] = self.to(d, place, half, d)

        def total(self):
            self.pair_copy[0].wait_recv()
            value = self.summed(0)
            for d, half, place in ((1, 0, 0), (3, 1, 1)):
                self.near[d].wait_recv()
                self.near[d, half].wait_recv()
                value = value + self.ring[place, self.pair_rows(), :].astype(F32)
            return value

        def release(self):
            for copy in self.pair_copy.values():
                copy.wait_send()
                pending.remove(copy)

    class WeightGather:
        def __init__(self, ref, fetched):
            self.ref = ref
            for copy in fetched:
                copy.wait()
            own = ref.at[f_index]
            self.along_z = {
                d: remote(own, own, device(dz=d), ref.at[ylo * 4 + wrap(z - d)]) for d in DIST
            }
            held, coming = ref.at[pl.ds(ylo * 4, 4)], ref.at[pl.ds((1 - ylo) * 4, 4)]
            self.sems = sems()
            self.all_y = Remote(self.sems, held, held, device(dy=1), coming)
            self.spread(0)

        def spread(self, d):
            if d:
                self.along_z[d].wait_recv()
            held = ylo * 4 + wrap(z - d)
            for dy, part in ((1, pl.ds(0, 64)), (3, pl.ds(64, 64))):
                block = self.ref.at[held, part]
                Remote(self.sems, block, block, device(dy=dy), block).start()

        def finish(self):
            self.all_y.wait_recv()
            pending.append(self.all_y)

    class WeightGrad:
        def __init__(self, cols, gw, z1, y1, z2s, y2s, y2, z2, full, out):
            self.cols, self.gw, self.z1, self.y1 = cols, gw, z1, y1
            self.z2s, self.y2s, self.y2, self.z2 = z2s, y2s, y2, z2
            self.full, self.out = full, out
            self.left = slice(0, FIRST[cols])
            self.right = slice(FIRST[cols], cols)

        def stage_one(self):
            self.one_z, self.one_y = {}, {}
            for d in DIST:
                to_z, to_y = wrap(z + d), wrap(y + d)
                slot = self.z1.at[SLOT[d]]
                self.one_z[d] = remote(
                    self.gw.at[:, to_z, :, self.left], slot, device(dz=d), slot
                )
                slot = self.y1.at[SLOT[d]]
                half = rows(lax.div(to_y, 2) * 64, 64)
                self.one_y[d] = remote(
                    self.gw.at[lax.rem(to_y, 2), :, half, self.right], slot, device(dy=d), slot
                )

        def stage_two(self):
            for d in DIST:
                self.one_z[d].wait_recv()
            total = self.gw[:, z, :, self.left].astype(F32)
            for d in DIST:
                total = total + self.z1[SLOT[d]].astype(F32)
            self.z2s[...] = total.astype(BF16).reshape(self.z2s.shape)
            self.two_y, self.two_z = {}, {}
            for d in DIST:
                to_y = wrap(y + d)
                slot = self.y2.at[SLOT[d]]
                self.two_y[d] = remote(
                    self.z2s.at[lax.rem(to_y, 2), lax.div(to_y, 2)], slot, device(dy=d), slot
                )
            for d in DIST:
                self.one_y[d].wait_recv()
            total = self.gw[ylo, :, rows(yhi * 64, 64), self.right].astype(F32)
            for d in DIST:
                total = total + self.y1[SLOT[d]].astype(F32)
            self.y2s[...] = total.astype(BF16)
            for d in DIST:
                slot = self.z2.at[SLOT[d]]
                self.two_z[d] = remote(self.y2s.at[wrap(z + d)], slot, device(dz=d), slot)

        def stage_three(self):
            for d in DIST:
                self.two_y[d].wait_recv()
            total = self.z2s[ylo, yhi].astype(F32)
            for d in DIST:
                total = total + self.y2[SLOT[d]].astype(F32)
            self.full[yhi, x, core, :, self.left] = total.astype(BF16)
            for d in DIST:
                self.two_z[d].wait_recv()
            total = self.y2s[z].astype(F32)
            for d in DIST:
                total = total + self.z2[SLOT[d]].astype(F32)
            self.full[yhi, x, core, :, self.right] = total.astype(BF16)
            own = self.full.at[yhi, x, core]
            self.three = []
            for flip in (0, 1):
                for d in (0,) + DIST:
                    if d or flip:
                        from_hi = 1 - yhi if flip else yhi
                        self.three.append(
                            remote(
                                own, own, device(dx=d, dy=2 * flip),
                                self.full.at[from_hi, wrap(x - d), core],
                            )
                        )

        def stage_four(self):
            for copy in self.three:
                copy.wait_recv()
            held = self.full.at[:, :, core]
            self.four = remote(held, held, sibling, self.full.at[:, :, 1 - core])

        def stage_five(self):
            self.four.wait_recv()
            fetch(self.full, self.out)

    grad_m = WeightGrad(COLS_MLP, gw_m, z1_m, y1_m, z2s_m, y2s_m, y2_m, z2_m, f_m, out_m)
    grad_o = WeightGrad(COLS_OUT, gw_o, z1_o, y1_o, z2s_o, y2s_o, y2_o, z2_o, f_o, out_o)
    grad_a = WeightGrad(COLS_QKV, gw_a, z1_a, y1_a, z2s_a, y2s_a, y2_a, z2_a, f_a, out_a)

    def weight_grad(gw, parts, first, last):
        def chunk(index, carry):
            lanes = pl.ds(pl.multiple_of(index * 256, 256), 256)
            for left, right, cols, turned in parts:
                width = right.shape[-1]
                if turned:
                    value = mm(left[lanes, :], right[...].reshape(1024, width))
                else:
                    value = mm_first(
                        left[..., lanes].reshape(1024, 256), right[...].reshape(1024, width)
                    )
                block = pl.ds(lax.rem(index, 2) * 2, 2)
                gw[lax.div(index, 2), block, :, cols] = value.astype(BF16).reshape(2, 128, width)
            return carry

        lax.fori_loop(first, last, chunk, 0)

    with jax.named_scope("first_norm"):
        vx[:, :, 128:256] = jnp.ones((8, 256, 128), BF16)
        gain_own[...] = jnp.zeros_like(gain_own)
        for copy in fetch_tok:
            copy.wait()
        inputs = tok[...].astype(F32)
        g1[x, rows(core * 128, 128), :] = (inputs * rms_scale(inputs) * ng_ref[...]).astype(BF16)
    with jax.named_scope("entry_barrier"):
        pl.semaphore_wait(barrier, len(partners))
    with jax.named_scope("gather_start"):
        rows_one = gather_plain(g1)
        gather_a = WeightGather(w_a, fetch_a)
        rows_one.relay()
        for d in DIST:
            gather_a.spread(d)
            rows_one.forward(d)
        for copy in fetch_rest:
            copy.wait()
        gather_a.finish()
        gather_o = WeightGather(w_o, fetch_o)
        gather_m = WeightGather(w_m, fetch_m)
        rows_cot = gather_batches(g3)

    def project(t):
        value = mm(g1[t], w_a[...].reshape(1024, COLS_QKV))
        cosine, sine = rope_split(rope[t])
        raw[t] = value[:, 0:384]
        for head in range(3):
            one = value[:, head * 128 : head * 128 + 128]
            gain = qg_ref[...] if head < 2 else kg_ref[...]
            scaled = one * rms_scale(one) * gain
            turned = (scaled * cosine + swap_halves(scaled) * sine).astype(BF16)
            if head < 2:
                qh[t, head * 256 : head * 256 + 256, :] = turned
            else:
                kk[yhi * 4 + t] = turned
        vx[yhi * 4 + t, :, 0:128] = value[:, 384:512].astype(BF16)

    with jax.named_scope("qkv"):
        for d in (0,) + DIST:
            rows_one.ready(d)
            project(wrap(x - d))

    across = device(dy=2)
    keys_half = kk.at[0:4]
    values_half = vx.at[0:4, :, 0:128]
    send_keys = Remote(sems(), keys_half, keys_half, across, keys_half)
    send_values = Remote(sems(), values_half, values_half, across, values_half)

    @pl.when(yhi == 0)
    def _():
        send_keys.start()
        send_values.start()

    def scores_full(i, key_rows):
        return jnp.exp2(mm_last(qh[i], key_rows) * SCALE_LOG2)

    def attend_own(i, carry):
        row = lax.broadcasted_iota(jnp.int32, (512, 256), 0)
        col = lax.broadcasted_iota(jnp.int32, (512, 256), 1)
        soft = jnp.where(col <= lax.rem(row, 256), scores_full(i, kk[yhi * 4 + i]), 0.0)
        oa[i] = mm(soft.astype(BF16), vx[yhi * 4 + i])

        def inner(j, carry):
            soft = scores_full(i, kk[yhi * 4 + j]).astype(BF16)
            oa[i] += mm(soft, vx[yhi * 4 + j])
            return carry

        lax.fori_loop(0, i, inner, 0)
        return carry

    with jax.named_scope("attend_own"):
        lax.fori_loop(0, 4, attend_own, 0)
        rows_cot.relay()
        for d in DIST:
            gather_o.spread(d)
        gather_m.spread(1)

    def attend_across(i):
        @pl.when(yhi == 1)
        def _():
            def step(j, carry):
                two = pl.ds(j * 2, 2)
                soft = scores_full(i, kk[two].reshape(512, 128)).astype(BF16)
                oa[i] += mm(soft, vx[two].reshape(512, 256))
                return carry

            lax.fori_loop(0, 2, step, 0)

    def attend_end(i):
        both = oa[i]
        total = both[:, 128:256]
        exact = both[:, 0:128] / total
        oa[i, :, 0:128] = exact
        lse_row[i] = jnp.transpose(jnp.log(total) * math.log2(math.e))[0:8, :]
        exact = exact.astype(BF16)
        for head in range(2):
            for which in range(2):
                for batch in range(2):
                    start = head * 256 + which * 128 + batch * 64
                    att[batch, i, which * 64 : which * 64 + 64, head * 128 : head * 128 + 128] = (
                        exact[start : start + 64]
                    )

    branch = [Scatter(0, 0, 32, batch) for batch in range(2)]
    order = (2, 1, 3, 0)
    with jax.named_scope("attend_across"):
        @pl.when(yhi == 1)
        def _():
            send_keys.wait_recv()
            send_values.wait_recv()

        for place, d in enumerate(order):
            t = wrap(x + d)
            attend_across(t)
            attend_end(t)
            if place == 0:
                gather_o.finish()
            for batch in range(2):
                branch[batch].store(d, mm_last(att[batch, t], w_o[...].reshape(1024, COLS_OUT)))
            if place:
                for batch in range(2):
                    branch[batch].forward(order[place - 1])
            if place < 2:
                gather_m.spread(DIST[place + 1])
                rows_cot.forward(DIST[place])
            elif place == 2:
                rows_cot.forward(2)

    def batch_rows(batch):
        return slice(batch * 64, batch * 64 + 64)

    rows_two = []
    with jax.named_scope("resid"):
        for batch in range(2):
            branch[batch].relay()
        for batch in range(2):
            value = branch[batch].total() + tok[batch_rows(batch), :].astype(F32)
            resid[batch_rows(batch), :] = value
            g2[batch, x, rows(core * 64, 64), :] = (
                value * rms_scale(value) * mg_ref[...]
            ).astype(BF16)
            rows_two.append(gather_batch(g2, batch))
        g1_turned[...] = jnp.transpose(g1[...].reshape(1024, 1024))
        gather_m.finish()
        for batch in range(2):
            rows_two[batch].relay()
            branch[batch].release()

    back_two = [Scatter(1, 1, 32, batch) for batch in range(2)]

    def feed_forward(batch, d):
        t = wrap(x - d)
        rows_two[batch].ready(d)
        w_gate_up = w_m[:, :, 0:768].reshape(1024, 768)
        w_d = w_m[:, :, 768:1152].reshape(1024, 384)
        both = mm(g2[batch, t], w_gate_up)
        d_hidden = mm(g3[batch, t], w_d)
        gate, up = both[:, 0:384], both[:, 384:768]
        sig = jax.nn.sigmoid(gate)
        active = gate * sig
        hid[batch, t] = (active * up).astype(BF16)
        dgu[batch, t, :, 0:384] = (d_hidden * up * sig * (1.0 + gate * (1.0 - sig))).astype(BF16)
        dgu[batch, t, :, 384:768] = (d_hidden * active).astype(BF16)
        back_two[batch].store((4 - d) % 4, mm_last(dgu[batch, t], w_gate_up))

    with jax.named_scope("mlp"):
        for d in (0,) + DIST:
            rows_cot.ready(d)
        feed_forward(0, 0)
        rows_two[0].forward(1)
        rows_two[0].forward(3)
        feed_forward(1, 0)
        feed_forward(0, 1)
        rows_two[0].forward(2)
        feed_forward(0, 3)
        rows_two[1].forward(1)
        rows_two[1].forward(3)
        back_two[0].forward(3)
        feed_forward(0, 2)
        back_two[0].forward(1)
        feed_forward(1, 1)
        back_two[0].forward(2)
        rows_two[1].forward(2)
        feed_forward(1, 3)
        back_two[1].forward(3)
        back_two[1].forward(1)
        feed_forward(1, 2)
        back_two[0].relay()
        back_two[1].forward(2)

    mlp_grads = ((g2, dgu, slice(0, 768), False), (g3, hid, slice(768, 1152), False))
    rows_back = []

    def back_resid(batch):
        part = batch_rows(batch)
        d_normed = back_two[batch].total()
        value = resid[part, :]
        scaling = rms_scale(value)
        normed = value * scaling
        gain_own[0:1, :] += jnp.sum(d_normed * normed, 0, keepdims=True)
        d_normed = d_normed * mg_ref[...]
        value = scaling * (
            d_normed - normed * jnp.mean(d_normed * normed, -1, keepdims=True)
        ) + g3[batch, x, rows(core * 64, 64), :].astype(F32)
        d_resid[part, :] = value
        g4[batch, x, rows(core * 64, 64), :] = value.astype(BF16)
        rows_back.append(gather_batch(g4, batch))

    with jax.named_scope("d_resid"):
        back_resid(0)
        back_two[1].relay()
        weight_grad(gw_m, mlp_grads, 0, 2)
        back_resid(1)
        rows_back[0].relay()
        weight_grad(gw_m, mlp_grads, 2, 4)
        grad_m.stage_one()
        rows_back[1].relay()

    mlp_out = Scatter(2, 0, 64)

    def mlp_block(d):
        w_d = w_m[:, :, 768:1152].reshape(1024, 384)
        t = wrap(x + d)
        for batch in range(2):
            value = mm_last(hid[batch, t], w_d).astype(BF16)
            for which in range(2):
                start = which * 128 + batch * 64
                mlp_out.part[d, start : start + 64, :] = value[which * 64 : which * 64 + 64]
        mlp_out.emit(d)

    def back_out(t):
        for batch in range(2):
            value = mm(g4[batch, t], w_o[...].reshape(1024, COLS_OUT)).astype(BF16)
            for head in range(2):
                for which in range(2):
                    start = head * 256 + which * 128 + batch * 64
                    do[t, start : start + 64, :] = value[
                        which * 64 : which * 64 + 64, head * 128 : head * 128 + 128
                    ]
        product = do[t].astype(F32) * oa[t, :, 0:128]
        delta_row[t] = jnp.broadcast_to(
            jnp.sum(jnp.transpose(product), 0, keepdims=True), (8, 512)
        )

    def tile(i, start, size, masked):
        keys = pl.ds(start, size)
        width = 256 * size
        key_rows, queries, grads = kk[keys].reshape(width, 128), qh[i], do[i]
        soft = jnp.exp2(mm_last(key_rows, queries) * SCALE_LOG2 - lse_row[i, 0:1, :])
        if masked:
            row = lax.broadcasted_iota(jnp.int32, (width, 512), 0)
            col = lax.broadcasted_iota(jnp.int32, (width, 512), 1)
            soft = jnp.where(row <= lax.rem(col, 256), soft, 0.0)
        d_soft = mm_last(vx[keys, :, 0:128].reshape(width, 128), grads)
        d_scores = (soft * (d_soft - delta_row[i, 0:1, :])).astype(BF16)
        dv[keys] += mm(soft.astype(BF16), grads).reshape(size, 256, 128)
        dk[keys] += mm(d_scores, queries).reshape(size, 256, 128)
        dq[i] += mm_first(d_scores, key_rows)

    def back_across(t):
        @pl.when(yhi == 1)
        def _():
            def step(j, carry):
                tile(t, j * 2, 2, False)
                return carry

            lax.fori_loop(0, 2, step, 0)

    send_back = Remote(sems(), dkv_send, dkv_recv, across, dkv_recv)
    with jax.named_scope("attend_back_across"):
        dq[...] = jnp.zeros_like(dq)
        dk[...] = jnp.zeros_like(dk)
        dv[...] = jnp.zeros_like(dv)
        for place, d in enumerate((0,) + DIST):
            rows_back[0].ready(d)
            rows_back[1].ready(d)
            back_out(wrap(x - d))
            if place == 0:
                for batch in range(2):
                    rows_back[batch].forward(1)
                    rows_back[batch].forward(3)
            elif place == 1:
                for batch in range(2):
                    rows_back[batch].forward(2)
            elif place == 2:
                for to in order:
                    mlp_block(to)
            else:
                grad_m.stage_two()
                for to in order[:3]:
                    mlp_out.forward(to)
            back_across(wrap(x - d))

        @pl.when(yhi == 1)
        def _():
            dkv_send[0] = dk[0:4].astype(BF16)
            dkv_send[1] = dv[0:4].astype(BF16)
            send_back.start()

    with jax.named_scope("out_weight_grads"):
        weight_grad(gw_o, ((g4, att, slice(0, 256), False),), 0, 4)
        grad_o.stage_one()
        mlp_out.relay()
        grad_m.stage_three()

    with jax.named_scope("attend_back_own"):

        def back_own(i, carry):
            tile(i, yhi * 4 + i, 1, True)

            def inner(j, carry):
                tile(i, yhi * 4 + j, 1, False)
                return carry

            lax.fori_loop(0, i, inner, 0)
            return carry

        lax.fori_loop(0, 4, back_own, 0)

    with jax.named_scope("mixed"):
        grad_o.stage_two()
        mixed_ref[...] = (resid[...] + mlp_out.total()).astype(BF16)

    with jax.named_scope("head_norm_back"):

        @pl.when(yhi == 0)
        def _():
            send_back.wait_recv()
            dk[0:4] += dkv_recv[0].astype(F32)
            dv[0:4] += dkv_recv[1].astype(F32)

        def head_back(t, carry):
            q_sum, k_sum = carry
            cosine, sine = rope_split(rope[t])
            for head in range(3):
                one = raw[t, :, head * 128 : head * 128 + 128]
                if head < 2:
                    grads, gain = dq[t, head * 256 : head * 256 + 256, :], qg_ref[...]
                else:
                    grads, gain = dk[yhi * 4 + t], kg_ref[...]
                grads = grads * SCALE
                grads = grads * cosine - swap_halves(grads) * sine
                scaling = rms_scale(one)
                normed = one * scaling
                part = jnp.sum(grads * normed, 0, keepdims=True)
                if head < 2:
                    q_sum = q_sum + part
                else:
                    k_sum = k_sum + part
                grads = grads * gain
                value = scaling * (grads - normed * jnp.mean(grads * normed, -1, keepdims=True))
                dqkv[t, :, head * 128 : head * 128 + 128] = value.astype(BF16)
            dqkv[t, :, 384:512] = dv[yhi * 4 + t].astype(BF16)
            return q_sum, k_sum

        zero = jnp.zeros((1, 128), F32)
        q_sum, k_sum = lax.fori_loop(0, 4, head_back, (zero, zero))
        gain_own[2:3, 0:128] = q_sum
        gain_own[2:3, 128:256] = k_sum

    with jax.named_scope("qkv_weight_grads"):
        weight_grad(gw_a, ((g1_turned, dqkv, slice(0, 512), True),), 0, 4)
        grad_a.stage_one()
    with jax.named_scope("d_normed"):
        for batch in range(2):
            back_two[batch].release()
        back_one = Scatter(3, 1, 64)
        for place, d in enumerate(order):
            back_one.store(d, mm_last(dqkv[wrap(x + d)], w_a[...].reshape(1024, COLS_QKV)))
            if place:
                back_one.forward(order[place - 1])
        grad_m.stage_four()
        back_one.relay()
        grad_o.stage_three()
        grad_a.stage_two()
    with jax.named_scope("input_grad"):
        d_normed = back_one.total()
        inputs = tok[...].astype(F32)
        scaling = rms_scale(inputs)
        normed = inputs * scaling
        gain_own[1:2, :] = jnp.sum(d_normed * normed, 0, keepdims=True)
        d_normed = d_normed * ng_ref[...]
        ig_ref[...] = (
            scaling * (d_normed - normed * jnp.mean(d_normed * normed, -1, keepdims=True))
            + d_resid[...]
        )

    def ring_sum(slots, place, value, reach):
        slots[place] = value
        copies = []
        for d in DIST:
            own = slots.at[place]
            copies.append(remote(own, own, reach(d), slots.at[wrap(place - d)]))
        return copies

    def ring_total(slots, copies):
        for copy in copies:
            copy.wait_recv()
        return ((slots[0] + slots[1]) + slots[2]) + slots[3]

    with jax.named_scope("tail"):
        pair = remote(gain_own, gain_sib, sibling, gain_sib)
        grad_a.stage_three()
        pair.wait_recv()
        copies = ring_sum(gain_x, x, gain_own[...] + gain_sib[...], lambda d: device(dx=d))
        grad_m.stage_five()
        grad_o.stage_four()
        value = ring_total(gain_x, copies)
        copies = ring_sum(gain_y, y, value, lambda d: device(dy=d))
        grad_o.stage_five()
        value = ring_total(gain_y, copies)
        copies = ring_sum(gain_z, z, value, lambda d: device(dz=d))
        grad_a.stage_four()
        gains_ref[...] = ring_total(gain_z, copies)
        grad_a.stage_five()
    with jax.named_scope("drain"):
        drain()

        @pl.when(yhi == 0)
        def _():
            send_keys.wait_send()
            send_values.wait_send()

        @pl.when(yhi == 1)
        def _():
            send_back.wait_send()

        for copy in local[-3:]:
            copy.wait()


def rope_table(length):
    half = HEAD_DIM // 2
    freqs = np.power(np.float32(THETA), np.float32(-2.0) * np.arange(half, dtype=np.float32) / HEAD_DIM)
    angles = np.arange(length, dtype=np.float32)[:, None] * freqs.astype(np.float32)[None, :]
    table = np.concatenate([np.cos(angles), np.sin(angles)], 1).astype(np.float32)
    return table.reshape(length // 256, 256, HEAD_DIM)


def on_device(
    tokens, cotangent, w_query, w_key, w_value, w_output, w_gate, w_up, w_down,
    norm_gain, mlp_gain, query_gain, key_gain,
):
    vmem = pl.BlockSpec(memory_space=pltpu.VMEM)
    hbm = pl.BlockSpec(memory_space=pl.ANY)
    groups = (COLS_MLP, COLS_OUT, COLS_QKV)

    def v(shape, dtype=BF16):
        return pltpu.VMEM(shape, dtype)

    scratch = [v((128, 1024)), v((1, 1024), F32), v((1, 1024), F32), v((1, 128), F32), v((1, 128), F32)]
    scratch += [v((4, 256, 1024))]
    scratch += [v((2, 4, 128, 1024)) for _ in range(3)]
    scratch += [v((1024, 1024))]
    scratch += [v((8, 128, COLS_QKV)), v((8, 128, COLS_OUT)), v((8, 128, COLS_MLP))]
    scratch += [
        v((4, 256, 384), F32),
        v((4, 512, 128)),
        v((8, 256, 128)),
        v((8, 256, 256)),
        v((4, 256, 128), F32),
        v((4, 512, 256), F32),
        v((2, 4, 128, 256)),
        v((4, 512, 128)),
        v((4, 512, 128), F32),
        v((8, 256, 128), F32),
        v((8, 256, 128), F32),
        v((4, 256, 512)),
        v((2, 4, 128, 384)),
        v((2, 4, 128, 768)),
        v((4, 8, 512), F32),
        v((4, 8, 512), F32),
        v((128, 1024), F32),
        v((128, 1024), F32),
        v((2, 4, 256, 1024)),
        v((4, 4, 128, 1024)),
        v((4, 3, 128, 1024)),
        v((2, 4, 256, 128)),
        v((2, 4, 256, 128)),
    ]
    scratch += [v((2, 4, 128, cols)) for cols in groups]
    scratch += [v((3, 2, 128, FIRST[cols])) for cols in groups]
    scratch += [v((3, 4, 64, cols - FIRST[cols])) for cols in groups]
    scratch += [v((2, 2, 64, FIRST[cols])) for cols in groups]
    scratch += [v((4, 64, cols - FIRST[cols])) for cols in groups]
    scratch += [v((3, 64, FIRST[cols])) for cols in groups]
    scratch += [v((3, 64, cols - FIRST[cols])) for cols in groups]
    scratch += [v((2, 4, 2, 64, cols)) for cols in groups]
    scratch += [v((8, 1024), F32), v((8, 1024), F32)]
    scratch += [v((4, 8, 1024), F32) for _ in range(3)]
    scratch += [
        pltpu.SemaphoreType.DMA((COPIES,)),
        pltpu.SemaphoreType.DMA((COPIES,)),
        pltpu.SemaphoreType.DMA((LOCAL_COPIES,)),
    ]
    mixed, input_grad, full_m, full_o, full_a, gains = pl.pallas_call(
        kernel,
        name="layer",
        out_shape=(
            jax.ShapeDtypeStruct((128, 1024), BF16),
            jax.ShapeDtypeStruct((128, 1024), F32),
            *(jax.ShapeDtypeStruct((2, 4, 2, 64, cols), BF16) for cols in groups),
            jax.ShapeDtypeStruct((8, 1024), F32),
        ),
        in_specs=[hbm] * 14,
        out_specs=(vmem, vmem, hbm, hbm, hbm, vmem),
        scratch_shapes=scratch,
        compiler_params=pltpu.CompilerParams(
            collective_id=0, has_side_effects=True, vmem_limit_bytes=63 * 2**20
        ),
    )(
        tokens, cotangent, w_query, w_key, w_value, w_output, w_gate, w_up, w_down,
        norm_gain[None, :], mlp_gain[None, :], query_gain[None, :], key_gain[None, :],
        jnp.asarray(rope_table(2048)),
    )

    return pl.pallas_call(
        finish,
        name="finish",
        grid=(8,),
        out_shape=(
            jax.ShapeDtypeStruct((128, 1024), BF16),
            jax.ShapeDtypeStruct((128, 1024), F32),
            *(jax.ShapeDtypeStruct((128, 8 * width), F32) for width in (256, 128, 128, 256, 384, 384, 384)),
            jax.ShapeDtypeStruct((1024,), F32),
            jax.ShapeDtypeStruct((1024,), F32),
            jax.ShapeDtypeStruct((128,), F32),
            jax.ShapeDtypeStruct((128,), F32),
        ),
        in_specs=[
            pl.BlockSpec((16, 1024), lambda j: (j, 0)),
            pl.BlockSpec((16, 1024), lambda j: (j, 0)),
            *(pl.BlockSpec((2, 1, 64, cols), lambda j: (0, j, 0, 0)) for cols in groups),
            pl.BlockSpec((8, 1024), lambda j: (0, 0)),
        ],
        out_specs=(
            pl.BlockSpec((16, 1024), lambda j: (j, 0)),
            pl.BlockSpec((16, 1024), lambda j: (j, 0)),
            *(pl.BlockSpec((128, width), lambda j: (0, j)) for width in (256, 128, 128, 256, 384, 384, 384)),
            pl.BlockSpec((1024,), lambda j: (0,)),
            pl.BlockSpec((1024,), lambda j: (0,)),
            pl.BlockSpec((128,), lambda j: (0,)),
            pl.BlockSpec((128,), lambda j: (0,)),
        ),
    )(
        mixed, input_grad, full_m.reshape(2, 8, 64, COLS_MLP), full_o.reshape(2, 8, 64, COLS_OUT),
        full_a.reshape(2, 8, 64, COLS_QKV), gains,
    )


def finish(
    mixed, input_grad, full_m, full_o, full_a, gains,
    out_mixed, out_input, out_q, out_k, out_v, out_o, out_g, out_u, out_d,
    out_norm, out_mlp, out_qg, out_kg,
):
    out_mixed[...] = mixed[...]
    out_input[...] = input_grad[...]
    for out, full, start in (
        (out_q, full_a, 0), (out_k, full_a, 256), (out_v, full_a, 384), (out_o, full_o, 0),
        (out_g, full_m, 0), (out_u, full_m, 384), (out_d, full_m, 768),
    ):
        width = out.shape[1]
        for half in range(2):
            out[half * 64 : half * 64 + 64, :] = full[half, 0, :, start : start + width].astype(F32)

    @pl.when(pl.program_id(0) == 0)
    def _():
        out_norm[...] = gains[1, :]
        out_mlp[...] = gains[0, :]
        out_qg[...] = gains[2, 0:128]
        out_kg[...] = gains[2, 128:256]


def solution(mesh):
    rows = P(("fsdp", "ctx"), None)
    weight = P("fsdp", None)
    return jax.shard_map(
        on_device,
        mesh=mesh,
        in_specs=(rows, rows) + (weight,) * 7 + (P(),) * 4,
        out_specs=(rows, rows) + (weight,) * 7 + (P(),) * 4,
        check_vma=False,
    )
```

```python
import math

import jax
import jax.numpy as jnp
import numpy as np
from jax import lax
from jax.experimental import pallas as pl
from jax.experimental.pallas import tpu as pltpu
from jax.sharding import PartitionSpec as P

MESH = pl.DeviceIdType.MESH
EPSILON = 1e-06
THETA = 1000000.0
HEAD_DIM = 128
SCALE = 1.0 / math.sqrt(HEAD_DIM)
SCALE_LOG2 = SCALE * math.log2(math.e)
F32 = jnp.float32
BF16 = jnp.bfloat16
DIST = (1, 3, 2)
SLOT = {1: 0, 3: 1, 2: 2}
COPIES = 187
LOCAL_COPIES = 20
COLS_MLP, COLS_OUT, COLS_QKV = 1152, 256, 512
GROUPS = {"m1": (640, 128), "m2": (512, 128), "o": (256, 128), "q": (256, 128), "kv": (256, 128)}


def mm(left, right):
    return jnp.dot(left, right, preferred_element_type=F32)


def mm_last(left, right):
    return lax.dot_general(left, right, (((1,), (1,)), ((), ())), preferred_element_type=F32)


def mm_first(left, right):
    return lax.dot_general(left, right, (((0,), (0,)), ((), ())), preferred_element_type=F32)


def rms_scale(rows):
    return lax.rsqrt(jnp.mean(rows * rows, -1, keepdims=True) + EPSILON)


def swap_halves(heads):
    return pltpu.roll(heads, HEAD_DIM // 2, 1)


def rope_split(table):
    lane = lax.broadcasted_iota(jnp.int32, table.shape, 1)
    other = swap_halves(table)
    cosine = jnp.where(lane < HEAD_DIM // 2, table, other)
    sine = jnp.where(lane < HEAD_DIM // 2, -other, table)
    return cosine, sine


class Remote:
    def __init__(self, sems, src, dst, device, landing):
        self.sems, self.device = sems, device
        self.src, self.dst, self.landing = src, dst, landing

    def describe(self, src, dst, device):
        send, recv, index = self.sems
        return pltpu.make_async_remote_copy(
            src_ref=src,
            dst_ref=dst,
            send_sem=send.at[index],
            recv_sem=recv.at[index],
            device_id=device,
            device_id_type=MESH,
        )

    def launch(self, src, dst, device):
        self.describe(src, dst, device).start()

    def start(self):
        self.launch(self.src, self.dst, self.device)

    def wait_send(self):
        self.describe(self.src, self.dst, self.device).wait_send()

    def wait_recv(self):
        self.describe(self.landing, self.landing, self.device).wait_recv()


def kernel(
    tok_hbm, cot_hbm, wq, wk, wv, wo, wg, wu, wd, ng_hbm, mg_hbm, qg_hbm, kg_hbm, rope_hbm,
    mixed_ref, ig_ref, out, gains_ref,
    tok, ng_ref, mg_ref, qg_ref, kg_ref,
    g1, g2, g3, g4, g1_turned, w_a, w_o, w_m, raw, qh, kv, rope, oa, att, do, dq, dk, dv, dqkv,
    hid, dgu, lse_row, delta_row, resid, d_resid,
    rs_send, rs_sib, rs_x, dkv_send, dkv_recv, gain_early, early_x, early_yz, late_x, late_yz,
    gw, z1, y1, z2s, y2s, y2, z2, full, send, recv, local_sem,
):
    f_index = lax.axis_index("fsdp")
    c_index = lax.axis_index("ctx")
    z = lax.rem(f_index, 4)
    ylo = lax.div(f_index, 4)
    core = lax.rem(c_index, 2)
    x = lax.rem(lax.div(c_index, 2), 4)
    yhi = lax.div(c_index, 8)
    y = yhi * 2 + ylo
    slice_index = x * 2 + core

    def wrap(value):
        return lax.rem(value + 8, 4)

    def device(dx=0, dy=0, dz=0, dcore=0):
        to_x, to_y, to_z = wrap(x + dx), wrap(y + dy), wrap(z + dz)
        to_core = lax.rem(core + dcore, 2)
        return {
            "fsdp": lax.rem(to_y, 2) * 4 + to_z,
            "ctx": lax.div(to_y, 2) * 8 + to_x * 2 + to_core,
        }

    counter = [0]

    def sems():
        index = counter[0]
        counter[0] += 1
        assert index < COPIES
        return (send, recv, index)

    pending = []

    def remote(src, dst, to, landing):
        copy = Remote(sems(), src, dst, to, landing)
        copy.start()
        pending.append(copy)
        return copy

    def several(copies, total):
        copy = Remote(sems(), total, total, sibling, total)
        for src, dst, to in copies:
            copy.launch(src, dst, to)
        pending.append(copy)
        return copy

    def drain():
        while pending:
            pending.pop().wait_send()

    def rows(start, size):
        return pl.ds(pl.multiple_of(start, size), size)

    sibling = device(dcore=1)
    partners = [sibling]
    partners += [device(dx=d) for d in DIST]
    partners += [device(dy=d) for d in DIST]
    partners += [device(dx=d, dcore=1) for d in DIST]
    partners += [device(dz=d) for d in DIST]
    partners += [device(dy=a, dz=b) for a in DIST for b in DIST]
    partners += [device(dx=d, dy=2) for d in DIST]

    def columns(ref, width):
        return ref.at[:, pl.ds(pl.multiple_of(slice_index * width, 128), width)]

    local = []

    def fetch(src, dst):
        assert len(local) < LOCAL_COPIES
        copy = pltpu.make_async_copy(src, dst, local_sem.at[len(local)])
        copy.start()
        local.append(copy)
        return copy

    fetch_tok = [fetch(tok_hbm, tok), fetch(ng_hbm, ng_ref)]
    fetch_a = [
        fetch(columns(wq, 256), w_a.at[f_index, :, 0:256]),
        fetch(columns(wk, 128), w_a.at[f_index, :, 256:384]),
        fetch(columns(wv, 128), w_a.at[f_index, :, 384:512]),
    ]
    fetch_o = [fetch(columns(wo, 256), w_o.at[f_index])]
    fetch_m = [
        fetch(columns(wg, 384), w_m.at[f_index, :, 0:384]),
        fetch(columns(wu, 384), w_m.at[f_index, :, 384:768]),
        fetch(columns(wd, 384), w_m.at[f_index, :, 768:1152]),
    ]
    fetch_rest = [
        fetch(rope_hbm.at[pl.ds(yhi * 4, 4)], rope),
        fetch(cot_hbm.at[0:64], g3.at[0, x, rows(core * 64, 64)]),
        fetch(cot_hbm.at[64:128], g3.at[1, x, rows(core * 64, 64)]),
        fetch(mg_hbm, mg_ref),
        fetch(qg_hbm, qg_ref),
        fetch(kg_hbm, kg_ref),
    ]

    barrier = pltpu.get_barrier_semaphore()
    for partner in partners:
        pl.semaphore_signal(barrier, inc=1, device_id=partner, device_id_type=MESH)

    class Gather:
        def __init__(self, part, whole):
            self.part, self.whole = part, whole

            def to(dx, half):
                block = part(x, core, half)
                return remote(block, block, device(dx=dx), part(wrap(x - dx), core, half))

            self.plus = {0: to(1, 0)}
            self.minus = {1: to(3, 1)}
            self.plus[1] = to(1, 1)
            self.minus[0] = to(3, 0)
            own = whole(x, core)
            self.pair = {0: remote(own, own, sibling, whole(x, 1 - core))}

        def relay(self):
            self.plus[0].wait_recv()
            block = self.part(wrap(x - 1), core, 0)
            self.far_plus = remote(block, block, device(dx=1), self.part(wrap(x - 2), core, 0))
            self.minus[1].wait_recv()
            block = self.part(wrap(x + 1), core, 1)
            self.far_minus = remote(block, block, device(dx=3), self.part(wrap(x + 2), core, 1))

        def forward(self, d):
            if d == 1:
                self.plus[1].wait_recv()
            elif d == 3:
                self.minus[0].wait_recv()
            else:
                self.far_plus.wait_recv()
                self.far_minus.wait_recv()
            block = self.whole(wrap(x - d), core)
            self.pair[d] = remote(block, block, sibling, self.whole(wrap(x - d), 1 - core))

        def ready(self, d):
            self.pair[d].wait_recv()

    def gather_plain(ref):
        return Gather(
            lambda t, c, half: ref.at[t, rows(c * 128 + half * 64, 64)],
            lambda t, c: ref.at[t, rows(c * 128, 128)],
        )

    def gather_batch(ref, batch):
        return Gather(
            lambda t, c, half: ref.at[batch, t, rows(c * 64 + half * 32, 32)],
            lambda t, c: ref.at[batch, t, rows(c * 64, 64)],
        )

    def gather_batches(ref):
        return Gather(
            lambda t, c, half: ref.at[half, t, rows(c * 64, 64)],
            lambda t, c: ref.at[:, t, rows(c * 64, 64)],
        )

    class Scatter:
        def __init__(self, index, buffer, half, batch=0):
            self.half, self.batch = half, batch
            self.part, self.pair, self.ring = rs_send.at[buffer], rs_sib.at[index], rs_x.at[index]
            self.pair_copy, self.near, self.far = {}, {}, {}

        def part_rows(self, which, half=None):
            start = self.batch * 4 * self.half + which * 2 * self.half
            if half is None:
                return rows(start, 2 * self.half)
            return rows(start + half * self.half, self.half)

        def pair_rows(self, half=None):
            start = self.batch * 2 * self.half
            if half is None:
                return pl.ds(start, 2 * self.half)
            return pl.ds(start + half * self.half, self.half)

        def emit(self, d):
            slot = self.pair.at[d, self.pair_rows()]
            self.pair_copy[d] = remote(self.part.at[d, self.part_rows(1 - core)], slot, sibling, slot)

        def store(self, d, value):
            self.part[d, pl.ds(self.batch * 4 * self.half, 4 * self.half), :] = value.astype(BF16)
            self.emit(d)

        def summed(self, d, half=None):
            return self.part[d, self.part_rows(core, half), :].astype(F32) + self.pair[
                d, self.pair_rows(half), :
            ].astype(F32)

        def to(self, d, place, half, dx):
            slot = self.ring.at[place, self.pair_rows(half)]
            return remote(self.pair.at[d, self.pair_rows(half)], slot, device(dx=dx), slot)

        def forward(self, d):
            self.pair_copy[d].wait_recv()
            if d == 2:
                self.pair[d, self.pair_rows(), :] = self.summed(d).astype(BF16)
                self.far = {0: self.to(2, 2, 0, 1), 1: self.to(2, 2, 1, 3)}
            else:
                half, place = (1, 0) if d == 1 else (0, 1)
                self.pair[d, self.pair_rows(half), :] = self.summed(d, half).astype(BF16)
                self.near[d] = self.to(d, place, half, d)

        def relay(self):
            for d, half, place in ((1, 0, 0), (3, 1, 1)):
                self.far[half].wait_recv()
                value = self.summed(d, half) + self.ring[2, self.pair_rows(half), :].astype(F32)
                self.pair[d, self.pair_rows(half), :] = value.astype(BF16)
                self.near[d, half] = self.to(d, place, half, d)

        def total(self):
            self.pair_copy[0].wait_recv()
            value = self.summed(0)
            for d, half, place in ((1, 0, 0), (3, 1, 1)):
                self.near[d].wait_recv()
                self.near[d, half].wait_recv()
                value = value + self.ring[place, self.pair_rows(), :].astype(F32)
            return value

        def release(self):
            for copy in self.pair_copy.values():
                copy.wait_send()
                pending.remove(copy)

    class WeightGather:
        def __init__(self, ref, fetched):
            self.ref = ref
            for copy in fetched:
                copy.wait()
            own = ref.at[f_index]
            self.along_z = {
                d: remote(own, own, device(dz=d), ref.at[ylo * 4 + wrap(z - d)]) for d in DIST
            }
            held, coming = ref.at[pl.ds(ylo * 4, 4)], ref.at[pl.ds((1 - ylo) * 4, 4)]
            self.along_y = Remote(sems(), held, held, sibling, coming)

        def spread(self, d):
            if d:
                self.along_z[d].wait_recv()
            held = ylo * 4 + wrap(z - d)
            for dy, part in ((1, pl.ds(0, 64)), (3, pl.ds(64, 64))):
                block = self.ref.at[held, part]
                self.along_y.launch(block, block, device(dy=dy))

        def finish(self):
            self.along_y.wait_recv()
            pending.append(self.along_y)

    class WeightGrad:
        def __init__(self, name):
            cols, first = GROUPS[name]
            self.gw, self.z1, self.y1, self.z2s = gw[name], z1[name], y1[name], z2s[name]
            self.y2s, self.y2, self.z2 = y2s[name], y2[name], z2[name]
            self.full, self.out = full[name], out[name]
            self.left, self.right = slice(0, first), slice(first, cols)

        def stage_one(self):
            copies = []
            for d in DIST:
                src = self.gw.at[:, wrap(z + d), :, self.left]
                copies.append((src, self.z1.at[SLOT[d]], device(dz=d)))
            self.one_z = several(copies, self.z1)
            copies = []
            for d in DIST:
                to_y = wrap(y + d)
                half = rows(lax.div(to_y, 2) * 64, 64)
                src = self.gw.at[lax.rem(to_y, 2), :, half, self.right]
                copies.append((src, self.y1.at[SLOT[d]], device(dy=d)))
            self.one_y = several(copies, self.y1)

        def stage_two(self):
            self.one_z.wait_recv()
            total = self.gw[:, z, :, self.left].astype(F32)
            for d in DIST:
                total = total + self.z1[SLOT[d]].astype(F32)
            self.z2s[...] = total.astype(BF16).reshape(self.z2s.shape)
            copies = []
            for d in DIST:
                to_y = wrap(y + d)
                src = self.z2s.at[lax.rem(to_y, 2), lax.div(to_y, 2)]
                copies.append((src, self.y2.at[SLOT[d]], device(dy=d)))
            self.two_y = several(copies, self.y2)
            self.one_y.wait_recv()
            total = self.gw[ylo, :, rows(yhi * 64, 64), self.right].astype(F32)
            for d in DIST:
                total = total + self.y1[SLOT[d]].astype(F32)
            self.y2s[...] = total.astype(BF16)
            copies = []
            for d in DIST:
                copies.append((self.y2s.at[wrap(z + d)], self.z2.at[SLOT[d]], device(dz=d)))
            self.two_z = several(copies, self.z2)

        def sums(self):
            self.two_y.wait_recv()
            total = self.z2s[ylo, yhi].astype(F32)
            for d in DIST:
                total = total + self.y2[SLOT[d]].astype(F32)
            self.full[yhi, x, core, :, self.left] = total.astype(BF16)
            self.two_z.wait_recv()
            total = self.y2s[z].astype(F32)
            for d in DIST:
                total = total + self.z2[SLOT[d]].astype(F32)
            self.full[yhi, x, core, :, self.right] = total.astype(BF16)

        def stage_three(self):
            self.sums()
            own = self.full.at[yhi, x, core]
            self.flip = remote(own, own, device(dy=2), self.full.at[1 - yhi, x, core])

        def stage_four(self):
            self.flip.wait_recv()
            both = self.full.at[:, x, core]
            self.ring = [
                remote(both, both, device(dx=d), self.full.at[:, wrap(x - d), core]) for d in DIST
            ]

        def stage_direct(self):
            self.sums()
            own = self.full.at[yhi, x, core]
            self.ring = [
                remote(own, own, device(dx=d), self.full.at[yhi, wrap(x - d), core]) for d in DIST
            ]
            copies = [(own, own, device(dx=d, dy=2)) for d in (0,) + DIST]
            self.ring.append(several(copies, self.full.at[1 - yhi, :, core]))

        def stage_five(self):
            for copy in self.ring:
                copy.wait_recv()
            held = self.full.at[:, :, core]
            self.pair = remote(held, held, sibling, self.full.at[:, :, 1 - core])

        def stage_six(self):
            self.pair.wait_recv()
            fetch(self.full, self.out)

    grad_m1, grad_m2, grad_o = WeightGrad("m1"), WeightGrad("m2"), WeightGrad("o")
    grad_q, grad_kv = WeightGrad("q"), WeightGrad("kv")

    def weight_grad(parts):
        def chunk(index, carry):
            lanes = pl.ds(pl.multiple_of(index * 256, 256), 256)
            block = pl.ds(lax.rem(index, 2) * 2, 2)
            for left, right, source, target, cols, turned in parts:
                width = cols.stop - cols.start
                operand = right[..., source].reshape(1024, width)
                if turned:
                    value = mm(left[lanes, :], operand)
                else:
                    value = mm_first(left[..., lanes].reshape(1024, 256), operand)
                target[lax.div(index, 2), block, :, cols] = value.astype(BF16).reshape(
                    2, 128, width
                )
            return carry

        lax.fori_loop(0, 4, chunk, 0)

    with jax.named_scope("first_norm"):
        kv[:, :, 256:384] = jnp.ones((8, 256, 128), BF16)
        gain_early[...] = jnp.zeros_like(gain_early)
        for copy in fetch_tok:
            copy.wait()
        inputs = tok[...].astype(F32)
        g1[x, rows(core * 128, 128), :] = (inputs * rms_scale(inputs) * ng_ref[...]).astype(BF16)
    with jax.named_scope("entry_barrier"):
        pl.semaphore_wait(barrier, len(partners))
    with jax.named_scope("gather_start"):
        rows_one = gather_plain(g1)
        gather_a = WeightGather(w_a, fetch_a)
        gather_a.spread(0)
        rows_one.relay()
        for d in DIST:
            gather_a.spread(d)
            rows_one.forward(d)
        for copy in fetch_rest:
            copy.wait()
        gather_o = WeightGather(w_o, fetch_o)
        gather_a.finish()
        gather_o.spread(0)
        gather_m = WeightGather(w_m, fetch_m)
        rows_cot = gather_batches(g3)

    def project(t):
        value = mm(g1[t], w_a[...].reshape(1024, COLS_QKV))
        cosine, sine = rope_split(rope[t])
        raw[t] = value[:, 0:384]
        for head in range(3):
            one = value[:, head * 128 : head * 128 + 128]
            gain = qg_ref[...] if head < 2 else kg_ref[...]
            scaled = one * rms_scale(one) * gain
            turned = (scaled * cosine + swap_halves(scaled) * sine).astype(BF16)
            if head < 2:
                qh[t, head * 256 : head * 256 + 256, :] = turned
            else:
                kv[yhi * 4 + t, :, 0:128] = turned
        kv[yhi * 4 + t, :, 128:256] = value[:, 384:512].astype(BF16)

    across = device(dy=2)
    send_kv = {}
    with jax.named_scope("qkv"):
        for d in (0,) + DIST:
            rows_one.ready(d)
            project(wrap(x - d))
            block = kv.at[wrap(x - d), :, 0:256]
            send_kv[d] = Remote(sems(), block, block, across, block)

            @pl.when(yhi == 0)
            def _(copy=send_kv[d]):
                copy.start()

        for d in DIST:
            gather_o.spread(d)

    def add_scores(i, j):
        soft = jnp.exp2(mm_last(qh[i], kv[j, :, 0:128]) * SCALE_LOG2).astype(BF16)
        oa[i] += mm(soft, kv[j, :, 128:384])

    def attend_own(i, carry):
        j = yhi * 4 + i
        row = lax.broadcasted_iota(jnp.int32, (512, 256), 0)
        col = lax.broadcasted_iota(jnp.int32, (512, 256), 1)
        soft = jnp.exp2(mm_last(qh[i], kv[j, :, 0:128]) * SCALE_LOG2)
        soft = jnp.where(col <= lax.rem(row, 256), soft, 0.0)
        oa[i] = mm(soft.astype(BF16), kv[j, :, 128:384])

        def inner(k, carry):
            add_scores(i, yhi * 4 + k)
            return carry

        lax.fori_loop(0, i, inner, 0)
        return carry

    with jax.named_scope("attend_own"):
        lax.fori_loop(0, 4, attend_own, 0)
        rows_cot.relay()
        rows_cot.forward(1)
        rows_cot.forward(3)

    with jax.named_scope("attend_across"):

        @pl.when(yhi == 1)
        def _():
            for d in (0,) + DIST:
                send_kv[d].wait_recv()

                def step(i, carry, j=wrap(x - d)):
                    add_scores(i, j)
                    return carry

                lax.fori_loop(0, 4, step, 0)

        @pl.when(yhi == 0)
        def _():
            for d in (0,) + DIST:
                send_kv[d].wait_send()

        rows_cot.forward(2)
        gather_m.spread(0)
        gather_m.spread(1)
        gather_m.spread(3)

    def attend_end(i):
        both = oa[i]
        total = both[:, 128:256]
        exact = both[:, 0:128] / total
        oa[i, :, 0:128] = exact
        lse_row[i] = jnp.transpose(jnp.log(total) * math.log2(math.e))[0:8, :]
        exact = exact.astype(BF16)
        for head in range(2):
            for which in range(2):
                for batch in range(2):
                    start = head * 256 + which * 128 + batch * 64
                    att[batch, i, which * 64 : which * 64 + 64, head * 128 : head * 128 + 128] = (
                        exact[start : start + 64]
                    )

    branch = [Scatter(0, 0, 32, batch) for batch in range(2)]
    order = (2, 1, 3, 0)
    with jax.named_scope("branch"):
        gather_o.finish()
        for place, d in enumerate(order):
            t = wrap(x + d)
            attend_end(t)
            for batch in range(2):
                branch[batch].store(d, mm_last(att[batch, t], w_o[...].reshape(1024, COLS_OUT)))
            if place:
                for batch in range(2):
                    branch[batch].forward(order[place - 1])
        gather_m.spread(2)

    def batch_rows(batch):
        return slice(batch * 64, batch * 64 + 64)

    rows_two = []
    with jax.named_scope("resid"):
        for batch in range(2):
            branch[batch].relay()
        for batch in range(2):
            value = branch[batch].total() + tok[batch_rows(batch), :].astype(F32)
            resid[batch_rows(batch), :] = value
            g2[batch, x, rows(core * 64, 64), :] = (
                value * rms_scale(value) * mg_ref[...]
            ).astype(BF16)
            rows_two.append(gather_batch(g2, batch))
        g1_turned[...] = jnp.transpose(g1[...].reshape(1024, 1024))
        gather_m.finish()
        for batch in range(2):
            rows_two[batch].relay()
            branch[batch].release()

    back_two = [Scatter(1, 1, 32, batch) for batch in range(2)]

    def feed_forward(batch, d):
        t = wrap(x - d)
        rows_two[batch].ready(d)
        w_gate_up = w_m[:, :, 0:768].reshape(1024, 768)
        w_d = w_m[:, :, 768:1152].reshape(1024, 384)
        both = mm(g2[batch, t], w_gate_up)
        d_hidden = mm(g3[batch, t], w_d)
        gate, up = both[:, 0:384], both[:, 384:768]
        sig = jax.nn.sigmoid(gate)
        active = gate * sig
        hid[batch, t] = (active * up).astype(BF16)
        dgu[batch, t, :, 0:384] = (d_hidden * up * sig * (1.0 + gate * (1.0 - sig))).astype(BF16)
        dgu[batch, t, :, 384:768] = (d_hidden * active).astype(BF16)
        back_two[batch].store((4 - d) % 4, mm_last(dgu[batch, t], w_gate_up))

    with jax.named_scope("mlp"):
        for d in (0,) + DIST:
            rows_cot.ready(d)
        feed_forward(0, 0)
        rows_two[0].forward(1)
        rows_two[0].forward(3)
        feed_forward(1, 0)
        feed_forward(0, 1)
        rows_two[0].forward(2)
        feed_forward(0, 3)
        rows_two[1].forward(1)
        rows_two[1].forward(3)
        back_two[0].forward(3)
        feed_forward(0, 2)
        back_two[0].forward(1)
        feed_forward(1, 1)
        back_two[0].forward(2)
        rows_two[1].forward(2)
        feed_forward(1, 3)
        back_two[1].forward(3)
        back_two[1].forward(1)
        feed_forward(1, 2)
        back_two[0].relay()
        back_two[1].forward(2)

    grads_m1 = ((g2, dgu, slice(0, 640), grad_m1.gw, slice(0, 640), False),)
    grads_m2 = (
        (g2, dgu, slice(640, 768), grad_m2.gw, slice(0, 128), False),
        (g3, hid, slice(0, 384), grad_m2.gw, slice(128, 512), False),
    )
    grads_o = ((g4, att, slice(0, 256), grad_o.gw, slice(0, 256), False),)
    grads_q = ((g1_turned, dqkv, slice(0, 256), grad_q.gw, slice(0, 256), True),)
    grads_kv = ((g1_turned, dqkv, slice(256, 512), grad_kv.gw, slice(0, 256), True),)
    rows_back = []

    def back_resid(batch):
        part = batch_rows(batch)
        d_normed = back_two[batch].total()
        value = resid[part, :]
        scaling = rms_scale(value)
        normed = value * scaling
        gain_early[:, 0:1024] += jnp.sum(d_normed * normed, 0, keepdims=True)
        d_normed = d_normed * mg_ref[...]
        value = scaling * (
            d_normed - normed * jnp.mean(d_normed * normed, -1, keepdims=True)
        ) + g3[batch, x, rows(core * 64, 64), :].astype(F32)
        d_resid[part, :] = value
        g4[batch, x, rows(core * 64, 64), :] = value.astype(BF16)
        rows_back.append(gather_batch(g4, batch))

    with jax.named_scope("d_resid"):
        weight_grad(grads_m1)
        grad_m1.stage_one()
        back_resid(0)
        back_two[1].relay()
        back_resid(1)
        rows_back[0].relay()
        weight_grad(grads_m2)
        grad_m2.stage_one()
        rows_back[1].relay()

    mlp_out = Scatter(2, 0, 64)

    def mlp_block(d):
        w_d = w_m[:, :, 768:1152].reshape(1024, 384)
        t = wrap(x + d)
        for batch in range(2):
            value = mm_last(hid[batch, t], w_d).astype(BF16)
            for which in range(2):
                start = which * 128 + batch * 64
                mlp_out.part[d, start : start + 64, :] = value[which * 64 : which * 64 + 64]
        mlp_out.emit(d)

    def back_out(t):
        for batch in range(2):
            value = mm(g4[batch, t], w_o[...].reshape(1024, COLS_OUT)).astype(BF16)
            for head in range(2):
                for which in range(2):
                    start = head * 256 + which * 128 + batch * 64
                    do[t, start : start + 64, :] = value[
                        which * 64 : which * 64 + 64, head * 128 : head * 128 + 128
                    ]
        product = do[t].astype(F32) * oa[t, :, 0:128]
        delta_row[t] = jnp.broadcast_to(
            jnp.sum(jnp.transpose(product), 0, keepdims=True), (8, 512)
        )

    def tile(i, start, size, masked):
        keys = pl.ds(start, size)
        width = 256 * size
        key_rows, queries, grads = kv[keys, :, 0:128].reshape(width, 128), qh[i], do[i]
        soft = jnp.exp2(mm_last(key_rows, queries) * SCALE_LOG2 - lse_row[i, 0:1, :])
        if masked:
            row = lax.broadcasted_iota(jnp.int32, (width, 512), 0)
            col = lax.broadcasted_iota(jnp.int32, (width, 512), 1)
            soft = jnp.where(row <= lax.rem(col, 256), soft, 0.0)
        d_soft = mm_last(kv[keys, :, 128:256].reshape(width, 128), grads)
        d_scores = (soft * (d_soft - delta_row[i, 0:1, :])).astype(BF16)
        dv[keys] += mm(soft.astype(BF16), grads).reshape(size, 256, 128)
        dk[keys] += mm(d_scores, queries).reshape(size, 256, 128)
        dq[i] += mm_first(d_scores, key_rows)

    def back_across(t):
        @pl.when(yhi == 1)
        def _():
            def step(j, carry):
                tile(t, j * 2, 2, False)
                return carry

            lax.fori_loop(0, 2, step, 0)

    send_back = [
        Remote(sems(), dkv_send.at[pair], dkv_recv.at[pair], across, dkv_recv.at[pair])
        for pair in range(2)
    ]

    def back_across_end(pair):
        @pl.when(yhi == 1)
        def _():
            for d in (3, 2):
                tile(wrap(x - d), pair * 2, 2, False)
            two = slice(pair * 2, pair * 2 + 2)
            dkv_send[pair, :, :, 0:128] = dk[two].astype(BF16)
            dkv_send[pair, :, :, 128:256] = dv[two].astype(BF16)
            send_back[pair].start()

    def back_ready(d):
        for batch in range(2):
            rows_back[batch].ready(d)
        back_out(wrap(x - d))

    def back_forward(d):
        for batch in range(2):
            rows_back[batch].forward(d)

    with jax.named_scope("attend_back_across"):
        dq[...] = jnp.zeros_like(dq)
        dk[...] = jnp.zeros_like(dk)
        dv[...] = jnp.zeros_like(dv)
        back_ready(0)
        back_forward(1)
        back_forward(3)
        back_across(x)
        back_ready(1)
        back_forward(2)
        back_across(wrap(x - 1))
        back_ready(3)
        back_ready(2)
        for to in order:
            mlp_block(to)
        back_across_end(0)
        grad_m1.stage_two()
        for to in order[:3]:
            mlp_out.forward(to)
        back_across_end(1)
    with jax.named_scope("out_weight_grads"):
        weight_grad(grads_o)
        grad_o.stage_one()
        mlp_out.relay()
        grad_m2.stage_two()

    with jax.named_scope("attend_back_own"):

        def back_own(i, carry):
            tile(i, yhi * 4 + i, 1, True)

            def inner(j, carry):
                tile(i, yhi * 4 + j, 1, False)
                return carry

            lax.fori_loop(0, i, inner, 0)
            return carry

        lax.fori_loop(0, 3, back_own, 0)
        grad_m1.stage_three()
        lax.fori_loop(3, 4, back_own, 0)
        grad_m2.stage_three()

    with jax.named_scope("mixed"):
        mixed_ref[...] = (resid[...] + mlp_out.total()).astype(BF16)

    def head_back(t, head):
        cosine, sine = rope_split(rope[t])
        one = raw[t, :, head * 128 : head * 128 + 128]
        if head < 2:
            grads, gain = dq[t, head * 256 : head * 256 + 256, :], qg_ref[...]
        else:
            grads, gain = dk[yhi * 4 + t], kg_ref[...]
        grads = grads * SCALE
        grads = grads * cosine - swap_halves(grads) * sine
        scaling = rms_scale(one)
        normed = one * scaling
        part = jnp.sum(grads * normed, 0, keepdims=True)
        grads = grads * gain
        value = scaling * (grads - normed * jnp.mean(grads * normed, -1, keepdims=True))
        dqkv[t, :, head * 128 : head * 128 + 128] = value.astype(BF16)
        return part

    def query_back(t, carry):
        return carry + head_back(t, 0) + head_back(t, 1)

    def key_back(t, carry):
        dqkv[t, :, 384:512] = dv[yhi * 4 + t].astype(BF16)
        return carry + head_back(t, 2)

    def over_x(slots, value):
        slots[slice_index] = value
        own = slots.at[slice_index]
        copies = [(own, own, sibling)]
        copies += [(own, own, device(dx=d, dcore=flip)) for d in DIST for flip in (0, 1)]
        return several(copies, slots.at[0:7])

    def over_yz(slots, value):
        place = y * 4 + z
        slots[place] = value
        own = slots.at[place]
        steps = (0,) + DIST
        copies = [(own, own, device(dy=a, dz=b)) for a in steps for b in steps if a or b]
        return several(copies, slots.at[0:15])

    def total_of(slots, copies):
        copies.wait_recv()
        value = slots[0]
        for place in range(1, slots.shape[0]):
            value = value + slots[place]
        return value

    with jax.named_scope("head_norm_back"):
        zero = jnp.zeros((1, 128), F32)
        gain_early[:, 1024:1152] = lax.fori_loop(0, 4, query_back, zero)

    with jax.named_scope("qkv_weight_grads"):
        weight_grad(grads_q)
        grad_q.stage_one()
        grad_m1.stage_four()

        @pl.when(yhi == 0)
        def _():
            for pair in range(2):
                send_back[pair].wait_recv()
                two = slice(pair * 2, pair * 2 + 2)
                dk[two] += dkv_recv[pair, :, :, 0:128].astype(F32)
                dv[two] += dkv_recv[pair, :, :, 128:256].astype(F32)

        gain_early[:, 1152:1280] = lax.fori_loop(0, 4, key_back, zero)
        weight_grad(grads_kv)
        grad_kv.stage_one()
        grad_o.stage_two()
    with jax.named_scope("d_normed"):
        for batch in range(2):
            back_two[batch].release()
        back_one = Scatter(3, 1, 64)
        for place, d in enumerate(order):
            back_one.store(d, mm_last(dqkv[wrap(x + d)], w_a[...].reshape(1024, COLS_QKV)))
            if place:
                back_one.forward(order[place - 1])
        early = over_x(early_x, gain_early[...])
        grad_o.stage_three()
        grad_q.stage_two()
        back_one.relay()
        grad_kv.stage_two()
        grad_m2.stage_four()
        grad_q.stage_direct()
    with jax.named_scope("input_grad"):
        d_normed = back_one.total()
        inputs = tok[...].astype(F32)
        scaling = rms_scale(inputs)
        normed = inputs * scaling
        late = over_x(late_x, jnp.sum(d_normed * normed, 0, keepdims=True))
        d_normed = d_normed * ng_ref[...]
        ig_ref[...] = (
            scaling * (d_normed - normed * jnp.mean(d_normed * normed, -1, keepdims=True))
            + d_resid[...]
        )

    with jax.named_scope("tail"):
        grad_kv.stage_direct()
        grad_o.stage_four()
        early = over_yz(early_yz, total_of(early_x, early))
        grad_m1.stage_five()
        late = over_yz(late_yz, total_of(late_x, late))
        grad_m2.stage_five()
        grad_m1.stage_six()
        grad_q.stage_five()
        gain_early[...] = total_of(early_yz, early)
        grad_m2.stage_six()
        grad_kv.stage_five()
        grad_o.stage_five()
        gains_ref[0:1, :] = gain_early[:, 0:1024]
        gains_ref[2:3, 0:256] = gain_early[:, 1024:1280]
        gains_ref[1:2, :] = total_of(late_yz, late)
        grad_q.stage_six()
        grad_kv.stage_six()
        grad_o.stage_six()
    with jax.named_scope("drain"):
        drain()

        @pl.when(yhi == 1)
        def _():
            for copy in send_back:
                copy.wait_send()

        for copy in local[-5:]:
            copy.wait()


def rope_table(length):
    half = HEAD_DIM // 2
    freqs = np.power(np.float32(THETA), np.float32(-2.0) * np.arange(half, dtype=np.float32) / HEAD_DIM)
    angles = np.arange(length, dtype=np.float32)[:, None] * freqs.astype(np.float32)[None, :]
    table = np.concatenate([np.cos(angles), np.sin(angles)], 1).astype(np.float32)
    return table.reshape(length // 256, 256, HEAD_DIM)


def on_device(
    tokens, cotangent, w_query, w_key, w_value, w_output, w_gate, w_up, w_down,
    norm_gain, mlp_gain, query_gain, key_gain,
):
    vmem = pl.BlockSpec(memory_space=pltpu.VMEM)
    hbm = pl.BlockSpec(memory_space=pl.ANY)

    def v(shape, dtype=BF16):
        return pltpu.VMEM(shape, dtype)

    scratch = [v((128, 1024)), v((1, 1024), F32), v((1, 1024), F32), v((1, 128), F32), v((1, 128), F32)]
    scratch += [v((4, 256, 1024))]
    scratch += [v((2, 4, 128, 1024)) for _ in range(3)]
    scratch += [v((1024, 1024))]
    scratch += [v((8, 128, COLS_QKV)), v((8, 128, COLS_OUT)), v((8, 128, COLS_MLP))]
    scratch += [
        v((4, 256, 384), F32),
        v((4, 512, 128)),
        v((8, 256, 384)),
        v((4, 256, 128), F32),
        v((4, 512, 256), F32),
        v((2, 4, 128, 256)),
        v((4, 512, 128)),
        v((4, 512, 128), F32),
        v((8, 256, 128), F32),
        v((8, 256, 128), F32),
        v((4, 256, 512)),
        v((2, 4, 128, 384)),
        v((2, 4, 128, 768)),
        v((4, 8, 512), F32),
        v((4, 8, 512), F32),
        v((128, 1024), F32),
        v((128, 1024), F32),
        v((2, 4, 256, 1024)),
        v((4, 4, 128, 1024)),
        v((4, 3, 128, 1024)),
        v((2, 2, 256, 256)),
        v((2, 2, 256, 256)),
    ]
    scratch += [v((1, 1280), F32)]
    scratch += [v((8, 1, 1280), F32), v((16, 1, 1280), F32)]
    scratch += [v((8, 1, 1024), F32), v((16, 1, 1024), F32)]
    shapes = (
        lambda cols, first: (2, 4, 128, cols),
        lambda cols, first: (3, 2, 128, first),
        lambda cols, first: (3, 4, 64, cols - first),
        lambda cols, first: (2, 2, 64, first),
        lambda cols, first: (4, 64, cols - first),
        lambda cols, first: (3, 64, first),
        lambda cols, first: (3, 64, cols - first),
        lambda cols, first: (2, 4, 2, 64, cols),
    )
    scratch += [{name: v(shape(*cols)) for name, cols in GROUPS.items()} for shape in shapes]
    scratch += [
        pltpu.SemaphoreType.DMA((COPIES,)),
        pltpu.SemaphoreType.DMA((COPIES,)),
        pltpu.SemaphoreType.DMA((LOCAL_COPIES,)),
    ]
    mixed, input_grad, grads, gains = pl.pallas_call(
        kernel,
        name="layer",
        out_shape=(
            jax.ShapeDtypeStruct((128, 1024), BF16),
            jax.ShapeDtypeStruct((128, 1024), F32),
            {n: jax.ShapeDtypeStruct((2, 4, 2, 64, c[0]), BF16) for n, c in GROUPS.items()},
            jax.ShapeDtypeStruct((8, 1024), F32),
        ),
        in_specs=[hbm] * 14,
        out_specs=(vmem, vmem, {name: hbm for name in GROUPS}, vmem),
        scratch_shapes=scratch,
        compiler_params=pltpu.CompilerParams(
            collective_id=0, has_side_effects=True, vmem_limit_bytes=63 * 2**20
        ),
    )(
        tokens, cotangent, w_query, w_key, w_value, w_output, w_gate, w_up, w_down,
        norm_gain[None, :], mlp_gain[None, :], query_gain[None, :], key_gain[None, :],
        jnp.asarray(rope_table(2048)),
    )

    widths = (256, 128, 128, 256, 384, 384, 384)
    return pl.pallas_call(
        finish,
        name="finish",
        out_shape=(
            jax.ShapeDtypeStruct((128, 1024), BF16),
            jax.ShapeDtypeStruct((128, 1024), F32),
            *(jax.ShapeDtypeStruct((128, 8 * width), F32) for width in widths),
            jax.ShapeDtypeStruct((1024,), F32),
            jax.ShapeDtypeStruct((1024,), F32),
            jax.ShapeDtypeStruct((128,), F32),
            jax.ShapeDtypeStruct((128,), F32),
        ),
        in_specs=[vmem, vmem, {name: hbm for name in GROUPS}, vmem],
        out_specs=(vmem,) * 2 + (hbm,) * 7 + (vmem,) * 4,
        scratch_shapes=[
            {name: v((2, 8, 64, cols[0])) for name, cols in GROUPS.items()},
            tuple(v((128, 8 * width), F32) for width in widths),
            pltpu.SemaphoreType.DMA((12,)),
        ],
        compiler_params=pltpu.CompilerParams(vmem_limit_bytes=63 * 2**20),
    )(
        mixed, input_grad,
        {name: grads[name].reshape(2, 8, 64, cols[0]) for name, cols in GROUPS.items()}, gains,
    )


def finish(
    mixed, input_grad, grads, gains,
    out_mixed, out_input, out_q, out_k, out_v, out_o, out_g, out_u, out_d,
    out_norm, out_mlp, out_qg, out_kg, held, wide, sems,
):
    arrived = {}
    for index, name in enumerate(GROUPS):
        arrived[name] = pltpu.make_async_copy(grads[name], held[name], sems.at[index])
        arrived[name].start()
    sent = []
    wide_q, wide_k, wide_v, wide_o, wide_g, wide_u, wide_d = wide
    for index, (name, out, place, pieces) in enumerate((
        ("m1", out_g, wide_g, (("m1", 0, 384, 0),)),
        ("m2", out_u, wide_u, (("m1", 384, 256, 0), ("m2", 0, 128, 256))),
        ("m2", out_d, wide_d, (("m2", 128, 384, 0),)),
        ("o", out_o, wide_o, (("o", 0, 256, 0),)),
        ("q", out_q, wide_q, (("q", 0, 256, 0),)),
        ("kv", out_k, wide_k, (("kv", 0, 128, 0),)),
        ("kv", out_v, wide_v, (("kv", 128, 128, 0),)),
    )):
        if name in arrived:
            arrived.pop(name).wait()
        width = place.shape[1] // 8
        for group, start, size, at in pieces:
            for half in range(2):
                for j in range(8):
                    place[half * 64 : half * 64 + 64, j * width + at : j * width + at + size] = (
                        held[group][half, j, :, start : start + size].astype(F32)
                    )
        copy = pltpu.make_async_copy(place, out, sems.at[5 + index])
        copy.start()
        sent.append(copy)
    out_mixed[...] = mixed[...]
    out_input[...] = input_grad[...]
    out_norm[...] = gains[1, :]
    out_mlp[...] = gains[0, :]
    out_qg[...] = gains[2, 0:128]
    out_kg[...] = gains[2, 128:256]
    for copy in sent:
        copy.wait()


def solution(mesh):
    rows = P(("fsdp", "ctx"), None)
    weight = P("fsdp", None)
    return jax.shard_map(
        on_device,
        mesh=mesh,
        in_specs=(rows, rows) + (weight,) * 7 + (P(),) * 4,
        out_specs=(rows, rows) + (weight,) * 7 + (P(),) * 4,
        check_vma=False,
    )
```

```python
import math

import jax
import jax.numpy as jnp
import numpy as np
from jax import lax
from jax.experimental import pallas as pl
from jax.experimental.pallas import tpu as pltpu
from jax.sharding import PartitionSpec as P

MESH = pl.DeviceIdType.MESH
EPSILON = 1e-06
THETA = 1000000.0
HEAD_DIM = 128
SCALE = 1.0 / math.sqrt(HEAD_DIM)
SCALE_LOG2 = SCALE * math.log2(math.e)
F32 = jnp.float32
BF16 = jnp.bfloat16
DIST = (1, 3, 2)
SLOT = {1: 0, 3: 1, 2: 2}
COPIES = 194
LOCAL_COPIES = 20
COLS_MLP, COLS_OUT, COLS_QKV = 1152, 256, 512
GROUPS = {"m1": (640, 384), "m2": (512, 256), "o": (256, 128), "q": (256, 128), "kv": (256, 128)}


def mm(left, right):
    return jnp.dot(left, right, preferred_element_type=F32)


def mm_last(left, right):
    return lax.dot_general(left, right, (((1,), (1,)), ((), ())), preferred_element_type=F32)


def mm_first(left, right):
    return lax.dot_general(left, right, (((0,), (0,)), ((), ())), preferred_element_type=F32)


def rms_scale(rows):
    return lax.rsqrt(jnp.mean(rows * rows, -1, keepdims=True) + EPSILON)


def swap_halves(heads):
    return pltpu.roll(heads, HEAD_DIM // 2, 1)


def rope_split(table):
    lane = lax.broadcasted_iota(jnp.int32, table.shape, 1)
    other = swap_halves(table)
    cosine = jnp.where(lane < HEAD_DIM // 2, table, other)
    sine = jnp.where(lane < HEAD_DIM // 2, -other, table)
    return cosine, sine


class Remote:
    def __init__(self, sems, src, dst, device, landing):
        self.sems, self.device = sems, device
        self.src, self.dst, self.landing = src, dst, landing

    def describe(self, src, dst, device):
        send, recv, index = self.sems
        return pltpu.make_async_remote_copy(
            src_ref=src,
            dst_ref=dst,
            send_sem=send.at[index],
            recv_sem=recv.at[index],
            device_id=device,
            device_id_type=MESH,
        )

    def launch(self, src, dst, device):
        self.describe(src, dst, device).start()

    def start(self):
        self.launch(self.src, self.dst, self.device)

    def wait_send(self):
        self.describe(self.src, self.dst, self.device).wait_send()

    def wait_recv(self):
        self.describe(self.landing, self.landing, self.device).wait_recv()


def kernel(
    tok_hbm, cot_hbm, wq, wk, wv, wo, wg, wu, wd, ng_hbm, mg_hbm, qg_hbm, kg_hbm, rope_hbm,
    mixed_ref, ig_ref, out, gains_ref,
    tok, ng_ref, mg_ref, qg_ref, kg_ref,
    g1, g2, g3, g4, g1_turned, w_a, w_o, w_m, raw, qh, kv, rope, oa, att, do, dq, dk, dv, dqkv,
    hid, dgu, lse_row, delta_row, resid, d_resid,
    rs_send, rs_sib, rs_x, dkv_send, dkv_recv, gain_early, early_x, early_yz, late_x, late_yz,
    gw, z1, y1, z2s, y2s, y2, z2, full, send, recv, local_sem,
):
    f_index = lax.axis_index("fsdp")
    c_index = lax.axis_index("ctx")
    z = lax.rem(f_index, 4)
    ylo = lax.div(f_index, 4)
    core = lax.rem(c_index, 2)
    x = lax.rem(lax.div(c_index, 2), 4)
    yhi = lax.div(c_index, 8)
    y = yhi * 2 + ylo
    slice_index = x * 2 + core

    def wrap(value):
        return lax.rem(value + 8, 4)

    def device(dx=0, dy=0, dz=0, dcore=0):
        to_x, to_y, to_z = wrap(x + dx), wrap(y + dy), wrap(z + dz)
        to_core = lax.rem(core + dcore, 2)
        return {
            "fsdp": lax.rem(to_y, 2) * 4 + to_z,
            "ctx": lax.div(to_y, 2) * 8 + to_x * 2 + to_core,
        }

    counter = [0]

    def sems():
        index = counter[0]
        counter[0] += 1
        assert index < COPIES
        return (send, recv, index)

    pending = []

    def remote(src, dst, to, landing):
        copy = Remote(sems(), src, dst, to, landing)
        copy.start()
        pending.append(copy)
        return copy

    def several(copies, total):
        copy = Remote(sems(), total, total, sibling, total)
        for src, dst, to in copies:
            copy.launch(src, dst, to)
        pending.append(copy)
        return copy

    def drain():
        while pending:
            pending.pop().wait_send()

    def rows(start, size):
        return pl.ds(pl.multiple_of(start, size), size)

    sibling = device(dcore=1)
    partners = [sibling]
    partners += [device(dx=d) for d in DIST]
    partners += [device(dy=d) for d in DIST]
    partners += [device(dx=d, dcore=1) for d in DIST]
    partners += [device(dz=d) for d in DIST]
    partners += [device(dy=a, dz=b) for a in DIST for b in DIST]
    partners += [device(dx=d, dy=2) for d in DIST]

    def columns(ref, width):
        return ref.at[:, pl.ds(pl.multiple_of(slice_index * width, 128), width)]

    local = []

    def fetch(src, dst):
        assert len(local) < LOCAL_COPIES
        copy = pltpu.make_async_copy(src, dst, local_sem.at[len(local)])
        copy.start()
        local.append(copy)
        return copy

    fetch_tok = [fetch(tok_hbm, tok), fetch(ng_hbm, ng_ref)]
    fetch_a = [
        fetch(columns(wq, 256), w_a.at[f_index, :, 0:256]),
        fetch(columns(wk, 128), w_a.at[f_index, :, 256:384]),
        fetch(columns(wv, 128), w_a.at[f_index, :, 384:512]),
    ]
    fetch_o = [fetch(columns(wo, 256), w_o.at[f_index])]
    fetch_m = [
        fetch(columns(wg, 384), w_m.at[f_index, :, 0:384]),
        fetch(columns(wu, 384), w_m.at[f_index, :, 384:768]),
        fetch(columns(wd, 384), w_m.at[f_index, :, 768:1152]),
    ]
    fetch_rest = [
        fetch(rope_hbm, rope),
        fetch(cot_hbm.at[0:64], g3.at[0, x, rows(core * 64, 64)]),
        fetch(cot_hbm.at[64:128], g3.at[1, x, rows(core * 64, 64)]),
        fetch(mg_hbm, mg_ref),
        fetch(qg_hbm, qg_ref),
        fetch(kg_hbm, kg_ref),
    ]

    barrier = pltpu.get_barrier_semaphore()
    for partner in partners:
        pl.semaphore_signal(barrier, inc=1, device_id=partner, device_id_type=MESH)

    class Gather:
        def __init__(self, part, whole, held=pending):
            def to(dx, half, steps):
                block = part(wrap(x - (steps - 1) * dx), core, half)
                landing = part(wrap(x - steps * dx), core, half)
                return Remote(sems(), block, block, device(dx=dx), landing)

            def to_pair(d):
                block = whole(wrap(x - d), core)
                return Remote(sems(), block, block, sibling, whole(wrap(x - d), 1 - core))

            self.held = held
            self.plus = {half: to(1, half, 1) for half in (0, 1)}
            self.minus = {half: to(3, half, 1) for half in (0, 1)}
            self.far_plus, self.far_minus = to(1, 0, 2), to(3, 1, 2)
            self.pair = {d: to_pair(d) for d in (0,) + DIST}

        def start(self, *copies):
            for copy in copies:
                copy.start()
                self.held.append(copy)

        def begin(self):
            self.start(self.plus[0], self.minus[1], self.plus[1], self.minus[0], self.pair[0])
            return self

        def relay(self):
            self.plus[0].wait_recv()
            self.start(self.far_plus)
            self.minus[1].wait_recv()
            self.start(self.far_minus)

        def forward(self, d):
            if d == 1:
                self.plus[1].wait_recv()
            elif d == 3:
                self.minus[0].wait_recv()
            else:
                self.far_plus.wait_recv()
                self.far_minus.wait_recv()
            self.start(self.pair[d])

        def ready(self, d):
            self.pair[d].wait_recv()

    def gather_plain(ref):
        return Gather(
            lambda t, c, half: ref.at[t, rows(c * 128 + half * 64, 64)],
            lambda t, c: ref.at[t, rows(c * 128, 128)],
        ).begin()

    def gather_batch(ref, batch):
        return Gather(
            lambda t, c, half: ref.at[batch, t, rows(c * 64 + half * 32, 32)],
            lambda t, c: ref.at[batch, t, rows(c * 64, 64)],
        ).begin()

    def gather_batches(ref):
        return Gather(
            lambda t, c, half: ref.at[half, t, rows(c * 64, 64)],
            lambda t, c: ref.at[:, t, rows(c * 64, 64)],
        ).begin()

    class Scatter:
        def __init__(self, index, buffer, half, batch=0):
            self.half, self.batch = half, batch
            self.part, self.pair, self.ring = rs_send.at[buffer], rs_sib.at[index], rs_x.at[index]
            self.pair_copy, self.near, self.far = {}, {}, {}

        def part_rows(self, which, half=None):
            start = self.batch * 4 * self.half + which * 2 * self.half
            if half is None:
                return rows(start, 2 * self.half)
            return rows(start + half * self.half, self.half)

        def pair_rows(self, half=None):
            start = self.batch * 2 * self.half
            if half is None:
                return pl.ds(start, 2 * self.half)
            return pl.ds(start + half * self.half, self.half)

        def emit(self, d):
            slot = self.pair.at[d, self.pair_rows()]
            self.pair_copy[d] = remote(self.part.at[d, self.part_rows(1 - core)], slot, sibling, slot)

        def store(self, d, value):
            self.part[d, pl.ds(self.batch * 4 * self.half, 4 * self.half), :] = value.astype(BF16)
            self.emit(d)

        def summed(self, d, half=None):
            return self.part[d, self.part_rows(core, half), :].astype(F32) + self.pair[
                d, self.pair_rows(half), :
            ].astype(F32)

        def to(self, d, place, half, dx):
            slot = self.ring.at[place, self.pair_rows(half)]
            return remote(self.pair.at[d, self.pair_rows(half)], slot, device(dx=dx), slot)

        def forward(self, d):
            self.pair_copy[d].wait_recv()
            if d == 2:
                self.pair[d, self.pair_rows(), :] = self.summed(d).astype(BF16)
                self.far = {0: self.to(2, 2, 0, 1), 1: self.to(2, 2, 1, 3)}
            else:
                half, place = (1, 0) if d == 1 else (0, 1)
                self.pair[d, self.pair_rows(half), :] = self.summed(d, half).astype(BF16)
                self.near[d] = self.to(d, place, half, d)

        def relay(self):
            for d, half, place in ((1, 0, 0), (3, 1, 1)):
                self.far[half].wait_recv()
                value = self.summed(d, half) + self.ring[2, self.pair_rows(half), :].astype(F32)
                self.pair[d, self.pair_rows(half), :] = value.astype(BF16)
                self.near[d, half] = self.to(d, place, half, d)

        def total(self):
            self.pair_copy[0].wait_recv()
            value = self.summed(0)
            for d, half, place in ((1, 0, 0), (3, 1, 1)):
                self.near[d].wait_recv()
                self.near[d, half].wait_recv()
                value = value + self.ring[place, self.pair_rows(), :].astype(F32)
            return value

        def release(self):
            for copy in self.pair_copy.values():
                copy.wait_send()
                pending.remove(copy)

    class WeightGather:
        def __init__(self, ref, fetched):
            self.ref = ref
            for copy in fetched:
                copy.wait()
            own = ref.at[f_index]
            self.along_z = {
                d: remote(own, own, device(dz=d), ref.at[ylo * 4 + wrap(z - d)]) for d in DIST
            }
            held, coming = ref.at[pl.ds(ylo * 4, 4)], ref.at[pl.ds((1 - ylo) * 4, 4)]
            self.along_y = Remote(sems(), held, held, sibling, coming)

        def spread(self, d):
            if d:
                self.along_z[d].wait_recv()
            held = ylo * 4 + wrap(z - d)
            for dy, part in ((1, pl.ds(0, 64)), (3, pl.ds(64, 64))):
                block = self.ref.at[held, part]
                self.along_y.launch(block, block, device(dy=dy))

        def finish(self):
            self.along_y.wait_recv()
            pending.append(self.along_y)

    class WeightGrad:
        def __init__(self, name, ring_first=False):
            cols, first = GROUPS[name]
            self.ring_first = ring_first
            self.gw, self.z1, self.y1, self.z2s = gw[name], z1[name], y1[name], z2s[name]
            self.y2s, self.y2, self.z2 = y2s[name], y2[name], z2[name]
            self.full, self.out = full[name], out[name]
            self.left, self.right = slice(0, first), slice(first, cols)

        def stage_one(self):
            copies = []
            for d in DIST:
                src = self.gw.at[:, wrap(z + d), :, self.left]
                copies.append((src, self.z1.at[SLOT[d]], device(dz=d)))
            self.one_z = several(copies, self.z1)
            copies = []
            for d in DIST:
                to_y = wrap(y + d)
                half = rows(lax.div(to_y, 2) * 64, 64)
                src = self.gw.at[lax.rem(to_y, 2), :, half, self.right]
                copies.append((src, self.y1.at[SLOT[d]], device(dy=d)))
            self.one_y = several(copies, self.y1)

        def stage_two(self):
            self.one_z.wait_recv()
            total = self.gw[:, z, :, self.left].astype(F32)
            for d in DIST:
                total = total + self.z1[SLOT[d]].astype(F32)
            self.z2s[...] = total.astype(BF16).reshape(self.z2s.shape)
            copies = []
            for d in DIST:
                to_y = wrap(y + d)
                src = self.z2s.at[lax.rem(to_y, 2), lax.div(to_y, 2)]
                copies.append((src, self.y2.at[SLOT[d]], device(dy=d)))
            self.two_y = several(copies, self.y2)
            self.one_y.wait_recv()
            total = self.gw[ylo, :, rows(yhi * 64, 64), self.right].astype(F32)
            for d in DIST:
                total = total + self.y1[SLOT[d]].astype(F32)
            self.y2s[...] = total.astype(BF16)
            copies = []
            for d in DIST:
                copies.append((self.y2s.at[wrap(z + d)], self.z2.at[SLOT[d]], device(dz=d)))
            self.two_z = several(copies, self.z2)

        def sums(self):
            self.two_y.wait_recv()
            total = self.z2s[ylo, yhi].astype(F32)
            for d in DIST:
                total = total + self.y2[SLOT[d]].astype(F32)
            self.full[yhi, x, core, :, self.left] = total.astype(BF16)
            self.two_z.wait_recv()
            total = self.y2s[z].astype(F32)
            for d in DIST:
                total = total + self.z2[SLOT[d]].astype(F32)
            self.full[yhi, x, core, :, self.right] = total.astype(BF16)

        def stage_three(self):
            self.sums()
            own = self.full.at[yhi, x, core]
            if self.ring_first:
                self.ring = [
                    remote(own, own, device(dx=d), self.full.at[yhi, wrap(x - d), core])
                    for d in DIST
                ]
            else:
                self.flip = remote(own, own, device(dy=2), self.full.at[1 - yhi, x, core])

        def stage_four(self):
            if self.ring_first:
                for copy in self.ring:
                    copy.wait_recv()
                held = self.full.at[yhi, :, core]
                self.ring = [remote(held, held, device(dy=2), self.full.at[1 - yhi, :, core])]
            else:
                self.flip.wait_recv()
                held = self.full.at[:, x, core]
                self.ring = [
                    remote(held, held, device(dx=d), self.full.at[:, wrap(x - d), core])
                    for d in DIST
                ]

        def stage_direct(self):
            self.sums()
            own = self.full.at[yhi, x, core]
            self.ring = [
                remote(own, own, device(dx=d), self.full.at[yhi, wrap(x - d), core]) for d in DIST
            ]
            copies = [(own, own, device(dx=d, dy=2)) for d in (0,) + DIST]
            self.ring.append(several(copies, self.full.at[1 - yhi, :, core]))

        def stage_five(self):
            for copy in self.ring:
                copy.wait_recv()
            held = self.full.at[:, :, core]
            self.pair = remote(held, held, sibling, self.full.at[:, :, 1 - core])

        def stage_six(self):
            self.pair.wait_recv()
            fetch(self.full, self.out)

    grad_m1, grad_m2, grad_o = WeightGrad("m1"), WeightGrad("m2", True), WeightGrad("o")
    grad_q, grad_kv = WeightGrad("q"), WeightGrad("kv")

    def weight_grad(parts):
        def chunk(index, carry):
            lanes = pl.ds(pl.multiple_of(index * 256, 256), 256)
            block = pl.ds(lax.rem(index, 2) * 2, 2)
            for left, right, source, target, cols, turned in parts:
                width = cols.stop - cols.start
                operand = right[..., source].reshape(1024, width)
                if turned:
                    value = mm(left[lanes, :], operand)
                else:
                    value = mm_first(left[..., lanes].reshape(1024, 256), operand)
                target[lax.div(index, 2), block, :, cols] = value.astype(BF16).reshape(
                    2, 128, width
                )
            return carry

        lax.fori_loop(0, 4, chunk, 0)

    with jax.named_scope("first_norm"):
        kv[:, :, 256:384] = jnp.ones((8, 256, 128), BF16)
        gain_early[...] = jnp.zeros_like(gain_early)
        for copy in fetch_tok:
            copy.wait()
        inputs = tok[...].astype(F32)
        g1[x, rows(core * 128, 128), :] = (inputs * rms_scale(inputs) * ng_ref[...]).astype(BF16)
    with jax.named_scope("entry_barrier"):
        pl.semaphore_wait(barrier, len(partners))
    across = device(dy=2)
    far_held = []
    far = Gather(
        lambda t, c, half: g1_turned.at[rows(t * 256 + c * 128 + half * 64, 64)],
        lambda t, c: g1_turned.at[rows(t * 256 + c * 128, 128)],
        far_held,
    )
    with jax.named_scope("gather_start"):
        rows_one = gather_plain(g1)
        gather_a = WeightGather(w_a, fetch_a)
        gather_a.spread(0)
        place = rows(x * 256 + core * 128, 128)
        send_rows = Remote(
            sems(), g1.at[x, rows(core * 128, 128)], g1_turned.at[place], across, g1_turned.at[place]
        )

        @pl.when(yhi == 0)
        def _():
            send_rows.start()

        rows_one.relay()
        gather_a.spread(1)
        rows_one.forward(1)
        gather_a.spread(3)
        rows_one.forward(3)
        gather_o = WeightGather(w_o, fetch_o)

        @pl.when(yhi == 1)
        def _():
            send_rows.wait_recv()
            far.begin()

        gather_a.spread(2)
        gather_m = WeightGather(w_m, fetch_m)
        rows_one.forward(2)
        for copy in fetch_rest:
            copy.wait()

        @pl.when(yhi == 1)
        def _():
            far.relay()

        gather_a.finish()
        for d in (0,) + DIST:
            gather_o.spread(d)
        gather_m.spread(0)

    def project(t):
        value = mm(g1[t], w_a[...].reshape(1024, COLS_QKV))
        cosine, sine = rope_split(rope[yhi * 4 + t])
        raw[t] = value[:, 0:384]
        for head in range(3):
            one = value[:, head * 128 : head * 128 + 128]
            gain = qg_ref[...] if head < 2 else kg_ref[...]
            scaled = one * rms_scale(one) * gain
            turned = (scaled * cosine + swap_halves(scaled) * sine).astype(BF16)
            if head < 2:
                qh[t, head * 256 : head * 256 + 256, :] = turned
            else:
                kv[yhi * 4 + t, :, 0:128] = turned
        kv[yhi * 4 + t, :, 128:256] = value[:, 384:512].astype(BF16)

    def project_far(t):
        value = mm(
            g1_turned[rows(t * 256, 256), :], w_a[:, :, 256:512].reshape(1024, 256)
        )
        cosine, sine = rope_split(rope[t])
        scaled = value[:, 0:128] * rms_scale(value[:, 0:128]) * kg_ref[...]
        kv[t, :, 0:128] = (scaled * cosine + swap_halves(scaled) * sine).astype(BF16)
        kv[t, :, 128:256] = value[:, 128:256].astype(BF16)

    with jax.named_scope("qkv"):
        for place, d in enumerate((0,) + DIST):
            rows_one.ready(d)
            project(wrap(x - d))
            if place == 2:

                @pl.when(yhi == 1)
                def _():
                    far.forward(1)
                    far.forward(3)

        rows_cot = gather_batches(g3)

    def attend_own(i):
        size = 256 * (i + 1)
        block = pl.ds(yhi * 4, i + 1)
        soft = jnp.exp2(mm_last(qh[i], kv[block, :, 0:128].reshape(size, 128)) * SCALE_LOG2)
        row = lax.broadcasted_iota(jnp.int32, (512, size), 0)
        col = lax.broadcasted_iota(jnp.int32, (512, size), 1)
        soft = jnp.where(col <= lax.rem(row, 256) + 256 * i, soft, 0.0).astype(BF16)
        oa[i] = mm(soft, kv[block, :, 128:384].reshape(size, 256))

    with jax.named_scope("attend_own"):
        for i in range(3):
            attend_own(i)
        rows_cot.relay()
        gather_m.spread(1)
        gather_m.spread(3)
        attend_own(3)

        @pl.when(yhi == 1)
        def _():
            far.forward(2)
            for d in (0,) + DIST:
                far.ready(d)
                project_far(wrap(x - d))
            for copy in far_held:
                copy.wait_send()

    def attend_across(i):
        @pl.when(yhi == 1)
        def _():
            def step(j, carry):
                two = pl.ds(j * 2, 2)
                soft = jnp.exp2(mm_last(qh[i], kv[two, :, 0:128].reshape(512, 128)) * SCALE_LOG2)
                oa[i] += mm(soft.astype(BF16), kv[two, :, 128:384].reshape(512, 256))
                return carry

            lax.fori_loop(0, 2, step, 0)

    def attend_end(i):
        both = oa[i]
        total = both[:, 128:256]
        exact = both[:, 0:128] / total
        oa[i, :, 0:128] = exact
        lse_row[i] = jnp.transpose(jnp.log(total) * math.log2(math.e))[0:8, :]
        exact = exact.astype(BF16)
        for head in range(2):
            for which in range(2):
                for batch in range(2):
                    start = head * 256 + which * 128 + batch * 64
                    att[batch, i, which * 64 : which * 64 + 64, head * 128 : head * 128 + 128] = (
                        exact[start : start + 64]
                    )

    branch = [Scatter(0, 0, 32, batch) for batch in range(2)]
    order = (2, 1, 3, 0)
    with jax.named_scope("branch"):
        for place, d in enumerate(order):
            t = wrap(x + d)
            attend_across(t)
            attend_end(t)
            if place == 0:
                gather_o.finish()
            for batch in range(2):
                branch[batch].store(d, mm_last(att[batch, t], w_o[...].reshape(1024, COLS_OUT)))
            if place:
                for batch in range(2):
                    branch[batch].forward(order[place - 1])
                rows_cot.forward(DIST[place - 1])
            if place == 0:
                gather_m.spread(2)

    def batch_rows(batch):
        return slice(batch * 64, batch * 64 + 64)

    rows_two = []
    with jax.named_scope("resid"):
        for batch in range(2):
            branch[batch].relay()
        for batch in range(2):
            value = branch[batch].total() + tok[batch_rows(batch), :].astype(F32)
            resid[batch_rows(batch), :] = value
            g2[batch, x, rows(core * 64, 64), :] = (
                value * rms_scale(value) * mg_ref[...]
            ).astype(BF16)
            rows_two.append(gather_batch(g2, batch))
        g1_turned[...] = jnp.transpose(g1[...].reshape(1024, 1024))
        for batch in range(2):
            rows_two[batch].relay()
            branch[batch].release()
        gather_m.finish()

    back_two = [Scatter(1, 1, 32, batch) for batch in range(2)]

    def feed_forward(batch, d):
        t = wrap(x - d)
        rows_two[batch].ready(d)
        w_gate_up = w_m[:, :, 0:768].reshape(1024, 768)
        w_d = w_m[:, :, 768:1152].reshape(1024, 384)
        both = mm(g2[batch, t], w_gate_up)
        d_hidden = mm(g3[batch, t], w_d)
        gate, up = both[:, 0:384], both[:, 384:768]
        sig = jax.nn.sigmoid(gate)
        active = gate * sig
        hid[batch, t] = (active * up).astype(BF16)
        dgu[batch, t, :, 0:384] = (d_hidden * up * sig * (1.0 + gate * (1.0 - sig))).astype(BF16)
        dgu[batch, t, :, 384:768] = (d_hidden * active).astype(BF16)
        back_two[batch].store((4 - d) % 4, mm_last(dgu[batch, t], w_gate_up))

    with jax.named_scope("mlp"):
        for d in (0,) + DIST:
            rows_cot.ready(d)
        feed_forward(0, 0)
        rows_two[0].forward(1)
        rows_two[0].forward(3)
        feed_forward(1, 0)
        feed_forward(0, 1)
        rows_two[0].forward(2)
        feed_forward(0, 3)
        rows_two[1].forward(1)
        rows_two[1].forward(3)
        back_two[0].forward(3)
        feed_forward(0, 2)
        back_two[0].forward(1)
        feed_forward(1, 1)
        back_two[0].forward(2)
        rows_two[1].forward(2)
        feed_forward(1, 3)
        back_two[1].forward(3)
        back_two[1].forward(1)
        feed_forward(1, 2)
        back_two[0].relay()
        back_two[1].forward(2)

    grads_m1 = ((g2, dgu, slice(0, 640), grad_m1.gw, slice(0, 640), False),)
    grads_m2 = (
        (g2, dgu, slice(640, 768), grad_m2.gw, slice(0, 128), False),
        (g3, hid, slice(0, 384), grad_m2.gw, slice(128, 512), False),
    )
    grads_o = ((g4, att, slice(0, 256), grad_o.gw, slice(0, 256), False),)
    grads_q = ((g1_turned, dqkv, slice(0, 256), grad_q.gw, slice(0, 256), True),)
    grads_kv = ((g1_turned, dqkv, slice(256, 512), grad_kv.gw, slice(0, 256), True),)
    rows_back = []

    def back_resid(batch):
        part = batch_rows(batch)
        d_normed = back_two[batch].total()
        value = resid[part, :]
        scaling = rms_scale(value)
        normed = value * scaling
        gain_early[:, 0:1024] += jnp.sum(d_normed * normed, 0, keepdims=True)
        d_normed = d_normed * mg_ref[...]
        value = scaling * (
            d_normed - normed * jnp.mean(d_normed * normed, -1, keepdims=True)
        ) + g3[batch, x, rows(core * 64, 64), :].astype(F32)
        d_resid[part, :] = value
        g4[batch, x, rows(core * 64, 64), :] = value.astype(BF16)
        rows_back.append(gather_batch(g4, batch))

    mlp_out = Scatter(2, 0, 64)

    def mlp_block(d):
        w_d = w_m[:, :, 768:1152].reshape(1024, 384)
        t = wrap(x + d)
        for batch in range(2):
            value = mm_last(hid[batch, t], w_d).astype(BF16)
            for which in range(2):
                start = which * 128 + batch * 64
                mlp_out.part[d, start : start + 64, :] = value[which * 64 : which * 64 + 64]
        mlp_out.emit(d)

    with jax.named_scope("d_resid"):
        weight_grad(grads_m1)
        grad_m1.stage_one()
        back_resid(0)
        back_two[1].relay()
        back_resid(1)
        rows_back[0].relay()
        weight_grad(grads_m2)
        grad_m2.stage_one()
        rows_back[1].relay()
        for to in order:
            mlp_block(to)

    def back_out(t):
        for batch in range(2):
            value = mm(g4[batch, t], w_o[...].reshape(1024, COLS_OUT)).astype(BF16)
            for head in range(2):
                for which in range(2):
                    start = head * 256 + which * 128 + batch * 64
                    do[t, start : start + 64, :] = value[
                        which * 64 : which * 64 + 64, head * 128 : head * 128 + 128
                    ]
        product = do[t].astype(F32) * oa[t, :, 0:128]
        delta_row[t] = jnp.broadcast_to(
            jnp.sum(jnp.transpose(product), 0, keepdims=True), (8, 512)
        )

    def tile(i, start, size, masked):
        keys = pl.ds(start, size)
        width = 256 * size
        key_rows, queries, grads = kv[keys, :, 0:128].reshape(width, 128), qh[i], do[i]
        soft = jnp.exp2(mm_last(key_rows, queries) * SCALE_LOG2 - lse_row[i, 0:1, :])
        if masked:
            row = lax.broadcasted_iota(jnp.int32, (width, 512), 0)
            col = lax.broadcasted_iota(jnp.int32, (width, 512), 1)
            soft = jnp.where(row <= lax.rem(col, 256) + (width - 256), soft, 0.0)
        d_soft = mm_last(kv[keys, :, 128:256].reshape(width, 128), grads)
        d_scores = (soft * (d_soft - delta_row[i, 0:1, :])).astype(BF16)
        dv[keys] += mm(soft.astype(BF16), grads).reshape(size, 256, 128)
        dk[keys] += mm(d_scores, queries).reshape(size, 256, 128)
        dq[i] += mm_first(d_scores, key_rows)

    def back_across(t):
        @pl.when(yhi == 1)
        def _():
            tile(t, 0, 4, False)

    send_back = [
        Remote(sems(), dkv_send.at[pair], dkv_recv.at[pair], across, dkv_recv.at[pair])
        for pair in range(2)
    ]

    def back_across_end(pair):
        @pl.when(yhi == 1)
        def _():
            for d in (3, 2):
                tile(wrap(x - d), pair * 2, 2, False)
            two = slice(pair * 2, pair * 2 + 2)
            dkv_send[pair, :, :, 0:128] = dk[two].astype(BF16)
            dkv_send[pair, :, :, 128:256] = dv[two].astype(BF16)
            send_back[pair].start()

    def back_ready(d):
        for batch in range(2):
            rows_back[batch].ready(d)
        back_out(wrap(x - d))

    def back_forward(d):
        for batch in range(2):
            rows_back[batch].forward(d)

    with jax.named_scope("attend_back_across"):
        dq[...] = jnp.zeros_like(dq)
        dk[...] = jnp.zeros_like(dk)
        dv[...] = jnp.zeros_like(dv)
        back_ready(0)
        back_forward(1)
        back_forward(3)
        back_across(x)
        back_ready(1)
        back_forward(2)
        grad_m1.stage_two()
        back_across(wrap(x - 1))
        back_ready(3)
        back_ready(2)
        for to in order[:3]:
            mlp_out.forward(to)
        back_across_end(0)
        grad_m2.stage_two()
        grad_m1.stage_three()
        back_across_end(1)
    with jax.named_scope("out_weight_grads"):
        mlp_out.relay()
        weight_grad(grads_o)
        grad_o.stage_one()
        grad_m2.stage_three()

    with jax.named_scope("attend_back_own"):

        for i in range(3):
            tile(i, yhi * 4, i + 1, True)
        grad_m1.stage_four()
        tile(3, yhi * 4, 4, True)
        grad_m2.stage_four()

    with jax.named_scope("mixed"):
        mixed_ref[...] = (resid[...] + mlp_out.total()).astype(BF16)

    def head_back(t, head):
        cosine, sine = rope_split(rope[yhi * 4 + t])
        one = raw[t, :, head * 128 : head * 128 + 128]
        if head < 2:
            grads, gain = dq[t, head * 256 : head * 256 + 256, :], qg_ref[...]
        else:
            grads, gain = dk[yhi * 4 + t], kg_ref[...]
        grads = grads * SCALE
        grads = grads * cosine - swap_halves(grads) * sine
        scaling = rms_scale(one)
        normed = one * scaling
        part = jnp.sum(grads * normed, 0, keepdims=True)
        grads = grads * gain
        value = scaling * (grads - normed * jnp.mean(grads * normed, -1, keepdims=True))
        dqkv[t, :, head * 128 : head * 128 + 128] = value.astype(BF16)
        return part

    def query_back(t, carry):
        return carry + head_back(t, 0) + head_back(t, 1)

    def key_back(t, carry):
        dqkv[t, :, 384:512] = dv[yhi * 4 + t].astype(BF16)
        return carry + head_back(t, 2)

    def over_x(slots, value):
        slots[slice_index] = value
        own = slots.at[slice_index]
        copies = [(own, own, sibling)]
        copies += [(own, own, device(dx=d, dcore=flip)) for d in DIST for flip in (0, 1)]
        return several(copies, slots.at[0:7])

    def over_yz(slots, value):
        place = y * 4 + z
        slots[place] = value
        own = slots.at[place]
        steps = (0,) + DIST
        copies = [(own, own, device(dy=a, dz=b)) for a in steps for b in steps if a or b]
        return several(copies, slots.at[0:15])

    def total_of(slots, copies):
        copies.wait_recv()
        value = slots[0]
        for place in range(1, slots.shape[0]):
            value = value + slots[place]
        return value

    with jax.named_scope("head_norm_back"):
        zero = jnp.zeros((1, 128), F32)
        gain_early[:, 1024:1152] = lax.fori_loop(0, 4, query_back, zero)

    with jax.named_scope("qkv_weight_grads"):
        weight_grad(grads_q)
        grad_q.stage_one()

        @pl.when(yhi == 0)
        def _():
            for pair in range(2):
                send_back[pair].wait_recv()
                two = slice(pair * 2, pair * 2 + 2)
                dk[two] += dkv_recv[pair, :, :, 0:128].astype(F32)
                dv[two] += dkv_recv[pair, :, :, 128:256].astype(F32)

        gain_early[:, 1152:1280] = lax.fori_loop(0, 4, key_back, zero)
        weight_grad(grads_kv)
        grad_kv.stage_one()
        grad_o.stage_two()
    with jax.named_scope("d_normed"):
        for batch in range(2):
            back_two[batch].release()
        back_one = Scatter(3, 1, 64)
        for place, d in enumerate(order):
            back_one.store(d, mm_last(dqkv[wrap(x + d)], w_a[...].reshape(1024, COLS_QKV)))
            if place:
                back_one.forward(order[place - 1])
        early = over_x(early_x, gain_early[...])
        grad_m1.stage_five()
        grad_q.stage_two()
        back_one.relay()
        grad_o.stage_three()
        grad_kv.stage_two()
        grad_q.stage_direct()
    with jax.named_scope("input_grad"):
        d_normed = back_one.total()
        inputs = tok[...].astype(F32)
        scaling = rms_scale(inputs)
        normed = inputs * scaling
        late = over_x(late_x, jnp.sum(d_normed * normed, 0, keepdims=True))
        d_normed = d_normed * ng_ref[...]
        ig_ref[...] = (
            scaling * (d_normed - normed * jnp.mean(d_normed * normed, -1, keepdims=True))
            + d_resid[...]
        )

    with jax.named_scope("tail"):
        grad_kv.stage_direct()
        early = over_yz(early_yz, total_of(early_x, early))
        grad_o.stage_four()
        grad_m2.stage_five()
        late = over_yz(late_yz, total_of(late_x, late))
        grad_m1.stage_six()
        grad_q.stage_five()
        gain_early[...] = total_of(early_yz, early)
        grad_m2.stage_six()
        grad_kv.stage_five()
        grad_o.stage_five()
        gains_ref[0:1, :] = gain_early[:, 0:1024]
        gains_ref[2:3, 0:256] = gain_early[:, 1024:1280]
        gains_ref[1:2, :] = total_of(late_yz, late)
        grad_q.stage_six()
        grad_kv.stage_six()
        grad_o.stage_six()
    with jax.named_scope("drain"):
        drain()

        @pl.when(yhi == 0)
        def _():
            send_rows.wait_send()

        @pl.when(yhi == 1)
        def _():
            for copy in send_back:
                copy.wait_send()

        for copy in local[-5:]:
            copy.wait()


def rope_table(length):
    half = HEAD_DIM // 2
    freqs = np.power(np.float32(THETA), np.float32(-2.0) * np.arange(half, dtype=np.float32) / HEAD_DIM)
    angles = np.arange(length, dtype=np.float32)[:, None] * freqs.astype(np.float32)[None, :]
    table = np.concatenate([np.cos(angles), np.sin(angles)], 1).astype(np.float32)
    return table.reshape(length // 256, 256, HEAD_DIM)


def on_device(
    tokens, cotangent, w_query, w_key, w_value, w_output, w_gate, w_up, w_down,
    norm_gain, mlp_gain, query_gain, key_gain,
):
    vmem = pl.BlockSpec(memory_space=pltpu.VMEM)
    hbm = pl.BlockSpec(memory_space=pl.ANY)

    def v(shape, dtype=BF16):
        return pltpu.VMEM(shape, dtype)

    scratch = [v((128, 1024)), v((1, 1024), F32), v((1, 1024), F32), v((1, 128), F32), v((1, 128), F32)]
    scratch += [v((4, 256, 1024))]
    scratch += [v((2, 4, 128, 1024)) for _ in range(3)]
    scratch += [v((1024, 1024))]
    scratch += [v((8, 128, COLS_QKV)), v((8, 128, COLS_OUT)), v((8, 128, COLS_MLP))]
    scratch += [
        v((4, 256, 384), F32),
        v((4, 512, 128)),
        v((8, 256, 384)),
        v((8, 256, 128), F32),
        v((4, 512, 256), F32),
        v((2, 4, 128, 256)),
        v((4, 512, 128)),
        v((4, 512, 128), F32),
        v((8, 256, 128), F32),
        v((8, 256, 128), F32),
        v((4, 256, 512)),
        v((2, 4, 128, 384)),
        v((2, 4, 128, 768)),
        v((4, 8, 512), F32),
        v((4, 8, 512), F32),
        v((128, 1024), F32),
        v((128, 1024), F32),
        v((2, 4, 256, 1024)),
        v((4, 4, 128, 1024)),
        v((4, 3, 128, 1024)),
        v((2, 2, 256, 256)),
        v((2, 2, 256, 256)),
    ]
    scratch += [v((1, 1280), F32)]
    scratch += [v((8, 1, 1280), F32), v((16, 1, 1280), F32)]
    scratch += [v((8, 1, 1024), F32), v((16, 1, 1024), F32)]
    shapes = (
        lambda cols, first: (2, 4, 128, cols),
        lambda cols, first: (3, 2, 128, first),
        lambda cols, first: (3, 4, 64, cols - first),
        lambda cols, first: (2, 2, 64, first),
        lambda cols, first: (4, 64, cols - first),
        lambda cols, first: (3, 64, first),
        lambda cols, first: (3, 64, cols - first),
        lambda cols, first: (2, 4, 2, 64, cols),
    )
    scratch += [{name: v(shape(*cols)) for name, cols in GROUPS.items()} for shape in shapes]
    scratch += [
        pltpu.SemaphoreType.DMA((COPIES,)),
        pltpu.SemaphoreType.DMA((COPIES,)),
        pltpu.SemaphoreType.DMA((LOCAL_COPIES,)),
    ]
    mixed, input_grad, grads, gains = pl.pallas_call(
        kernel,
        name="layer",
        out_shape=(
            jax.ShapeDtypeStruct((128, 1024), BF16),
            jax.ShapeDtypeStruct((128, 1024), F32),
            {n: jax.ShapeDtypeStruct((2, 4, 2, 64, c[0]), BF16) for n, c in GROUPS.items()},
            jax.ShapeDtypeStruct((8, 1024), F32),
        ),
        in_specs=[hbm] * 14,
        out_specs=(vmem, vmem, {name: hbm for name in GROUPS}, vmem),
        scratch_shapes=scratch,
        compiler_params=pltpu.CompilerParams(
            collective_id=0, has_side_effects=True, vmem_limit_bytes=63 * 2**20
        ),
    )(
        tokens, cotangent, w_query, w_key, w_value, w_output, w_gate, w_up, w_down,
        norm_gain[None, :], mlp_gain[None, :], query_gain[None, :], key_gain[None, :],
        jnp.asarray(rope_table(2048)),
    )

    widths = (256, 128, 128, 256, 384, 384, 384)
    return pl.pallas_call(
        finish,
        name="finish",
        out_shape=(
            jax.ShapeDtypeStruct((128, 1024), BF16),
            jax.ShapeDtypeStruct((128, 1024), F32),
            *(jax.ShapeDtypeStruct((128, 8 * width), F32) for width in widths),
            jax.ShapeDtypeStruct((1024,), F32),
            jax.ShapeDtypeStruct((1024,), F32),
            jax.ShapeDtypeStruct((128,), F32),
            jax.ShapeDtypeStruct((128,), F32),
        ),
        in_specs=[hbm, hbm, {name: hbm for name in GROUPS}, vmem],
        out_specs=(hbm,) * 9 + (vmem,) * 4,
        scratch_shapes=[
            {name: v((2, 8, 64, cols[0])) for name, cols in GROUPS.items()},
            tuple(v((128, 8 * width), F32) for width in widths),
            v((128, 1024)),
            v((128, 1024), F32),
            pltpu.SemaphoreType.DMA((23,)),
        ],
        compiler_params=pltpu.CompilerParams(vmem_limit_bytes=63 * 2**20),
    )(
        mixed, input_grad,
        {name: grads[name].reshape(2, 8, 64, cols[0]) for name, cols in GROUPS.items()}, gains,
    )


def finish(
    mixed, input_grad, grads, gains,
    out_mixed, out_input, out_q, out_k, out_v, out_o, out_g, out_u, out_d,
    out_norm, out_mlp, out_qg, out_kg, held, wide, held_mixed, held_input, sems,
):
    arrived = {}
    for index, name in enumerate(GROUPS):
        arrived[name] = pltpu.make_async_copy(grads[name], held[name], sems.at[index])
        arrived[name].start()
    through = [
        pltpu.make_async_copy(mixed, held_mixed, sems.at[19]),
        pltpu.make_async_copy(input_grad, held_input, sems.at[20]),
    ]
    for copy in through:
        copy.start()
    sent = []
    wide_q, wide_k, wide_v, wide_o, wide_g, wide_u, wide_d = wide
    for index, (name, out, place, pieces) in enumerate((
        ("m1", out_g, wide_g, (("m1", 0, 384, 0),)),
        ("m2", out_u, wide_u, (("m1", 384, 256, 0), ("m2", 0, 128, 256))),
        ("m2", out_d, wide_d, (("m2", 128, 384, 0),)),
        ("o", out_o, wide_o, (("o", 0, 256, 0),)),
        ("q", out_q, wide_q, (("q", 0, 256, 0),)),
        ("kv", out_k, wide_k, (("kv", 0, 128, 0),)),
        ("kv", out_v, wide_v, (("kv", 128, 128, 0),)),
    )):
        if name in arrived:
            arrived.pop(name).wait()
        width = place.shape[1] // 8
        for half in range(2):
            part = slice(half * 64, half * 64 + 64)
            for group, start, size, at in pieces:
                for j in range(8):
                    place[part, j * width + at : j * width + at + size] = held[group][
                        half, j, :, start : start + size
                    ].astype(F32)
            copy = pltpu.make_async_copy(place.at[part], out.at[part], sems.at[5 + index * 2 + half])
            copy.start()
            sent.append(copy)
    for copy in through:
        copy.wait()
    for held_rows, out, index in ((held_mixed, out_mixed, 21), (held_input, out_input, 22)):
        copy = pltpu.make_async_copy(held_rows, out, sems.at[index])
        copy.start()
        sent.append(copy)
    out_norm[...] = gains[1, :]
    out_mlp[...] = gains[0, :]
    out_qg[...] = gains[2, 0:128]
    out_kg[...] = gains[2, 128:256]
    for copy in sent:
        copy.wait()


def solution(mesh):
    rows = P(("fsdp", "ctx"), None)
    weight = P("fsdp", None)
    return jax.shard_map(
        on_device,
        mesh=mesh,
        in_specs=(rows, rows) + (weight,) * 7 + (P(),) * 4,
        out_specs=(rows, rows) + (weight,) * 7 + (P(),) * 4,
        check_vma=False,
    )
```

```python
import math

import jax
import jax.numpy as jnp
import numpy as np
from jax import lax
from jax.experimental import pallas as pl
from jax.experimental.pallas import tpu as pltpu
from jax.sharding import PartitionSpec as P

MESH = pl.DeviceIdType.MESH
EPSILON = 1e-06
THETA = 1000000.0
HEAD_DIM = 128
SCALE = 1.0 / math.sqrt(HEAD_DIM)
SCALE_LOG2 = SCALE * math.log2(math.e)
F32 = jnp.float32
BF16 = jnp.bfloat16
DIST = (1, 3, 2)
SLOT = {1: 0, 3: 1, 2: 2}
COPIES = 194
LOCAL_COPIES = 22
COLS_MLP, COLS_OUT, COLS_QKV = 1152, 256, 512
GROUPS = {"m1": (640, 384), "m2": (512, 256), "o": (256, 128), "q": (256, 128), "kv": (256, 128)}


def mm(left, right):
    return jnp.dot(left, right, preferred_element_type=F32)


def mm_last(left, right):
    return lax.dot_general(left, right, (((1,), (1,)), ((), ())), preferred_element_type=F32)


def mm_first(left, right):
    return lax.dot_general(left, right, (((0,), (0,)), ((), ())), preferred_element_type=F32)


def rms_scale(rows):
    return lax.rsqrt(jnp.mean(rows * rows, -1, keepdims=True) + EPSILON)


def swap_halves(heads):
    return pltpu.roll(heads, HEAD_DIM // 2, 1)


def rope_split(table):
    lane = lax.broadcasted_iota(jnp.int32, table.shape, 1)
    other = swap_halves(table)
    cosine = jnp.where(lane < HEAD_DIM // 2, table, other)
    sine = jnp.where(lane < HEAD_DIM // 2, -other, table)
    return cosine, sine


class Remote:
    def __init__(self, sems, src, dst, device, landing):
        self.sems, self.device = sems, device
        self.src, self.dst, self.landing = src, dst, landing

    def describe(self, src, dst, device):
        send, recv, index = self.sems
        return pltpu.make_async_remote_copy(
            src_ref=src,
            dst_ref=dst,
            send_sem=send.at[index],
            recv_sem=recv.at[index],
            device_id=device,
            device_id_type=MESH,
        )

    def launch(self, src, dst, device):
        self.describe(src, dst, device).start()

    def start(self):
        self.launch(self.src, self.dst, self.device)

    def wait_send(self):
        self.describe(self.src, self.dst, self.device).wait_send()

    def wait_recv(self):
        self.describe(self.landing, self.landing, self.device).wait_recv()


def kernel(
    tok_hbm, cot_hbm, wq, wk, wv, wo, wg, wu, wd, ng_hbm, mg_hbm, qg_hbm, kg_hbm, rope_hbm,
    mixed_out, ig_out, out, gains_ref,
    mixed_ref, ig_ref, tok, ng_ref, mg_ref, qg_ref, kg_ref,
    g1, g2, g3, g4, g1_turned, w_a, w_o, w_m, raw, qh, kv, rope, oa, att, do, dq, dk, dv, dqkv,
    hid, dgu, lse_row, delta_row, resid, d_resid,
    rs_send, rs_sib, rs_x, dkv_send, dkv_recv, gain_early, early_x, early_yz, late_x, late_yz,
    gw, z1, y1, z2s, y2s, y2, z2, full, send, recv, local_sem,
):
    f_index = lax.axis_index("fsdp")
    c_index = lax.axis_index("ctx")
    z = lax.rem(f_index, 4)
    ylo = lax.div(f_index, 4)
    core = lax.rem(c_index, 2)
    x = lax.rem(lax.div(c_index, 2), 4)
    yhi = lax.div(c_index, 8)
    y = yhi * 2 + ylo
    slice_index = x * 2 + core

    def wrap(value):
        return lax.rem(value + 8, 4)

    def device(dx=0, dy=0, dz=0, dcore=0):
        to_x, to_y, to_z = wrap(x + dx), wrap(y + dy), wrap(z + dz)
        to_core = lax.rem(core + dcore, 2)
        return {
            "fsdp": lax.rem(to_y, 2) * 4 + to_z,
            "ctx": lax.div(to_y, 2) * 8 + to_x * 2 + to_core,
        }

    counter = [0]

    def sems():
        index = counter[0]
        counter[0] += 1
        assert index < COPIES
        return (send, recv, index)

    pending = []

    def remote(src, dst, to, landing):
        copy = Remote(sems(), src, dst, to, landing)
        copy.start()
        pending.append(copy)
        return copy

    def several(copies, total):
        copy = Remote(sems(), total, total, sibling, total)
        for src, dst, to in copies:
            copy.launch(src, dst, to)
        pending.append(copy)
        return copy

    def drain():
        while pending:
            pending.pop().wait_send()

    def rows(start, size):
        return pl.ds(pl.multiple_of(start, size), size)

    sibling = device(dcore=1)
    partners = [sibling]
    partners += [device(dx=d) for d in DIST]
    partners += [device(dy=d) for d in DIST]
    partners += [device(dx=d, dcore=1) for d in DIST]
    partners += [device(dz=d) for d in DIST]
    partners += [device(dy=a, dz=b) for a in DIST for b in DIST]
    partners += [device(dx=d, dy=2) for d in DIST]

    def columns(ref, width):
        return ref.at[:, pl.ds(pl.multiple_of(slice_index * width, 128), width)]

    local = []

    def fetch(src, dst):
        assert len(local) < LOCAL_COPIES
        copy = pltpu.make_async_copy(src, dst, local_sem.at[len(local)])
        copy.start()
        local.append(copy)
        return copy

    fetch_tok = [fetch(tok_hbm, tok), fetch(ng_hbm, ng_ref)]
    fetch_a = [
        fetch(columns(wq, 256), w_a.at[f_index, :, 0:256]),
        fetch(columns(wk, 128), w_a.at[f_index, :, 256:384]),
        fetch(columns(wv, 128), w_a.at[f_index, :, 384:512]),
    ]
    fetch_o = [fetch(columns(wo, 256), w_o.at[f_index])]
    fetch_m = [
        fetch(columns(wg, 384), w_m.at[f_index, :, 0:384]),
        fetch(columns(wu, 384), w_m.at[f_index, :, 384:768]),
        fetch(columns(wd, 384), w_m.at[f_index, :, 768:1152]),
    ]
    fetch_rest = [
        fetch(rope_hbm, rope),
        fetch(cot_hbm.at[0:64], g3.at[0, x, rows(core * 64, 64)]),
        fetch(cot_hbm.at[64:128], g3.at[1, x, rows(core * 64, 64)]),
        fetch(mg_hbm, mg_ref),
        fetch(qg_hbm, qg_ref),
        fetch(kg_hbm, kg_ref),
    ]

    barrier = pltpu.get_barrier_semaphore()
    for partner in partners:
        pl.semaphore_signal(barrier, inc=1, device_id=partner, device_id_type=MESH)

    class Gather:
        def __init__(self, part, whole, held=pending):
            def to(dx, half, steps):
                block = part(wrap(x - (steps - 1) * dx), core, half)
                landing = part(wrap(x - steps * dx), core, half)
                return Remote(sems(), block, block, device(dx=dx), landing)

            def to_pair(d):
                block = whole(wrap(x - d), core)
                return Remote(sems(), block, block, sibling, whole(wrap(x - d), 1 - core))

            self.held = held
            self.plus = {half: to(1, half, 1) for half in (0, 1)}
            self.minus = {half: to(3, half, 1) for half in (0, 1)}
            self.far_plus, self.far_minus = to(1, 0, 2), to(3, 1, 2)
            self.pair = {d: to_pair(d) for d in (0,) + DIST}

        def start(self, *copies):
            for copy in copies:
                copy.start()
                self.held.append(copy)

        def begin(self):
            self.start(self.plus[0], self.minus[1], self.plus[1], self.minus[0], self.pair[0])
            return self

        def relay(self):
            self.plus[0].wait_recv()
            self.start(self.far_plus)
            self.minus[1].wait_recv()
            self.start(self.far_minus)

        def forward(self, d):
            if d == 1:
                self.plus[1].wait_recv()
            elif d == 3:
                self.minus[0].wait_recv()
            else:
                self.far_plus.wait_recv()
                self.far_minus.wait_recv()
            self.start(self.pair[d])

        def ready(self, d):
            self.pair[d].wait_recv()

    def gather_plain(ref):
        return Gather(
            lambda t, c, half: ref.at[t, rows(c * 128 + half * 64, 64)],
            lambda t, c: ref.at[t, rows(c * 128, 128)],
        ).begin()

    def gather_batch(ref, batch):
        return Gather(
            lambda t, c, half: ref.at[batch, t, rows(c * 64 + half * 32, 32)],
            lambda t, c: ref.at[batch, t, rows(c * 64, 64)],
        ).begin()

    def gather_batches(ref):
        return Gather(
            lambda t, c, half: ref.at[half, t, rows(c * 64, 64)],
            lambda t, c: ref.at[:, t, rows(c * 64, 64)],
        ).begin()

    class Scatter:
        def __init__(self, index, buffer, half, batch=0):
            self.half, self.batch = half, batch
            self.part, self.pair, self.ring = rs_send.at[buffer], rs_sib.at[index], rs_x.at[index]
            self.pair_copy, self.near, self.far = {}, {}, {}

        def part_rows(self, which, half=None):
            start = self.batch * 4 * self.half + which * 2 * self.half
            if half is None:
                return rows(start, 2 * self.half)
            return rows(start + half * self.half, self.half)

        def pair_rows(self, half=None):
            start = self.batch * 2 * self.half
            if half is None:
                return pl.ds(start, 2 * self.half)
            return pl.ds(start + half * self.half, self.half)

        def emit(self, d):
            slot = self.pair.at[d, self.pair_rows()]
            self.pair_copy[d] = remote(self.part.at[d, self.part_rows(1 - core)], slot, sibling, slot)

        def store(self, d, value):
            self.part[d, pl.ds(self.batch * 4 * self.half, 4 * self.half), :] = value.astype(BF16)
            self.emit(d)

        def summed(self, d, half=None):
            return self.part[d, self.part_rows(core, half), :].astype(F32) + self.pair[
                d, self.pair_rows(half), :
            ].astype(F32)

        def to(self, d, place, half, dx):
            slot = self.ring.at[place, self.pair_rows(half)]
            return remote(self.pair.at[d, self.pair_rows(half)], slot, device(dx=dx), slot)

        def forward(self, d):
            self.pair_copy[d].wait_recv()
            if d == 2:
                self.pair[d, self.pair_rows(), :] = self.summed(d).astype(BF16)
                self.far = {0: self.to(2, 2, 0, 1), 1: self.to(2, 2, 1, 3)}
            else:
                half, place = (1, 0) if d == 1 else (0, 1)
                self.pair[d, self.pair_rows(half), :] = self.summed(d, half).astype(BF16)
                self.near[d] = self.to(d, place, half, d)

        def relay(self):
            for d, half, place in ((1, 0, 0), (3, 1, 1)):
                self.far[half].wait_recv()
                value = self.summed(d, half) + self.ring[2, self.pair_rows(half), :].astype(F32)
                self.pair[d, self.pair_rows(half), :] = value.astype(BF16)
                self.near[d, half] = self.to(d, place, half, d)

        def total(self):
            self.pair_copy[0].wait_recv()
            value = self.summed(0)
            for d, half, place in ((1, 0, 0), (3, 1, 1)):
                self.near[d].wait_recv()
                self.near[d, half].wait_recv()
                value = value + self.ring[place, self.pair_rows(), :].astype(F32)
            return value

        def release(self):
            for copy in self.pair_copy.values():
                copy.wait_send()
                pending.remove(copy)

    class WeightGather:
        def __init__(self, ref, fetched):
            self.ref = ref
            for copy in fetched:
                copy.wait()
            own = ref.at[f_index]
            self.along_z = {
                d: remote(own, own, device(dz=d), ref.at[ylo * 4 + wrap(z - d)]) for d in DIST
            }
            held, coming = ref.at[pl.ds(ylo * 4, 4)], ref.at[pl.ds((1 - ylo) * 4, 4)]
            self.along_y = Remote(sems(), held, held, sibling, coming)

        def spread(self, d):
            if d:
                self.along_z[d].wait_recv()
            held = ylo * 4 + wrap(z - d)
            for dy, part in ((1, pl.ds(0, 64)), (3, pl.ds(64, 64))):
                block = self.ref.at[held, part]
                self.along_y.launch(block, block, device(dy=dy))

        def finish(self):
            self.along_y.wait_recv()
            pending.append(self.along_y)

    class WeightGrad:
        def __init__(self, name, ring_first=False):
            cols, first = GROUPS[name]
            self.ring_first = ring_first
            self.gw, self.z1, self.y1, self.z2s = gw[name], z1[name], y1[name], z2s[name]
            self.y2s, self.y2, self.z2 = y2s[name], y2[name], z2[name]
            self.full, self.out = full[name], out[name]
            self.left, self.right = slice(0, first), slice(first, cols)

        def stage_one(self):
            copies = []
            for d in DIST:
                src = self.gw.at[:, wrap(z + d), :, self.left]
                copies.append((src, self.z1.at[SLOT[d]], device(dz=d)))
            self.one_z = several(copies, self.z1)
            copies = []
            for d in DIST:
                to_y = wrap(y + d)
                half = rows(lax.div(to_y, 2) * 64, 64)
                src = self.gw.at[lax.rem(to_y, 2), :, half, self.right]
                copies.append((src, self.y1.at[SLOT[d]], device(dy=d)))
            self.one_y = several(copies, self.y1)

        def stage_two(self):
            self.one_z.wait_recv()
            total = self.gw[:, z, :, self.left].astype(F32)
            for d in DIST:
                total = total + self.z1[SLOT[d]].astype(F32)
            self.z2s[...] = total.astype(BF16).reshape(self.z2s.shape)
            copies = []
            for d in DIST:
                to_y = wrap(y + d)
                src = self.z2s.at[lax.rem(to_y, 2), lax.div(to_y, 2)]
                copies.append((src, self.y2.at[SLOT[d]], device(dy=d)))
            self.two_y = several(copies, self.y2)
            self.one_y.wait_recv()
            total = self.gw[ylo, :, rows(yhi * 64, 64), self.right].astype(F32)
            for d in DIST:
                total = total + self.y1[SLOT[d]].astype(F32)
            self.y2s[...] = total.astype(BF16)
            copies = []
            for d in DIST:
                copies.append((self.y2s.at[wrap(z + d)], self.z2.at[SLOT[d]], device(dz=d)))
            self.two_z = several(copies, self.z2)

        def sums(self):
            self.two_y.wait_recv()
            total = self.z2s[ylo, yhi].astype(F32)
            for d in DIST:
                total = total + self.y2[SLOT[d]].astype(F32)
            self.full[yhi, x, core, :, self.left] = total.astype(BF16)
            self.two_z.wait_recv()
            total = self.y2s[z].astype(F32)
            for d in DIST:
                total = total + self.z2[SLOT[d]].astype(F32)
            self.full[yhi, x, core, :, self.right] = total.astype(BF16)

        def stage_three(self):
            self.sums()
            own = self.full.at[yhi, x, core]
            if self.ring_first:
                self.ring = [
                    remote(own, own, device(dx=d), self.full.at[yhi, wrap(x - d), core])
                    for d in DIST
                ]
            else:
                self.flip = remote(own, own, device(dy=2), self.full.at[1 - yhi, x, core])

        def stage_four(self):
            if self.ring_first:
                for copy in self.ring:
                    copy.wait_recv()
                held = self.full.at[yhi, :, core]
                self.ring = [remote(held, held, device(dy=2), self.full.at[1 - yhi, :, core])]
            else:
                self.flip.wait_recv()
                held = self.full.at[:, x, core]
                self.ring = [
                    remote(held, held, device(dx=d), self.full.at[:, wrap(x - d), core])
                    for d in DIST
                ]

        def stage_direct(self):
            self.sums()
            own = self.full.at[yhi, x, core]
            self.ring = [
                remote(own, own, device(dx=d), self.full.at[yhi, wrap(x - d), core]) for d in DIST
            ]
            copies = [(own, own, device(dx=d, dy=2)) for d in (0,) + DIST]
            self.ring.append(several(copies, self.full.at[1 - yhi, :, core]))

        def stage_five(self):
            for copy in self.ring:
                copy.wait_recv()
            held = self.full.at[:, :, core]
            self.pair = remote(held, held, sibling, self.full.at[:, :, 1 - core])

        def stage_six(self):
            self.pair.wait_recv()
            fetch(self.full, self.out)

    grad_m1, grad_m2, grad_o = WeightGrad("m1"), WeightGrad("m2", True), WeightGrad("o")
    grad_q, grad_kv = WeightGrad("q"), WeightGrad("kv")

    def weight_grad(parts):
        def chunk(index, carry):
            lanes = pl.ds(pl.multiple_of(index * 256, 256), 256)
            block = pl.ds(lax.rem(index, 2) * 2, 2)
            for left, right, source, target, cols, turned in parts:
                width = cols.stop - cols.start
                operand = right[..., source].reshape(1024, width)
                if turned:
                    value = mm(left[lanes, :], operand)
                else:
                    value = mm_first(left[..., lanes].reshape(1024, 256), operand)
                target[lax.div(index, 2), block, :, cols] = value.astype(BF16).reshape(
                    2, 128, width
                )
            return carry

        lax.fori_loop(0, 4, chunk, 0)

    with jax.named_scope("first_norm"):
        kv[:, :, 256:384] = jnp.ones((8, 256, 128), BF16)
        gain_early[...] = jnp.zeros_like(gain_early)
        for copy in fetch_tok:
            copy.wait()
        inputs = tok[...].astype(F32)
        g1[x, rows(core * 128, 128), :] = (inputs * rms_scale(inputs) * ng_ref[...]).astype(BF16)
    with jax.named_scope("entry_barrier"):
        pl.semaphore_wait(barrier, len(partners))
    across = device(dy=2)
    far_held = []
    far = Gather(
        lambda t, c, half: g1_turned.at[rows(t * 256 + c * 128 + half * 64, 64)],
        lambda t, c: g1_turned.at[rows(t * 256 + c * 128, 128)],
        far_held,
    )
    with jax.named_scope("gather_start"):
        rows_one = gather_plain(g1)
        gather_a = WeightGather(w_a, fetch_a)
        gather_a.spread(0)
        place = rows(x * 256 + core * 128, 128)
        send_rows = Remote(
            sems(), g1.at[x, rows(core * 128, 128)], g1_turned.at[place], across, g1_turned.at[place]
        )

        @pl.when(yhi == 0)
        def _():
            send_rows.start()

        rows_one.relay()
        gather_a.spread(1)
        rows_one.forward(1)
        gather_a.spread(3)
        rows_one.forward(3)
        gather_o = WeightGather(w_o, fetch_o)

        @pl.when(yhi == 1)
        def _():
            send_rows.wait_recv()
            far.begin()

        gather_a.spread(2)
        gather_m = WeightGather(w_m, fetch_m)
        rows_one.forward(2)
        for copy in fetch_rest:
            copy.wait()

        @pl.when(yhi == 1)
        def _():
            far.relay()

        gather_a.finish()
        for d in (0,) + DIST:
            gather_o.spread(d)
        gather_m.spread(0)

    def project(t):
        value = mm(g1[t], w_a[...].reshape(1024, COLS_QKV))
        cosine, sine = rope_split(rope[yhi * 4 + t])
        raw[t] = value[:, 0:384]
        for head in range(3):
            one = value[:, head * 128 : head * 128 + 128]
            gain = qg_ref[...] if head < 2 else kg_ref[...]
            scaled = one * rms_scale(one) * gain
            turned = (scaled * cosine + swap_halves(scaled) * sine).astype(BF16)
            if head < 2:
                qh[t, head * 256 : head * 256 + 256, :] = turned
            else:
                kv[yhi * 4 + t, :, 0:128] = turned
        kv[yhi * 4 + t, :, 128:256] = value[:, 384:512].astype(BF16)

    def project_far(t):
        value = mm(
            g1_turned[rows(t * 256, 256), :], w_a[:, :, 256:512].reshape(1024, 256)
        )
        cosine, sine = rope_split(rope[t])
        scaled = value[:, 0:128] * rms_scale(value[:, 0:128]) * kg_ref[...]
        kv[t, :, 0:128] = (scaled * cosine + swap_halves(scaled) * sine).astype(BF16)
        kv[t, :, 128:256] = value[:, 128:256].astype(BF16)

    with jax.named_scope("qkv"):
        for place, d in enumerate((0,) + DIST):
            rows_one.ready(d)
            project(wrap(x - d))
            if place == 2:

                @pl.when(yhi == 1)
                def _():
                    far.forward(1)
                    far.forward(3)

        rows_cot = gather_batches(g3)

    def attend_own(i):
        size = 256 * (i + 1)
        block = pl.ds(yhi * 4, i + 1)
        soft = jnp.exp2(mm_last(qh[i], kv[block, :, 0:128].reshape(size, 128)) * SCALE_LOG2)
        row = lax.broadcasted_iota(jnp.int32, (512, size), 0)
        col = lax.broadcasted_iota(jnp.int32, (512, size), 1)
        soft = jnp.where(col <= lax.rem(row, 256) + 256 * i, soft, 0.0).astype(BF16)
        oa[i] = mm(soft, kv[block, :, 128:384].reshape(size, 256))

    with jax.named_scope("attend_own"):
        for i in range(3):
            attend_own(i)
        rows_cot.relay()
        gather_m.spread(1)
        gather_m.spread(3)
        attend_own(3)

        @pl.when(yhi == 1)
        def _():
            far.forward(2)
            for d in (0,) + DIST:
                far.ready(d)
                project_far(wrap(x - d))
            for copy in far_held:
                copy.wait_send()

    def attend_across(i):
        @pl.when(yhi == 1)
        def _():
            def step(j, carry):
                two = pl.ds(j * 2, 2)
                soft = jnp.exp2(mm_last(qh[i], kv[two, :, 0:128].reshape(512, 128)) * SCALE_LOG2)
                oa[i] += mm(soft.astype(BF16), kv[two, :, 128:384].reshape(512, 256))
                return carry

            lax.fori_loop(0, 2, step, 0)

    def attend_end(i):
        both = oa[i]
        total = both[:, 128:256]
        exact = both[:, 0:128] / total
        oa[i, :, 0:128] = exact
        lse_row[i] = jnp.transpose(jnp.log(total) * math.log2(math.e))[0:8, :]
        exact = exact.astype(BF16)
        for head in range(2):
            for which in range(2):
                for batch in range(2):
                    start = head * 256 + which * 128 + batch * 64
                    att[batch, i, which * 64 : which * 64 + 64, head * 128 : head * 128 + 128] = (
                        exact[start : start + 64]
                    )

    branch = [Scatter(0, 0, 32, batch) for batch in range(2)]
    order = (2, 1, 3, 0)
    with jax.named_scope("branch"):
        for place, d in enumerate(order):
            t = wrap(x + d)
            attend_across(t)
            attend_end(t)
            if place == 0:
                gather_o.finish()
            for batch in range(2):
                branch[batch].store(d, mm_last(att[batch, t], w_o[...].reshape(1024, COLS_OUT)))
            if place:
                for batch in range(2):
                    branch[batch].forward(order[place - 1])
                rows_cot.forward(DIST[place - 1])
            if place == 0:
                gather_m.spread(2)

    def batch_rows(batch):
        return slice(batch * 64, batch * 64 + 64)

    rows_two = []
    with jax.named_scope("resid"):
        for batch in range(2):
            branch[batch].relay()
        for batch in range(2):
            value = branch[batch].total() + tok[batch_rows(batch), :].astype(F32)
            resid[batch_rows(batch), :] = value
            g2[batch, x, rows(core * 64, 64), :] = (
                value * rms_scale(value) * mg_ref[...]
            ).astype(BF16)
            rows_two.append(gather_batch(g2, batch))
        g1_turned[...] = jnp.transpose(g1[...].reshape(1024, 1024))
        for batch in range(2):
            rows_two[batch].relay()
            branch[batch].release()
        gather_m.finish()

    back_two = [Scatter(1, 1, 32, batch) for batch in range(2)]

    def feed_forward(batch, d):
        t = wrap(x - d)
        rows_two[batch].ready(d)
        w_gate_up = w_m[:, :, 0:768].reshape(1024, 768)
        w_d = w_m[:, :, 768:1152].reshape(1024, 384)
        both = mm(g2[batch, t], w_gate_up)
        d_hidden = mm(g3[batch, t], w_d)
        gate, up = both[:, 0:384], both[:, 384:768]
        sig = jax.nn.sigmoid(gate)
        active = gate * sig
        hid[batch, t] = (active * up).astype(BF16)
        dgu[batch, t, :, 0:384] = (d_hidden * up * sig * (1.0 + gate * (1.0 - sig))).astype(BF16)
        dgu[batch, t, :, 384:768] = (d_hidden * active).astype(BF16)
        back_two[batch].store((4 - d) % 4, mm_last(dgu[batch, t], w_gate_up))

    with jax.named_scope("mlp"):
        for d in (0,) + DIST:
            rows_cot.ready(d)
        feed_forward(0, 0)
        rows_two[0].forward(1)
        rows_two[0].forward(3)
        feed_forward(1, 0)
        feed_forward(0, 1)
        rows_two[0].forward(2)
        feed_forward(0, 3)
        rows_two[1].forward(1)
        rows_two[1].forward(3)
        back_two[0].forward(3)
        feed_forward(0, 2)
        back_two[0].forward(1)
        feed_forward(1, 1)
        back_two[0].forward(2)
        rows_two[1].forward(2)
        feed_forward(1, 3)
        back_two[1].forward(3)
        back_two[1].forward(1)
        feed_forward(1, 2)
        back_two[0].relay()
        back_two[1].forward(2)

    grads_m1 = ((g2, dgu, slice(0, 640), grad_m1.gw, slice(0, 640), False),)
    grads_m2 = (
        (g2, dgu, slice(640, 768), grad_m2.gw, slice(0, 128), False),
        (g3, hid, slice(0, 384), grad_m2.gw, slice(128, 512), False),
    )
    grads_o = ((g4, att, slice(0, 256), grad_o.gw, slice(0, 256), False),)
    grads_q = ((g1_turned, dqkv, slice(0, 256), grad_q.gw, slice(0, 256), True),)
    grads_kv = ((g1_turned, dqkv, slice(256, 512), grad_kv.gw, slice(0, 256), True),)
    rows_back = []

    def back_resid(batch):
        part = batch_rows(batch)
        d_normed = back_two[batch].total()
        value = resid[part, :]
        scaling = rms_scale(value)
        normed = value * scaling
        gain_early[:, 0:1024] += jnp.sum(d_normed * normed, 0, keepdims=True)
        d_normed = d_normed * mg_ref[...]
        value = scaling * (
            d_normed - normed * jnp.mean(d_normed * normed, -1, keepdims=True)
        ) + g3[batch, x, rows(core * 64, 64), :].astype(F32)
        d_resid[part, :] = value
        g4[batch, x, rows(core * 64, 64), :] = value.astype(BF16)
        rows_back.append(gather_batch(g4, batch))

    mlp_out = Scatter(2, 0, 64)

    def mlp_block(d):
        w_d = w_m[:, :, 768:1152].reshape(1024, 384)
        t = wrap(x + d)
        for batch in range(2):
            value = mm_last(hid[batch, t], w_d).astype(BF16)
            for which in range(2):
                start = which * 128 + batch * 64
                mlp_out.part[d, start : start + 64, :] = value[which * 64 : which * 64 + 64]
        mlp_out.emit(d)

    with jax.named_scope("d_resid"):
        weight_grad(grads_m1)
        grad_m1.stage_one()
        back_resid(0)
        back_two[1].relay()
        back_resid(1)
        rows_back[0].relay()
        weight_grad(grads_m2)
        grad_m2.stage_one()
        rows_back[1].relay()
        for to in order:
            mlp_block(to)

    def back_out(t):
        for batch in range(2):
            value = mm(g4[batch, t], w_o[...].reshape(1024, COLS_OUT)).astype(BF16)
            for head in range(2):
                for which in range(2):
                    start = head * 256 + which * 128 + batch * 64
                    do[t, start : start + 64, :] = value[
                        which * 64 : which * 64 + 64, head * 128 : head * 128 + 128
                    ]
        product = do[t].astype(F32) * oa[t, :, 0:128]
        delta_row[t] = jnp.broadcast_to(
            jnp.sum(jnp.transpose(product), 0, keepdims=True), (8, 512)
        )

    def tile(i, start, size, masked):
        keys = pl.ds(start, size)
        width = 256 * size
        key_rows, queries, grads = kv[keys, :, 0:128].reshape(width, 128), qh[i], do[i]
        soft = jnp.exp2(mm_last(key_rows, queries) * SCALE_LOG2 - lse_row[i, 0:1, :])
        if masked:
            row = lax.broadcasted_iota(jnp.int32, (width, 512), 0)
            col = lax.broadcasted_iota(jnp.int32, (width, 512), 1)
            soft = jnp.where(row <= lax.rem(col, 256) + (width - 256), soft, 0.0)
        d_soft = mm_last(kv[keys, :, 128:256].reshape(width, 128), grads)
        d_scores = (soft * (d_soft - delta_row[i, 0:1, :])).astype(BF16)
        dv[keys] += mm(soft.astype(BF16), grads).reshape(size, 256, 128)
        dk[keys] += mm(d_scores, queries).reshape(size, 256, 128)
        dq[i] += mm_first(d_scores, key_rows)

    def back_across(t):
        @pl.when(yhi == 1)
        def _():
            tile(t, 0, 4, False)

    send_back = [
        Remote(sems(), dkv_send.at[pair], dkv_recv.at[pair], across, dkv_recv.at[pair])
        for pair in range(2)
    ]

    def back_across_end(pair):
        @pl.when(yhi == 1)
        def _():
            for d in (3, 2):
                tile(wrap(x - d), pair * 2, 2, False)
            two = slice(pair * 2, pair * 2 + 2)
            dkv_send[pair, :, :, 0:128] = dk[two].astype(BF16)
            dkv_send[pair, :, :, 128:256] = dv[two].astype(BF16)
            send_back[pair].start()

    def back_ready(d):
        for batch in range(2):
            rows_back[batch].ready(d)
        back_out(wrap(x - d))

    def back_forward(d):
        for batch in range(2):
            rows_back[batch].forward(d)

    with jax.named_scope("attend_back_across"):
        dq[...] = jnp.zeros_like(dq)
        dk[...] = jnp.zeros_like(dk)
        dv[...] = jnp.zeros_like(dv)
        back_ready(0)
        back_forward(1)
        back_forward(3)
        back_across(x)
        back_ready(1)
        back_forward(2)
        grad_m1.stage_two()
        back_across(wrap(x - 1))
        back_ready(3)
        back_ready(2)
        for to in order[:3]:
            mlp_out.forward(to)
        back_across_end(0)
        grad_m2.stage_two()
        grad_m1.stage_three()
        back_across_end(1)
    with jax.named_scope("out_weight_grads"):
        mlp_out.relay()
        weight_grad(grads_o)
        grad_o.stage_one()
        grad_m2.stage_three()

    with jax.named_scope("attend_back_own"):

        for i in range(3):
            tile(i, yhi * 4, i + 1, True)
        grad_m1.stage_four()
        tile(3, yhi * 4, 4, True)
        grad_m2.stage_four()

    with jax.named_scope("mixed"):
        mixed_ref[...] = (resid[...] + mlp_out.total()).astype(BF16)
        fetch(mixed_ref, mixed_out)

    def head_back(t, head):
        cosine, sine = rope_split(rope[yhi * 4 + t])
        one = raw[t, :, head * 128 : head * 128 + 128]
        if head < 2:
            grads, gain = dq[t, head * 256 : head * 256 + 256, :], qg_ref[...]
        else:
            grads, gain = dk[yhi * 4 + t], kg_ref[...]
        grads = grads * SCALE
        grads = grads * cosine - swap_halves(grads) * sine
        scaling = rms_scale(one)
        normed = one * scaling
        part = jnp.sum(grads * normed, 0, keepdims=True)
        grads = grads * gain
        value = scaling * (grads - normed * jnp.mean(grads * normed, -1, keepdims=True))
        dqkv[t, :, head * 128 : head * 128 + 128] = value.astype(BF16)
        return part

    def query_back(t, carry):
        return carry + head_back(t, 0) + head_back(t, 1)

    def key_back(t, carry):
        dqkv[t, :, 384:512] = dv[yhi * 4 + t].astype(BF16)
        return carry + head_back(t, 2)

    def over_x(slots, value):
        slots[slice_index] = value
        own = slots.at[slice_index]
        copies = [(own, own, sibling)]
        copies += [(own, own, device(dx=d, dcore=flip)) for d in DIST for flip in (0, 1)]
        return several(copies, slots.at[0:7])

    def over_yz(slots, value):
        place = y * 4 + z
        slots[place] = value
        own = slots.at[place]
        steps = (0,) + DIST
        copies = [(own, own, device(dy=a, dz=b)) for a in steps for b in steps if a or b]
        return several(copies, slots.at[0:15])

    def total_of(slots, copies):
        copies.wait_recv()
        value = slots[0]
        for place in range(1, slots.shape[0]):
            value = value + slots[place]
        return value

    with jax.named_scope("head_norm_back"):
        zero = jnp.zeros((1, 128), F32)
        gain_early[:, 1024:1152] = lax.fori_loop(0, 4, query_back, zero)

    with jax.named_scope("qkv_weight_grads"):
        weight_grad(grads_q)
        grad_q.stage_one()

        @pl.when(yhi == 0)
        def _():
            for pair in range(2):
                send_back[pair].wait_recv()
                two = slice(pair * 2, pair * 2 + 2)
                dk[two] += dkv_recv[pair, :, :, 0:128].astype(F32)
                dv[two] += dkv_recv[pair, :, :, 128:256].astype(F32)

        gain_early[:, 1152:1280] = lax.fori_loop(0, 4, key_back, zero)
        weight_grad(grads_kv)
        grad_kv.stage_one()
        grad_o.stage_two()
    with jax.named_scope("d_normed"):
        for batch in range(2):
            back_two[batch].release()
        back_one = Scatter(3, 1, 64)
        for place, d in enumerate(order):
            back_one.store(d, mm_last(dqkv[wrap(x + d)], w_a[...].reshape(1024, COLS_QKV)))
            if place:
                back_one.forward(order[place - 1])
        early = over_x(early_x, gain_early[...])
        norm_gain = jnp.zeros((1, 1024), F32)
        for d in range(4):
            part = back_one.part[d].astype(F32) * g1[wrap(x + d)].astype(F32)
            norm_gain = norm_gain + jnp.sum(part, 0, keepdims=True)
        late = over_x(late_x, norm_gain / ng_ref[...])
        grad_m1.stage_five()
        grad_q.stage_two()
        back_one.relay()
        grad_kv.stage_two()
        grad_q.stage_direct()
        grad_o.stage_direct()
        early = over_yz(early_yz, total_of(early_x, early))
        late = over_yz(late_yz, total_of(late_x, late))
        grad_kv.stage_direct()
    with jax.named_scope("input_grad"):
        d_normed = back_one.total()
        inputs = tok[...].astype(F32)
        scaling = rms_scale(inputs)
        normed = inputs * scaling
        d_normed = d_normed * ng_ref[...]
        ig_ref[...] = (
            scaling * (d_normed - normed * jnp.mean(d_normed * normed, -1, keepdims=True))
            + d_resid[...]
        )
        fetch(ig_ref, ig_out)

    with jax.named_scope("tail"):
        grad_m2.stage_five()
        grad_m1.stage_six()
        grad_q.stage_five()
        grad_o.stage_five()
        gain_early[...] = total_of(early_yz, early)
        gains_ref[0:1, :] = gain_early[:, 0:1024]
        gains_ref[2:3, 0:256] = gain_early[:, 1024:1280]
        gains_ref[1:2, :] = total_of(late_yz, late)
        grad_m2.stage_six()
        grad_kv.stage_five()
        grad_q.stage_six()
        grad_o.stage_six()
        grad_kv.stage_six()
    with jax.named_scope("drain"):
        drain()

        @pl.when(yhi == 0)
        def _():
            send_rows.wait_send()

        @pl.when(yhi == 1)
        def _():
            for copy in send_back:
                copy.wait_send()

        for copy in local[-7:]:
            copy.wait()


def rope_table(length):
    half = HEAD_DIM // 2
    freqs = np.power(np.float32(THETA), np.float32(-2.0) * np.arange(half, dtype=np.float32) / HEAD_DIM)
    angles = np.arange(length, dtype=np.float32)[:, None] * freqs.astype(np.float32)[None, :]
    table = np.concatenate([np.cos(angles), np.sin(angles)], 1).astype(np.float32)
    return table.reshape(length // 256, 256, HEAD_DIM)


def on_device(
    tokens, cotangent, w_query, w_key, w_value, w_output, w_gate, w_up, w_down,
    norm_gain, mlp_gain, query_gain, key_gain,
):
    vmem = pl.BlockSpec(memory_space=pltpu.VMEM)
    hbm = pl.BlockSpec(memory_space=pl.ANY)

    def v(shape, dtype=BF16):
        return pltpu.VMEM(shape, dtype)

    scratch = [v((128, 1024)), v((128, 1024), F32)]
    scratch += [v((128, 1024)), v((1, 1024), F32), v((1, 1024), F32), v((1, 128), F32), v((1, 128), F32)]
    scratch += [v((4, 256, 1024))]
    scratch += [v((2, 4, 128, 1024)) for _ in range(3)]
    scratch += [v((1024, 1024))]
    scratch += [v((8, 128, COLS_QKV)), v((8, 128, COLS_OUT)), v((8, 128, COLS_MLP))]
    scratch += [
        v((4, 256, 384), F32),
        v((4, 512, 128)),
        v((8, 256, 384)),
        v((8, 256, 128), F32),
        v((4, 512, 256), F32),
        v((2, 4, 128, 256)),
        v((4, 512, 128)),
        v((4, 512, 128), F32),
        v((8, 256, 128), F32),
        v((8, 256, 128), F32),
        v((4, 256, 512)),
        v((2, 4, 128, 384)),
        v((2, 4, 128, 768)),
        v((4, 8, 512), F32),
        v((4, 8, 512), F32),
        v((128, 1024), F32),
        v((128, 1024), F32),
        v((2, 4, 256, 1024)),
        v((4, 4, 128, 1024)),
        v((4, 3, 128, 1024)),
        v((2, 2, 256, 256)),
        v((2, 2, 256, 256)),
    ]
    scratch += [v((1, 1280), F32)]
    scratch += [v((8, 1, 1280), F32), v((16, 1, 1280), F32)]
    scratch += [v((8, 1, 1024), F32), v((16, 1, 1024), F32)]
    shapes = (
        lambda cols, first: (2, 4, 128, cols),
        lambda cols, first: (3, 2, 128, first),
        lambda cols, first: (3, 4, 64, cols - first),
        lambda cols, first: (2, 2, 64, first),
        lambda cols, first: (4, 64, cols - first),
        lambda cols, first: (3, 64, first),
        lambda cols, first: (3, 64, cols - first),
        lambda cols, first: (2, 4, 2, 64, cols),
    )
    scratch += [{name: v(shape(*cols)) for name, cols in GROUPS.items()} for shape in shapes]
    scratch += [
        pltpu.SemaphoreType.DMA((COPIES,)),
        pltpu.SemaphoreType.DMA((COPIES,)),
        pltpu.SemaphoreType.DMA((LOCAL_COPIES,)),
    ]
    mixed, input_grad, grads, gains = pl.pallas_call(
        kernel,
        name="layer",
        out_shape=(
            jax.ShapeDtypeStruct((128, 1024), BF16),
            jax.ShapeDtypeStruct((128, 1024), F32),
            {n: jax.ShapeDtypeStruct((2, 4, 2, 64, c[0]), BF16) for n, c in GROUPS.items()},
            jax.ShapeDtypeStruct((8, 1024), F32),
        ),
        in_specs=[hbm] * 14,
        out_specs=(hbm, hbm, {name: hbm for name in GROUPS}, vmem),
        scratch_shapes=scratch,
        compiler_params=pltpu.CompilerParams(
            collective_id=0, has_side_effects=True, vmem_limit_bytes=63 * 2**20
        ),
    )(
        tokens, cotangent, w_query, w_key, w_value, w_output, w_gate, w_up, w_down,
        norm_gain[None, :], mlp_gain[None, :], query_gain[None, :], key_gain[None, :],
        jnp.asarray(rope_table(2048)),
    )

    widths = (256, 128, 128, 256, 384, 384, 384)
    return pl.pallas_call(
        finish,
        name="finish",
        out_shape=(
            jax.ShapeDtypeStruct((128, 1024), BF16),
            jax.ShapeDtypeStruct((128, 1024), F32),
            *(jax.ShapeDtypeStruct((128, 8 * width), F32) for width in widths),
            jax.ShapeDtypeStruct((1024,), F32),
            jax.ShapeDtypeStruct((1024,), F32),
            jax.ShapeDtypeStruct((128,), F32),
            jax.ShapeDtypeStruct((128,), F32),
        ),
        in_specs=[hbm, hbm, {name: hbm for name in GROUPS}, vmem],
        out_specs=(hbm,) * 9 + (vmem,) * 4,
        scratch_shapes=[
            {name: v((2, 8, 64, cols[0])) for name, cols in GROUPS.items()},
            tuple(v((128, 8 * width), F32) for width in widths),
            v((128, 1024)),
            v((128, 1024), F32),
            pltpu.SemaphoreType.DMA((23,)),
        ],
        compiler_params=pltpu.CompilerParams(vmem_limit_bytes=63 * 2**20),
    )(
        mixed, input_grad,
        {name: grads[name].reshape(2, 8, 64, cols[0]) for name, cols in GROUPS.items()}, gains,
    )


def finish(
    mixed, input_grad, grads, gains,
    out_mixed, out_input, out_q, out_k, out_v, out_o, out_g, out_u, out_d,
    out_norm, out_mlp, out_qg, out_kg, held, wide, held_mixed, held_input, sems,
):
    arrived = {}
    for index, name in enumerate(GROUPS):
        arrived[name] = pltpu.make_async_copy(grads[name], held[name], sems.at[index])
        arrived[name].start()
    through = [
        pltpu.make_async_copy(mixed, held_mixed, sems.at[19]),
        pltpu.make_async_copy(input_grad, held_input, sems.at[20]),
    ]
    for copy in through:
        copy.start()
    sent = []
    wide_q, wide_k, wide_v, wide_o, wide_g, wide_u, wide_d = wide
    for index, (name, out, place, pieces) in enumerate((
        ("m1", out_g, wide_g, (("m1", 0, 384, 0),)),
        ("m2", out_u, wide_u, (("m1", 384, 256, 0), ("m2", 0, 128, 256))),
        ("m2", out_d, wide_d, (("m2", 128, 384, 0),)),
        ("o", out_o, wide_o, (("o", 0, 256, 0),)),
        ("q", out_q, wide_q, (("q", 0, 256, 0),)),
        ("kv", out_k, wide_k, (("kv", 0, 128, 0),)),
        ("kv", out_v, wide_v, (("kv", 128, 128, 0),)),
    )):
        if name in arrived:
            arrived.pop(name).wait()
        width = place.shape[1] // 8
        for half in range(2):
            part = slice(half * 64, half * 64 + 64)
            for group, start, size, at in pieces:
                for j in range(8):
                    place[part, j * width + at : j * width + at + size] = held[group][
                        half, j, :, start : start + size
                    ].astype(F32)
            copy = pltpu.make_async_copy(place.at[part], out.at[part], sems.at[5 + index * 2 + half])
            copy.start()
            sent.append(copy)
    for copy in through:
        copy.wait()
    for held_rows, out, index in ((held_mixed, out_mixed, 21), (held_input, out_input, 22)):
        copy = pltpu.make_async_copy(held_rows, out, sems.at[index])
        copy.start()
        sent.append(copy)
    out_norm[...] = gains[1, :]
    out_mlp[...] = gains[0, :]
    out_qg[...] = gains[2, 0:128]
    out_kg[...] = gains[2, 128:256]
    for copy in sent:
        copy.wait()


def solution(mesh):
    rows = P(("fsdp", "ctx"), None)
    weight = P("fsdp", None)
    return jax.shard_map(
        on_device,
        mesh=mesh,
        in_specs=(rows, rows) + (weight,) * 7 + (P(),) * 4,
        out_specs=(rows, rows) + (weight,) * 7 + (P(),) * 4,
        check_vma=False,
    )
```

```python
import math

import jax
import jax.numpy as jnp
import numpy as np
from jax import lax
from jax.experimental import pallas as pl
from jax.experimental.pallas import tpu as pltpu
from jax.sharding import PartitionSpec as P

MESH = pl.DeviceIdType.MESH
EPSILON = 1e-06
THETA = 1000000.0
HEAD_DIM = 128
SCALE = 1.0 / math.sqrt(HEAD_DIM)
SCALE_LOG2 = SCALE * math.log2(math.e)
F32 = jnp.float32
BF16 = jnp.bfloat16
DIST = (1, 3, 2)
SLOT = {1: 0, 3: 1, 2: 2}
COPIES = 194
LOCAL_COPIES = 22
COLS_MLP, COLS_OUT, COLS_QKV = 1152, 256, 512
GROUPS = {"m1": (640, 384), "m2": (512, 256), "o": (256, 128), "q": (256, 128), "kv": (256, 128)}


def mm(left, right):
    return jnp.dot(left, right, preferred_element_type=F32)


def mm_last(left, right):
    return lax.dot_general(left, right, (((1,), (1,)), ((), ())), preferred_element_type=F32)


def mm_first(left, right):
    return lax.dot_general(left, right, (((0,), (0,)), ((), ())), preferred_element_type=F32)


def rms_scale(rows):
    return lax.rsqrt(jnp.mean(rows * rows, -1, keepdims=True) + EPSILON)


def swap_halves(heads):
    return pltpu.roll(heads, HEAD_DIM // 2, 1)


def rope_split(table):
    lane = lax.broadcasted_iota(jnp.int32, table.shape, 1)
    other = swap_halves(table)
    cosine = jnp.where(lane < HEAD_DIM // 2, table, other)
    sine = jnp.where(lane < HEAD_DIM // 2, -other, table)
    return cosine, sine


class Remote:
    def __init__(self, sems, src, dst, device, landing):
        self.sems, self.device = sems, device
        self.src, self.dst, self.landing = src, dst, landing

    def describe(self, src, dst, device):
        send, recv, index = self.sems
        return pltpu.make_async_remote_copy(
            src_ref=src,
            dst_ref=dst,
            send_sem=send.at[index],
            recv_sem=recv.at[index],
            device_id=device,
            device_id_type=MESH,
        )

    def launch(self, src, dst, device):
        self.describe(src, dst, device).start()

    def start(self):
        self.launch(self.src, self.dst, self.device)

    def wait_send(self):
        self.describe(self.src, self.dst, self.device).wait_send()

    def wait_recv(self):
        self.describe(self.landing, self.landing, self.device).wait_recv()


def kernel(
    tok_hbm, cot_hbm, wq, wk, wv, wo, wg, wu, wd, ng_hbm, mg_hbm, qg_hbm, kg_hbm, rope_hbm,
    mixed_out, ig_out, out, gains_ref,
    mixed_ref, ig_ref, tok, ng_ref, mg_ref, qg_ref, kg_ref,
    g1, g2, g3, g4, g1_turned, w_a, w_o, w_m, raw, qh, kv, rope, oa, att, do, dq, dk, dv, dqkv,
    hid, dgu, lse_row, delta_row, resid, d_resid,
    rs_send, rs_sib, rs_x, dkv_send, dkv_recv, gain_early, early_x, early_yz, late_x, late_yz,
    gw, z1, y1, z2s, y2s, y2, z2, full, send, recv, local_sem,
):
    f_index = lax.axis_index("fsdp")
    c_index = lax.axis_index("ctx")
    z = lax.rem(f_index, 4)
    ylo = lax.div(f_index, 4)
    core = lax.rem(c_index, 2)
    x = lax.rem(lax.div(c_index, 2), 4)
    yhi = lax.div(c_index, 8)
    y = yhi * 2 + ylo
    slice_index = x * 2 + core

    def wrap(value):
        return lax.rem(value + 8, 4)

    def device(dx=0, dy=0, dz=0, dcore=0):
        to_x, to_y, to_z = wrap(x + dx), wrap(y + dy), wrap(z + dz)
        to_core = lax.rem(core + dcore, 2)
        return {
            "fsdp": lax.rem(to_y, 2) * 4 + to_z,
            "ctx": lax.div(to_y, 2) * 8 + to_x * 2 + to_core,
        }

    counter = [0]

    def sems():
        index = counter[0]
        counter[0] += 1
        assert index < COPIES
        return (send, recv, index)

    pending = []

    def remote(src, dst, to, landing):
        copy = Remote(sems(), src, dst, to, landing)
        copy.start()
        pending.append(copy)
        return copy

    def several(copies, total):
        copy = Remote(sems(), total, total, sibling, total)
        for src, dst, to in copies:
            copy.launch(src, dst, to)
        pending.append(copy)
        return copy

    def drain():
        while pending:
            pending.pop().wait_send()

    def rows(start, size):
        return pl.ds(pl.multiple_of(start, size), size)

    sibling = device(dcore=1)
    partners = [sibling]
    partners += [device(dx=d) for d in DIST]
    partners += [device(dy=d) for d in DIST]
    partners += [device(dx=d, dcore=1) for d in DIST]
    partners += [device(dz=d) for d in DIST]
    partners += [device(dy=a, dz=b) for a in DIST for b in DIST]
    partners += [device(dx=d, dy=2) for d in DIST]

    def columns(ref, width):
        return ref.at[:, pl.ds(pl.multiple_of(slice_index * width, 128), width)]

    local = []

    def fetch(src, dst):
        assert len(local) < LOCAL_COPIES
        copy = pltpu.make_async_copy(src, dst, local_sem.at[len(local)])
        copy.start()
        local.append(copy)
        return copy

    fetch_tok = [fetch(tok_hbm, tok), fetch(ng_hbm, ng_ref)]
    fetch_a = [
        fetch(columns(wq, 256), w_a.at[f_index, :, 0:256]),
        fetch(columns(wk, 128), w_a.at[f_index, :, 256:384]),
        fetch(columns(wv, 128), w_a.at[f_index, :, 384:512]),
    ]
    fetch_o = [fetch(columns(wo, 256), w_o.at[f_index])]
    fetch_m = [
        fetch(columns(wg, 384), w_m.at[f_index, :, 0:384]),
        fetch(columns(wu, 384), w_m.at[f_index, :, 384:768]),
        fetch(columns(wd, 384), w_m.at[f_index, :, 768:1152]),
    ]
    fetch_rest = [
        fetch(rope_hbm, rope),
        fetch(cot_hbm.at[0:64], g3.at[0, x, rows(core * 64, 64)]),
        fetch(cot_hbm.at[64:128], g3.at[1, x, rows(core * 64, 64)]),
        fetch(mg_hbm, mg_ref),
        fetch(qg_hbm, qg_ref),
        fetch(kg_hbm, kg_ref),
    ]

    barrier = pltpu.get_barrier_semaphore()
    for partner in partners:
        pl.semaphore_signal(barrier, inc=1, device_id=partner, device_id_type=MESH)

    class Gather:
        def __init__(self, part, whole, held=pending):
            def to(dx, half, steps):
                block = part(wrap(x - (steps - 1) * dx), core, half)
                landing = part(wrap(x - steps * dx), core, half)
                return Remote(sems(), block, block, device(dx=dx), landing)

            def to_pair(d):
                block = whole(wrap(x - d), core)
                return Remote(sems(), block, block, sibling, whole(wrap(x - d), 1 - core))

            self.held = held
            self.plus = {half: to(1, half, 1) for half in (0, 1)}
            self.minus = {half: to(3, half, 1) for half in (0, 1)}
            self.far_plus, self.far_minus = to(1, 0, 2), to(3, 1, 2)
            self.pair = {d: to_pair(d) for d in (0,) + DIST}

        def start(self, *copies):
            for copy in copies:
                copy.start()
                self.held.append(copy)

        def begin(self):
            self.start(self.plus[0], self.minus[1], self.plus[1], self.minus[0], self.pair[0])
            return self

        def relay(self):
            self.plus[0].wait_recv()
            self.start(self.far_plus)
            self.minus[1].wait_recv()
            self.start(self.far_minus)

        def forward(self, d):
            if d == 1:
                self.plus[1].wait_recv()
            elif d == 3:
                self.minus[0].wait_recv()
            else:
                self.far_plus.wait_recv()
                self.far_minus.wait_recv()
            self.start(self.pair[d])

        def ready(self, d):
            self.pair[d].wait_recv()

    def gather_plain(ref):
        return Gather(
            lambda t, c, half: ref.at[t, rows(c * 128 + half * 64, 64)],
            lambda t, c: ref.at[t, rows(c * 128, 128)],
        ).begin()

    def gather_batch(ref, batch):
        return Gather(
            lambda t, c, half: ref.at[batch, t, rows(c * 64 + half * 32, 32)],
            lambda t, c: ref.at[batch, t, rows(c * 64, 64)],
        ).begin()

    def gather_batches(ref):
        return Gather(
            lambda t, c, half: ref.at[half, t, rows(c * 64, 64)],
            lambda t, c: ref.at[:, t, rows(c * 64, 64)],
        ).begin()

    class Scatter:
        def __init__(self, index, buffer, half, batch=0):
            self.half, self.batch = half, batch
            self.part, self.pair, self.ring = rs_send.at[buffer], rs_sib.at[index], rs_x.at[index]
            self.pair_copy, self.near, self.far = {}, {}, {}

        def part_rows(self, which, half=None):
            start = self.batch * 4 * self.half + which * 2 * self.half
            if half is None:
                return rows(start, 2 * self.half)
            return rows(start + half * self.half, self.half)

        def pair_rows(self, half=None):
            start = self.batch * 2 * self.half
            if half is None:
                return pl.ds(start, 2 * self.half)
            return pl.ds(start + half * self.half, self.half)

        def emit(self, d):
            slot = self.pair.at[d, self.pair_rows()]
            self.pair_copy[d] = remote(self.part.at[d, self.part_rows(1 - core)], slot, sibling, slot)

        def store(self, d, value):
            self.part[d, pl.ds(self.batch * 4 * self.half, 4 * self.half), :] = value.astype(BF16)
            self.emit(d)

        def summed(self, d, half=None):
            return self.part[d, self.part_rows(core, half), :].astype(F32) + self.pair[
                d, self.pair_rows(half), :
            ].astype(F32)

        def to(self, d, place, half, dx):
            slot = self.ring.at[place, self.pair_rows(half)]
            return remote(self.pair.at[d, self.pair_rows(half)], slot, device(dx=dx), slot)

        def forward(self, d):
            self.pair_copy[d].wait_recv()
            if d == 2:
                self.pair[d, self.pair_rows(), :] = self.summed(d).astype(BF16)
                self.far = {0: self.to(2, 2, 0, 1), 1: self.to(2, 2, 1, 3)}
            else:
                half, place = (1, 0) if d == 1 else (0, 1)
                self.pair[d, self.pair_rows(half), :] = self.summed(d, half).astype(BF16)
                self.near[d] = self.to(d, place, half, d)

        def relay(self):
            for d, half, place in ((1, 0, 0), (3, 1, 1)):
                self.far[half].wait_recv()
                value = self.summed(d, half) + self.ring[2, self.pair_rows(half), :].astype(F32)
                self.pair[d, self.pair_rows(half), :] = value.astype(BF16)
                self.near[d, half] = self.to(d, place, half, d)

        def total(self):
            self.pair_copy[0].wait_recv()
            value = self.summed(0)
            for d, half, place in ((1, 0, 0), (3, 1, 1)):
                self.near[d].wait_recv()
                self.near[d, half].wait_recv()
                value = value + self.ring[place, self.pair_rows(), :].astype(F32)
            return value

        def release(self):
            for copy in self.pair_copy.values():
                copy.wait_send()
                pending.remove(copy)

    class WeightGather:
        def __init__(self, ref, fetched):
            self.ref = ref
            for copy in fetched:
                copy.wait()
            own = ref.at[f_index]
            self.along_z = {
                d: remote(own, own, device(dz=d), ref.at[ylo * 4 + wrap(z - d)]) for d in DIST
            }
            held, coming = ref.at[pl.ds(ylo * 4, 4)], ref.at[pl.ds((1 - ylo) * 4, 4)]
            self.along_y = Remote(sems(), held, held, sibling, coming)

        def spread(self, d):
            if d:
                self.along_z[d].wait_recv()
            held = ylo * 4 + wrap(z - d)
            for dy, part in ((1, pl.ds(0, 64)), (3, pl.ds(64, 64))):
                block = self.ref.at[held, part]
                self.along_y.launch(block, block, device(dy=dy))

        def finish(self):
            self.along_y.wait_recv()
            pending.append(self.along_y)

    class WeightGrad:
        def __init__(self, name, ring_first=False):
            cols, first = GROUPS[name]
            self.ring_first = ring_first
            self.gw, self.z1, self.y1, self.z2s = gw[name], z1[name], y1[name], z2s[name]
            self.y2s, self.y2, self.z2 = y2s[name], y2[name], z2[name]
            self.full, self.out = full[name], out[name]
            self.left, self.right = slice(0, first), slice(first, cols)

        def stage_one(self):
            copies = []
            for d in DIST:
                src = self.gw.at[:, wrap(z + d), :, self.left]
                copies.append((src, self.z1.at[SLOT[d]], device(dz=d)))
            self.one_z = several(copies, self.z1)
            copies = []
            for d in DIST:
                to_y = wrap(y + d)
                half = rows(lax.div(to_y, 2) * 64, 64)
                src = self.gw.at[lax.rem(to_y, 2), :, half, self.right]
                copies.append((src, self.y1.at[SLOT[d]], device(dy=d)))
            self.one_y = several(copies, self.y1)

        def stage_two(self):
            self.one_z.wait_recv()
            total = self.gw[:, z, :, self.left].astype(F32)
            for d in DIST:
                total = total + self.z1[SLOT[d]].astype(F32)
            self.z2s[...] = total.astype(BF16).reshape(self.z2s.shape)
            copies = []
            for d in DIST:
                to_y = wrap(y + d)
                src = self.z2s.at[lax.rem(to_y, 2), lax.div(to_y, 2)]
                copies.append((src, self.y2.at[SLOT[d]], device(dy=d)))
            self.two_y = several(copies, self.y2)
            self.one_y.wait_recv()
            total = self.gw[ylo, :, rows(yhi * 64, 64), self.right].astype(F32)
            for d in DIST:
                total = total + self.y1[SLOT[d]].astype(F32)
            self.y2s[...] = total.astype(BF16)
            copies = []
            for d in DIST:
                copies.append((self.y2s.at[wrap(z + d)], self.z2.at[SLOT[d]], device(dz=d)))
            self.two_z = several(copies, self.z2)

        def sums(self):
            self.two_y.wait_recv()
            total = self.z2s[ylo, yhi].astype(F32)
            for d in DIST:
                total = total + self.y2[SLOT[d]].astype(F32)
            self.full[yhi, x, core, :, self.left] = total.astype(BF16)
            self.two_z.wait_recv()
            total = self.y2s[z].astype(F32)
            for d in DIST:
                total = total + self.z2[SLOT[d]].astype(F32)
            self.full[yhi, x, core, :, self.right] = total.astype(BF16)

        def stage_three(self):
            self.sums()
            own = self.full.at[yhi, x, core]
            if self.ring_first:
                self.ring = [
                    remote(own, own, device(dx=d), self.full.at[yhi, wrap(x - d), core])
                    for d in DIST
                ]
            else:
                self.flip = remote(own, own, device(dy=2), self.full.at[1 - yhi, x, core])

        def stage_four(self):
            if self.ring_first:
                for copy in self.ring:
                    copy.wait_recv()
                held = self.full.at[yhi, :, core]
                self.ring = [remote(held, held, device(dy=2), self.full.at[1 - yhi, :, core])]
            else:
                self.flip.wait_recv()
                held = self.full.at[:, x, core]
                self.ring = [
                    remote(held, held, device(dx=d), self.full.at[:, wrap(x - d), core])
                    for d in DIST
                ]

        def stage_direct(self):
            self.sums()
            own = self.full.at[yhi, x, core]
            self.ring = [
                remote(own, own, device(dx=d), self.full.at[yhi, wrap(x - d), core]) for d in DIST
            ]
            copies = [(own, own, device(dx=d, dy=2)) for d in (0,) + DIST]
            self.ring.append(several(copies, self.full.at[1 - yhi, :, core]))

        def stage_five(self):
            for copy in self.ring:
                copy.wait_recv()
            held = self.full.at[:, :, core]
            self.pair = remote(held, held, sibling, self.full.at[:, :, 1 - core])

        def stage_six(self):
            self.pair.wait_recv()
            fetch(self.full, self.out)

    grad_m1, grad_m2, grad_o = WeightGrad("m1"), WeightGrad("m2", True), WeightGrad("o")
    grad_q, grad_kv = WeightGrad("q"), WeightGrad("kv")

    def weight_grad(parts):
        def chunk(index, carry):
            lanes = pl.ds(pl.multiple_of(index * 256, 256), 256)
            block = pl.ds(lax.rem(index, 2) * 2, 2)
            for left, right, source, target, cols, turned in parts:
                width = cols.stop - cols.start
                operand = right[..., source].reshape(1024, width)
                if turned:
                    value = mm(left[lanes, :], operand)
                else:
                    value = mm_first(left[..., lanes].reshape(1024, 256), operand)
                target[lax.div(index, 2), block, :, cols] = value.astype(BF16).reshape(
                    2, 128, width
                )
            return carry

        lax.fori_loop(0, 4, chunk, 0)

    with jax.named_scope("first_norm"):
        kv[:, :, 256:384] = jnp.ones((8, 256, 128), BF16)
        gain_early[...] = jnp.zeros_like(gain_early)
        for copy in fetch_tok:
            copy.wait()
        inputs = tok[...].astype(F32)
        g1[x, rows(core * 128, 128), :] = (inputs * rms_scale(inputs) * ng_ref[...]).astype(BF16)
    with jax.named_scope("entry_barrier"):
        pl.semaphore_wait(barrier, len(partners))
    across = device(dy=2)
    far_held = []
    far = Gather(
        lambda t, c, half: g1_turned.at[rows(t * 256 + c * 128 + half * 64, 64)],
        lambda t, c: g1_turned.at[rows(t * 256 + c * 128, 128)],
        far_held,
    )
    with jax.named_scope("gather_start"):
        rows_one = gather_plain(g1)
        gather_a = WeightGather(w_a, fetch_a)
        gather_a.spread(0)
        place = rows(x * 256 + core * 128, 128)
        send_rows = Remote(
            sems(), g1.at[x, rows(core * 128, 128)], g1_turned.at[place], across, g1_turned.at[place]
        )

        @pl.when(yhi == 0)
        def _():
            send_rows.start()

        rows_one.relay()
        gather_a.spread(1)
        rows_one.forward(1)
        gather_a.spread(3)
        rows_one.forward(3)
        gather_o = WeightGather(w_o, fetch_o)

        @pl.when(yhi == 1)
        def _():
            send_rows.wait_recv()
            far.begin()

        gather_a.spread(2)
        gather_m = WeightGather(w_m, fetch_m)
        rows_one.forward(2)
        for copy in fetch_rest:
            copy.wait()

        @pl.when(yhi == 1)
        def _():
            far.relay()

        gather_a.finish()
        for d in (0,) + DIST:
            gather_o.spread(d)
        gather_m.spread(0)

    def project(t):
        value = mm(g1[t], w_a[...].reshape(1024, COLS_QKV))
        cosine, sine = rope_split(rope[yhi * 4 + t])
        raw[t] = value[:, 0:384]
        for head in range(3):
            one = value[:, head * 128 : head * 128 + 128]
            gain = qg_ref[...] if head < 2 else kg_ref[...]
            scaled = one * rms_scale(one) * gain
            turned = (scaled * cosine + swap_halves(scaled) * sine).astype(BF16)
            if head < 2:
                qh[t, head * 256 : head * 256 + 256, :] = turned
            else:
                kv[yhi * 4 + t, :, 0:128] = turned
        kv[yhi * 4 + t, :, 128:256] = value[:, 384:512].astype(BF16)

    def project_far(t):
        value = mm(
            g1_turned[rows(t * 256, 256), :], w_a[:, :, 256:512].reshape(1024, 256)
        )
        cosine, sine = rope_split(rope[t])
        scaled = value[:, 0:128] * rms_scale(value[:, 0:128]) * kg_ref[...]
        kv[t, :, 0:128] = (scaled * cosine + swap_halves(scaled) * sine).astype(BF16)
        kv[t, :, 128:256] = value[:, 128:256].astype(BF16)

    with jax.named_scope("qkv"):
        for place, d in enumerate((0,) + DIST):
            rows_one.ready(d)
            project(wrap(x - d))
            if place == 2:

                @pl.when(yhi == 1)
                def _():
                    far.forward(1)
                    far.forward(3)

        rows_cot = gather_batches(g3)

    def attend_own(i, carry):
        row = lax.broadcasted_iota(jnp.int32, (512, 256), 0)
        col = lax.broadcasted_iota(jnp.int32, (512, 256), 1)
        soft = jnp.exp2(mm_last(qh[i], kv[yhi * 4 + i, :, 0:128]) * SCALE_LOG2)
        soft = jnp.where(col <= lax.rem(row, 256), soft, 0.0)
        oa[i] = mm(soft.astype(BF16), kv[yhi * 4 + i, :, 128:384])

        def inner(k, carry):
            j = yhi * 4 + k
            soft = jnp.exp2(mm_last(qh[i], kv[j, :, 0:128]) * SCALE_LOG2).astype(BF16)
            oa[i] += mm(soft, kv[j, :, 128:384])
            return carry

        lax.fori_loop(0, i, inner, 0)
        return carry

    with jax.named_scope("attend_own"):
        lax.fori_loop(0, 3, attend_own, 0)
        rows_cot.relay()
        gather_m.spread(1)
        gather_m.spread(3)
        lax.fori_loop(3, 4, attend_own, 0)

        @pl.when(yhi == 1)
        def _():
            far.forward(2)
            for d in (0,) + DIST:
                far.ready(d)
                project_far(wrap(x - d))
            for copy in far_held:
                copy.wait_send()

    def attend_across(i):
        @pl.when(yhi == 1)
        def _():
            def step(j, carry):
                two = pl.ds(j * 2, 2)
                soft = jnp.exp2(mm_last(qh[i], kv[two, :, 0:128].reshape(512, 128)) * SCALE_LOG2)
                oa[i] += mm(soft.astype(BF16), kv[two, :, 128:384].reshape(512, 256))
                return carry

            lax.fori_loop(0, 2, step, 0)

    def attend_end(i):
        both = oa[i]
        total = both[:, 128:256]
        exact = both[:, 0:128] / total
        oa[i, :, 0:128] = exact
        lse_row[i] = jnp.transpose(jnp.log(total) * math.log2(math.e))[0:8, :]
        exact = exact.astype(BF16)
        for head in range(2):
            for which in range(2):
                for batch in range(2):
                    start = head * 256 + which * 128 + batch * 64
                    att[batch, i, which * 64 : which * 64 + 64, head * 128 : head * 128 + 128] = (
                        exact[start : start + 64]
                    )

    branch = [Scatter(0, 0, 32, batch) for batch in range(2)]
    order = (2, 1, 3, 0)
    with jax.named_scope("branch"):
        for place, d in enumerate(order):
            t = wrap(x + d)
            attend_across(t)
            attend_end(t)
            if place == 0:
                gather_o.finish()
            for batch in range(2):
                branch[batch].store(d, mm_last(att[batch, t], w_o[...].reshape(1024, COLS_OUT)))
            if place:
                for batch in range(2):
                    branch[batch].forward(order[place - 1])
                rows_cot.forward(DIST[place - 1])
            if place == 0:
                gather_m.spread(2)

    def batch_rows(batch):
        return slice(batch * 64, batch * 64 + 64)

    rows_two = []
    with jax.named_scope("resid"):
        for batch in range(2):
            branch[batch].relay()
        for batch in range(2):
            value = branch[batch].total() + tok[batch_rows(batch), :].astype(F32)
            resid[batch_rows(batch), :] = value
            g2[batch, x, rows(core * 64, 64), :] = (
                value * rms_scale(value) * mg_ref[...]
            ).astype(BF16)
            rows_two.append(gather_batch(g2, batch))
        g1_turned[...] = jnp.transpose(g1[...].reshape(1024, 1024))
        for batch in range(2):
            rows_two[batch].relay()
            branch[batch].release()
        gather_m.finish()

    back_two = [Scatter(1, 1, 32, batch) for batch in range(2)]

    def feed_forward(batch, d):
        t = wrap(x - d)
        rows_two[batch].ready(d)
        w_gate_up = w_m[:, :, 0:768].reshape(1024, 768)
        w_d = w_m[:, :, 768:1152].reshape(1024, 384)
        both = mm(g2[batch, t], w_gate_up)
        d_hidden = mm(g3[batch, t], w_d)
        gate, up = both[:, 0:384], both[:, 384:768]
        sig = jax.nn.sigmoid(gate)
        active = gate * sig
        hid[batch, t] = (active * up).astype(BF16)
        dgu[batch, t, :, 0:384] = (d_hidden * up * sig * (1.0 + gate * (1.0 - sig))).astype(BF16)
        dgu[batch, t, :, 384:768] = (d_hidden * active).astype(BF16)
        back_two[batch].store((4 - d) % 4, mm_last(dgu[batch, t], w_gate_up))

    with jax.named_scope("mlp"):
        for d in (0,) + DIST:
            rows_cot.ready(d)
        feed_forward(0, 0)
        rows_two[0].forward(1)
        rows_two[0].forward(3)
        feed_forward(1, 0)
        feed_forward(0, 1)
        rows_two[0].forward(2)
        feed_forward(0, 3)
        rows_two[1].forward(1)
        rows_two[1].forward(3)
        back_two[0].forward(3)
        feed_forward(0, 2)
        back_two[0].forward(1)
        feed_forward(1, 1)
        back_two[0].forward(2)
        rows_two[1].forward(2)
        feed_forward(1, 3)
        back_two[1].forward(3)
        back_two[1].forward(1)
        feed_forward(1, 2)
        back_two[0].relay()
        back_two[1].forward(2)

    grads_m1 = ((g2, dgu, slice(0, 640), grad_m1.gw, slice(0, 640), False),)
    grads_m2 = (
        (g2, dgu, slice(640, 768), grad_m2.gw, slice(0, 128), False),
        (g3, hid, slice(0, 384), grad_m2.gw, slice(128, 512), False),
    )
    grads_o = ((g4, att, slice(0, 256), grad_o.gw, slice(0, 256), False),)
    grads_q = ((g1_turned, dqkv, slice(0, 256), grad_q.gw, slice(0, 256), True),)
    grads_kv = ((g1_turned, dqkv, slice(256, 512), grad_kv.gw, slice(0, 256), True),)
    rows_back = []

    def back_resid(batch):
        part = batch_rows(batch)
        d_normed = back_two[batch].total()
        value = resid[part, :]
        scaling = rms_scale(value)
        normed = value * scaling
        gain_early[:, 0:1024] += jnp.sum(d_normed * normed, 0, keepdims=True)
        d_normed = d_normed * mg_ref[...]
        value = scaling * (
            d_normed - normed * jnp.mean(d_normed * normed, -1, keepdims=True)
        ) + g3[batch, x, rows(core * 64, 64), :].astype(F32)
        d_resid[part, :] = value
        g4[batch, x, rows(core * 64, 64), :] = value.astype(BF16)
        rows_back.append(gather_batch(g4, batch))

    mlp_out = Scatter(2, 0, 64)

    def mlp_block(d):
        w_d = w_m[:, :, 768:1152].reshape(1024, 384)
        t = wrap(x + d)
        for batch in range(2):
            value = mm_last(hid[batch, t], w_d).astype(BF16)
            for which in range(2):
                start = which * 128 + batch * 64
                mlp_out.part[d, start : start + 64, :] = value[which * 64 : which * 64 + 64]
        mlp_out.emit(d)

    with jax.named_scope("d_resid"):
        weight_grad(grads_m1)
        grad_m1.stage_one()
        back_resid(0)
        back_two[1].relay()
        back_resid(1)
        rows_back[0].relay()
        weight_grad(grads_m2)
        grad_m2.stage_one()
        rows_back[1].relay()
        for to in order:
            mlp_block(to)

    def back_out(t):
        for batch in range(2):
            value = mm(g4[batch, t], w_o[...].reshape(1024, COLS_OUT)).astype(BF16)
            for head in range(2):
                for which in range(2):
                    start = head * 256 + which * 128 + batch * 64
                    do[t, start : start + 64, :] = value[
                        which * 64 : which * 64 + 64, head * 128 : head * 128 + 128
                    ]
        product = do[t].astype(F32) * oa[t, :, 0:128]
        delta_row[t] = jnp.broadcast_to(
            jnp.sum(jnp.transpose(product), 0, keepdims=True), (8, 512)
        )

    def tile(i, start, size, masked):
        keys = pl.ds(start, size)
        width = 256 * size
        key_rows, queries, grads = kv[keys, :, 0:128].reshape(width, 128), qh[i], do[i]
        soft = jnp.exp2(mm_last(key_rows, queries) * SCALE_LOG2 - lse_row[i, 0:1, :])
        if masked:
            row = lax.broadcasted_iota(jnp.int32, (width, 512), 0)
            col = lax.broadcasted_iota(jnp.int32, (width, 512), 1)
            soft = jnp.where(row <= lax.rem(col, 256) + (width - 256), soft, 0.0)
        d_soft = mm_last(kv[keys, :, 128:256].reshape(width, 128), grads)
        d_scores = (soft * (d_soft - delta_row[i, 0:1, :])).astype(BF16)
        dv[keys] += mm(soft.astype(BF16), grads).reshape(size, 256, 128)
        dk[keys] += mm(d_scores, queries).reshape(size, 256, 128)
        dq[i] += mm_first(d_scores, key_rows)

    def back_across(t):
        @pl.when(yhi == 1)
        def _():
            def step(j, carry):
                tile(t, j * 2, 2, False)
                return carry

            lax.fori_loop(0, 2, step, 0)

    send_back = [
        Remote(sems(), dkv_send.at[pair], dkv_recv.at[pair], across, dkv_recv.at[pair])
        for pair in range(2)
    ]

    def back_across_end(pair):
        @pl.when(yhi == 1)
        def _():
            def step(k, carry):
                tile(wrap(x + 1 + k), pair * 2, 2, False)
                return carry

            lax.fori_loop(0, 2, step, 0)
            two = slice(pair * 2, pair * 2 + 2)
            dkv_send[pair, :, :, 0:128] = dk[two].astype(BF16)
            dkv_send[pair, :, :, 128:256] = dv[two].astype(BF16)
            send_back[pair].start()

    def back_ready(d):
        for batch in range(2):
            rows_back[batch].ready(d)
        back_out(wrap(x - d))

    def back_forward(d):
        for batch in range(2):
            rows_back[batch].forward(d)

    with jax.named_scope("attend_back_across"):
        dq[...] = jnp.zeros_like(dq)
        dk[...] = jnp.zeros_like(dk)
        dv[...] = jnp.zeros_like(dv)
        back_ready(0)
        back_forward(1)
        back_forward(3)
        back_across(x)
        back_ready(1)
        back_forward(2)
        grad_m1.stage_two()
        back_across(wrap(x - 1))
        back_ready(3)
        back_ready(2)
        for to in order[:3]:
            mlp_out.forward(to)
        back_across_end(0)
        grad_m2.stage_two()
        grad_m1.stage_three()
        back_across_end(1)
    with jax.named_scope("out_weight_grads"):
        mlp_out.relay()
        weight_grad(grads_o)
        grad_o.stage_one()
        grad_m2.stage_three()

    with jax.named_scope("attend_back_own"):

        def back_own(i, carry):
            tile(i, yhi * 4 + i, 1, True)

            def inner(j, carry):
                tile(i, yhi * 4 + j, 1, False)
                return carry

            lax.fori_loop(0, i, inner, 0)
            return carry

        lax.fori_loop(0, 3, back_own, 0)
        grad_m1.stage_four()
        lax.fori_loop(3, 4, back_own, 0)
        grad_m2.stage_four()

    with jax.named_scope("mixed"):
        mixed_ref[...] = (resid[...] + mlp_out.total()).astype(BF16)
        fetch(mixed_ref, mixed_out)

    def head_back(t, head):
        cosine, sine = rope_split(rope[yhi * 4 + t])
        one = raw[t, :, head * 128 : head * 128 + 128]
        if head < 2:
            grads, gain = dq[t, head * 256 : head * 256 + 256, :], qg_ref[...]
        else:
            grads, gain = dk[yhi * 4 + t], kg_ref[...]
        grads = grads * SCALE
        grads = grads * cosine - swap_halves(grads) * sine
        scaling = rms_scale(one)
        normed = one * scaling
        part = jnp.sum(grads * normed, 0, keepdims=True)
        grads = grads * gain
        value = scaling * (grads - normed * jnp.mean(grads * normed, -1, keepdims=True))
        dqkv[t, :, head * 128 : head * 128 + 128] = value.astype(BF16)
        return part

    def query_back(t, carry):
        return carry + head_back(t, 0) + head_back(t, 1)

    def key_back(t, carry):
        dqkv[t, :, 384:512] = dv[yhi * 4 + t].astype(BF16)
        return carry + head_back(t, 2)

    def over_x(slots, value):
        slots[slice_index] = value
        own = slots.at[slice_index]
        copies = [(own, own, sibling)]
        copies += [(own, own, device(dx=d, dcore=flip)) for d in DIST for flip in (0, 1)]
        return several(copies, slots.at[0:7])

    def over_yz(slots, value):
        place = y * 4 + z
        slots[place] = value
        own = slots.at[place]
        steps = (0,) + DIST
        copies = [(own, own, device(dy=a, dz=b)) for a in steps for b in steps if a or b]
        return several(copies, slots.at[0:15])

    def total_of(slots, copies):
        copies.wait_recv()
        value = slots[0]
        for place in range(1, slots.shape[0]):
            value = value + slots[place]
        return value

    with jax.named_scope("head_norm_back"):
        zero = jnp.zeros((1, 128), F32)
        gain_early[:, 1024:1152] = lax.fori_loop(0, 4, query_back, zero)

    with jax.named_scope("qkv_weight_grads"):
        weight_grad(grads_q)
        grad_q.stage_one()

        @pl.when(yhi == 0)
        def _():
            for pair in range(2):
                send_back[pair].wait_recv()
                two = slice(pair * 2, pair * 2 + 2)
                dk[two] += dkv_recv[pair, :, :, 0:128].astype(F32)
                dv[two] += dkv_recv[pair, :, :, 128:256].astype(F32)

        gain_early[:, 1152:1280] = lax.fori_loop(0, 4, key_back, zero)
        weight_grad(grads_kv)
        grad_kv.stage_one()
        grad_o.stage_two()
    with jax.named_scope("d_normed"):
        for batch in range(2):
            back_two[batch].release()
        back_one = Scatter(3, 1, 64)
        for place, d in enumerate(order):
            back_one.store(d, mm_last(dqkv[wrap(x + d)], w_a[...].reshape(1024, COLS_QKV)))
            if place:
                back_one.forward(order[place - 1])
        early = over_x(early_x, gain_early[...])
        norm_gain = jnp.zeros((1, 1024), F32)
        for d in range(4):
            part = back_one.part[d].astype(F32) * g1[wrap(x + d)].astype(F32)
            norm_gain = norm_gain + jnp.sum(part, 0, keepdims=True)
        late = over_x(late_x, norm_gain / ng_ref[...])
        grad_m1.stage_five()
        grad_q.stage_two()
        back_one.relay()
        grad_kv.stage_two()
        grad_q.stage_direct()
        grad_o.stage_direct()
        early = over_yz(early_yz, total_of(early_x, early))
        late = over_yz(late_yz, total_of(late_x, late))
        grad_kv.stage_direct()
    with jax.named_scope("input_grad"):
        d_normed = back_one.total()
        inputs = tok[...].astype(F32)
        scaling = rms_scale(inputs)
        normed = inputs * scaling
        d_normed = d_normed * ng_ref[...]
        ig_ref[...] = (
            scaling * (d_normed - normed * jnp.mean(d_normed * normed, -1, keepdims=True))
            + d_resid[...]
        )
        fetch(ig_ref, ig_out)

    with jax.named_scope("tail"):
        grad_m2.stage_five()
        grad_m1.stage_six()
        grad_q.stage_five()
        grad_o.stage_five()
        gain_early[...] = total_of(early_yz, early)
        gains_ref[0:1, :] = gain_early[:, 0:1024]
        gains_ref[2:3, 0:256] = gain_early[:, 1024:1280]
        gains_ref[1:2, :] = total_of(late_yz, late)
        grad_m2.stage_six()
        grad_kv.stage_five()
        grad_q.stage_six()
        grad_o.stage_six()
        grad_kv.stage_six()
    with jax.named_scope("drain"):
        drain()

        @pl.when(yhi == 0)
        def _():
            send_rows.wait_send()

        @pl.when(yhi == 1)
        def _():
            for copy in send_back:
                copy.wait_send()

        for copy in local[-7:]:
            copy.wait()


def rope_table(length):
    half = HEAD_DIM // 2
    freqs = np.power(np.float32(THETA), np.float32(-2.0) * np.arange(half, dtype=np.float32) / HEAD_DIM)
    angles = np.arange(length, dtype=np.float32)[:, None] * freqs.astype(np.float32)[None, :]
    table = np.concatenate([np.cos(angles), np.sin(angles)], 1).astype(np.float32)
    return table.reshape(length // 256, 256, HEAD_DIM)


def on_device(
    tokens, cotangent, w_query, w_key, w_value, w_output, w_gate, w_up, w_down,
    norm_gain, mlp_gain, query_gain, key_gain,
):
    vmem = pl.BlockSpec(memory_space=pltpu.VMEM)
    hbm = pl.BlockSpec(memory_space=pl.ANY)

    def v(shape, dtype=BF16):
        return pltpu.VMEM(shape, dtype)

    scratch = [v((128, 1024)), v((128, 1024), F32)]
    scratch += [v((128, 1024)), v((1, 1024), F32), v((1, 1024), F32), v((1, 128), F32), v((1, 128), F32)]
    scratch += [v((4, 256, 1024))]
    scratch += [v((2, 4, 128, 1024)) for _ in range(3)]
    scratch += [v((1024, 1024))]
    scratch += [v((8, 128, COLS_QKV)), v((8, 128, COLS_OUT)), v((8, 128, COLS_MLP))]
    scratch += [
        v((4, 256, 384), F32),
        v((4, 512, 128)),
        v((8, 256, 384)),
        v((8, 256, 128), F32),
        v((4, 512, 256), F32),
        v((2, 4, 128, 256)),
        v((4, 512, 128)),
        v((4, 512, 128), F32),
        v((8, 256, 128), F32),
        v((8, 256, 128), F32),
        v((4, 256, 512)),
        v((2, 4, 128, 384)),
        v((2, 4, 128, 768)),
        v((4, 8, 512), F32),
        v((4, 8, 512), F32),
        v((128, 1024), F32),
        v((128, 1024), F32),
        v((2, 4, 256, 1024)),
        v((4, 4, 128, 1024)),
        v((4, 3, 128, 1024)),
        v((2, 2, 256, 256)),
        v((2, 2, 256, 256)),
    ]
    scratch += [v((1, 1280), F32)]
    scratch += [v((8, 1, 1280), F32), v((16, 1, 1280), F32)]
    scratch += [v((8, 1, 1024), F32), v((16, 1, 1024), F32)]
    shapes = (
        lambda cols, first: (2, 4, 128, cols),
        lambda cols, first: (3, 2, 128, first),
        lambda cols, first: (3, 4, 64, cols - first),
        lambda cols, first: (2, 2, 64, first),
        lambda cols, first: (4, 64, cols - first),
        lambda cols, first: (3, 64, first),
        lambda cols, first: (3, 64, cols - first),
        lambda cols, first: (2, 4, 2, 64, cols),
    )
    scratch += [{name: v(shape(*cols)) for name, cols in GROUPS.items()} for shape in shapes]
    scratch += [
        pltpu.SemaphoreType.DMA((COPIES,)),
        pltpu.SemaphoreType.DMA((COPIES,)),
        pltpu.SemaphoreType.DMA((LOCAL_COPIES,)),
    ]
    mixed, input_grad, grads, gains = pl.pallas_call(
        kernel,
        name="layer",
        out_shape=(
            jax.ShapeDtypeStruct((128, 1024), BF16),
            jax.ShapeDtypeStruct((128, 1024), F32),
            {n: jax.ShapeDtypeStruct((2, 4, 2, 64, c[0]), BF16) for n, c in GROUPS.items()},
            jax.ShapeDtypeStruct((8, 1024), F32),
        ),
        in_specs=[hbm] * 14,
        out_specs=(hbm, hbm, {name: hbm for name in GROUPS}, vmem),
        scratch_shapes=scratch,
        compiler_params=pltpu.CompilerParams(
            collective_id=0, has_side_effects=True, vmem_limit_bytes=63 * 2**20
        ),
    )(
        tokens, cotangent, w_query, w_key, w_value, w_output, w_gate, w_up, w_down,
        norm_gain[None, :], mlp_gain[None, :], query_gain[None, :], key_gain[None, :],
        jnp.asarray(rope_table(2048)),
    )

    widths = (256, 128, 128, 256, 384, 384, 384)
    return pl.pallas_call(
        finish,
        name="finish",
        out_shape=(
            jax.ShapeDtypeStruct((128, 1024), BF16),
            jax.ShapeDtypeStruct((128, 1024), F32),
            *(jax.ShapeDtypeStruct((128, 8 * width), F32) for width in widths),
            jax.ShapeDtypeStruct((1024,), F32),
            jax.ShapeDtypeStruct((1024,), F32),
            jax.ShapeDtypeStruct((128,), F32),
            jax.ShapeDtypeStruct((128,), F32),
        ),
        in_specs=[hbm, hbm, {name: hbm for name in GROUPS}, vmem],
        out_specs=(hbm,) * 9 + (vmem,) * 4,
        scratch_shapes=[
            {name: v((2, 8, 64, cols[0])) for name, cols in GROUPS.items()},
            tuple(v((128, 8 * width), F32) for width in widths),
            v((128, 1024)),
            v((128, 1024), F32),
            pltpu.SemaphoreType.DMA((23,)),
        ],
        compiler_params=pltpu.CompilerParams(vmem_limit_bytes=63 * 2**20),
    )(
        mixed, input_grad,
        {name: grads[name].reshape(2, 8, 64, cols[0]) for name, cols in GROUPS.items()}, gains,
    )


def finish(
    mixed, input_grad, grads, gains,
    out_mixed, out_input, out_q, out_k, out_v, out_o, out_g, out_u, out_d,
    out_norm, out_mlp, out_qg, out_kg, held, wide, held_mixed, held_input, sems,
):
    arrived = {}
    for index, name in enumerate(GROUPS):
        arrived[name] = pltpu.make_async_copy(grads[name], held[name], sems.at[index])
        arrived[name].start()
    through = [
        pltpu.make_async_copy(mixed, held_mixed, sems.at[19]),
        pltpu.make_async_copy(input_grad, held_input, sems.at[20]),
    ]
    for copy in through:
        copy.start()
    sent = []
    wide_q, wide_k, wide_v, wide_o, wide_g, wide_u, wide_d = wide
    for index, (name, out, place, pieces) in enumerate((
        ("m1", out_g, wide_g, (("m1", 0, 384, 0),)),
        ("m2", out_u, wide_u, (("m1", 384, 256, 0), ("m2", 0, 128, 256))),
        ("m2", out_d, wide_d, (("m2", 128, 384, 0),)),
        ("o", out_o, wide_o, (("o", 0, 256, 0),)),
        ("q", out_q, wide_q, (("q", 0, 256, 0),)),
        ("kv", out_k, wide_k, (("kv", 0, 128, 0),)),
        ("kv", out_v, wide_v, (("kv", 128, 128, 0),)),
    )):
        if name in arrived:
            arrived.pop(name).wait()
        width = place.shape[1] // 8
        for half in range(2):
            part = slice(half * 64, half * 64 + 64)
            for group, start, size, at in pieces:
                for j in range(8):
                    place[part, j * width + at : j * width + at + size] = held[group][
                        half, j, :, start : start + size
                    ].astype(F32)
            copy = pltpu.make_async_copy(place.at[part], out.at[part], sems.at[5 + index * 2 + half])
            copy.start()
            sent.append(copy)
    for copy in through:
        copy.wait()
    for held_rows, out, index in ((held_mixed, out_mixed, 21), (held_input, out_input, 22)):
        copy = pltpu.make_async_copy(held_rows, out, sems.at[index])
        copy.start()
        sent.append(copy)
    out_norm[...] = gains[1, :]
    out_mlp[...] = gains[0, :]
    out_qg[...] = gains[2, 0:128]
    out_kg[...] = gains[2, 128:256]
    for copy in sent:
        copy.wait()


def solution(mesh):
    rows = P(("fsdp", "ctx"), None)
    weight = P("fsdp", None)
    return jax.shard_map(
        on_device,
        mesh=mesh,
        in_specs=(rows, rows) + (weight,) * 7 + (P(),) * 4,
        out_specs=(rows, rows) + (weight,) * 7 + (P(),) * 4,
        check_vma=False,
    )
```
